32 devices in a mesh: grp: 4 (over y, x), tp: 8 (over z, core).
Axes of the slice: x: 2, y: 2, z: 4, core: 2. Of those that a mesh axis runs over, the one named last changes fastest.
Arguments:
- vision_in: bfloat16 [2048, 3200], P(('grp', 'tp')), may hold values from -6 to 6
- vis_gain: float32 [3200], replicated, may hold values from 0.5 to 2
- first_weight: bfloat16 [3200, 12800], P(None, 'tp'), may hold values from -0.109375 to 0.109375
- second_weight: bfloat16 [12800, 3200], P('tp'), may hold values from -0.0546875 to 0.0546875
- layer_scale: float32 [3200], replicated, may hold values from 0.3 to 1.5
- proj_gain: float32 [12800], replicated, may hold values from 0.5 to 2
- proj_weight: bfloat16 [12800, 8192], P(None, 'tp'), may hold values from -0.0546875 to 0.0546875
- text_embed: bfloat16 [4608, 8192], P('grp', 'tp'), may hold values from -6 to 6
- dest_row: int32 [512], replicated, may hold values from 0 to 4607, as said below
- cotangent: bfloat16 [4608, 8192], P('grp', 'tp'), may hold values from -6 to 6
Outputs:
- seq_embed: bfloat16 [4608, 8192], P('grp', 'tp')
- grad_vision: bfloat16 [2048, 3200], P(('grp', 'tp'))
The draws below stay inside these ranges and needn't reach their ends.
Inputs may be any that keep to these rules, and one draw needn't show every extreme that they name: `dest_row`: all values distinct. Sequence h is rows h * 1152 to (h + 1) * 1152 - 1. The 128 merged rows of index g of grp form four images of 32 rows each; each image fills consecutive token rows of its own sequence, four different sequences for one index of grp, inside positions g * (288) to (g + 1) * 288 - 1 of that sequence. Image j of index g goes to sequence (g + k_j) mod 4 with four distinct shifts k_j common to all g, among them 1 and 2; so at most, and exactly, 32 rows go from one index of grp to one sequence, and every sequence receives four images from four different indices of grp.
All inputs are finite; a program needn't handle non-finite values.
Results may differ from the reference program's by a relative error of at most 0.025.
Values may be sent and summed in bfloat16 or wider, within the bound.
No kernel may reach another device: no remote copies, remote signals or barrier semaphores. Data moves between devices by JAX's collectives and lax.ppermute only.
A program may use at most 128 MiB of HBM per device.

```python
import math
import jax
import jax.numpy as jnp
from jax import lax

VD = 3200
VFF = 12800
LD = 8192
SEQ_LEN = 1152
PD = 12800
MROWS_DEV = 128
PATCHES = 2048
MROWS = 512
TOKENS = 4608


def draw_dest_row(key, part):
    groups = MROWS // MROWS_DEV
    run_len = MROWS_DEV // 4
    region = SEQ_LEN // groups
    half_way = groups // 2
    key_one, key_two = jax.random.split(key, 2)
    shuffled = jax.random.permutation(key_one, groups).astype(jnp.int32)
    flagged = jnp.logical_or(shuffled == 1, shuffled == half_way).astype(jnp.int32)
    ranking = jnp.argsort(flagged * groups + jnp.arange(groups, dtype=jnp.int32), stable=True)
    others = shuffled[ranking][:2]
    shifts = jnp.concatenate([jnp.array([1, half_way], dtype=jnp.int32), others]).astype(jnp.int32)
    sources = jnp.arange(groups, dtype=jnp.int32)
    targets = (sources[:, None] + shifts[None, :]) % groups
    offsets = jax.random.randint(key_two, (groups, 4), 0, region - run_len + 1)
    starts = targets * SEQ_LEN + sources[:, None] * region + offsets
    rows = starts[:, :, None] + jnp.arange(run_len, dtype=jnp.int32)[None, None, :]
    return rows.reshape(-1).astype(jnp.int32)


def level_of(own_key, dims, cuts, low, top_value):
    gain, own = 1.0, jax.random.fold_in(own_key, 6)
    for position, blocks in cuts:
        steps = jnp.exp(jax.random.uniform(jax.random.fold_in(own, position), (blocks,), jnp.float32, low / len(cuts), top_value / len(cuts)))
        gain = gain * jnp.repeat(steps, dims[position] // blocks).reshape([-1 if axis == position else 1 for axis in range(len(dims))])
    return gain


def noise(rng, extent, spread, limit, shards=(), held_as=jnp.bfloat16):
    level = level_of(rng, extent, shards, -0.22, 0.18) if shards else 1.0
    result = jax.random.normal(rng, extent, jnp.float32) * spread * level
    return jnp.minimum(jnp.maximum(result, -limit), limit).astype(held_as)


def setup_inputs(seed: int = 0) -> dict:
    splits = jax.random.split(jax.random.key(seed), 11)
    vision_in = noise(splits[0], (PATCHES, VD), 1.0, 6.0, ((0, 32),))
    vis_gain = jnp.clip(jnp.exp(jax.random.uniform(splits[1], (VD,), jnp.float32, math.log(0.5), math.log(2.0))), 0.5, 2.0)
    first_weight = noise(splits[2], (VD, VFF), VD ** -0.5, 0.109375, ((1, 8),))
    second_weight = noise(splits[3], (VFF, VD), VFF ** -0.5, 0.0546875, ((0, 8),))
    layer_scale = jnp.clip(jnp.exp(jax.random.uniform(splits[4], (VD,), jnp.float32, math.log(0.3), math.log(1.5))), 0.3, 1.5)
    proj_gain = jnp.clip(jnp.exp(jax.random.uniform(splits[5], (PD,), jnp.float32, math.log(0.5), math.log(2.0))), 0.5, 2.0)
    proj_weight = noise(splits[6], (PD, LD), PD ** -0.5, 0.0546875, ((1, 8),))
    text_embed = noise(splits[7], (TOKENS, LD), 1.0, 6.0, ((0, 4), (1, 8)))
    dest_row = draw_dest_row(jax.random.fold_in(splits[10], 71), 0)
    cotangent = noise(splits[9], (TOKENS, LD), 1.0, 6.0, ((0, 4), (1, 8)))
    return dict(vision_in=vision_in, vis_gain=vis_gain, first_weight=first_weight, second_weight=second_weight, layer_scale=layer_scale, proj_gain=proj_gain, proj_weight=proj_weight, text_embed=text_embed, dest_row=dest_row, cotangent=cotangent)


vis_eps = 1e-06
proj_eps = 1e-05

def layer_norm(values, scale_vec, epsilon):
    mean_val = lax.optimization_barrier(jnp.mean(values, -1, keepdims=True))
    centred = values - mean_val
    inv_std = lax.rsqrt(lax.optimization_barrier(jnp.mean(centred * centred, -1, keepdims=True)) + epsilon)
    normed = centred * inv_std
    return (normed * scale_vec, normed, inv_std)

def norm_back(upstream, scale_vec, normed, inv_std):
    scaled = upstream * scale_vec
    return inv_std * (scaled - lax.optimization_barrier(jnp.mean(scaled, -1, keepdims=True)) - normed * lax.optimization_barrier(jnp.mean(scaled * normed, -1, keepdims=True)))

def gelu_slope(values):
    cumul = 0.5 * (1.0 + lax.erf(values * 0.7071067811865476))
    dense = jnp.exp(-0.5 * values * values) * 0.3989422804014327
    return cumul + values * dense

def reference(vision_in, vis_gain, first_weight, second_weight, layer_scale, proj_gain, proj_weight, text_embed, dest_row, cotangent):
    patch_float = vision_in.astype(jnp.float32)
    normed_in, patch_hat, patch_inv = layer_norm(patch_float, vis_gain, vis_eps)
    first_pre = jnp.dot(normed_in.astype(jnp.bfloat16), first_weight, preferred_element_type=jnp.float32)
    hidden = jax.nn.gelu(first_pre, approximate=False).astype(jnp.bfloat16)
    summed = jnp.dot(hidden, second_weight, preferred_element_type=jnp.float32)
    outputs = (patch_float + layer_scale * summed).astype(jnp.bfloat16)
    merged = outputs.reshape(MROWS, PD)
    merged_norm, merged_hat, merged_inv = layer_norm(merged.astype(jnp.float32), proj_gain, proj_eps)
    proj_pre = jnp.dot(merged_norm.astype(jnp.bfloat16), proj_weight, preferred_element_type=jnp.float32)
    projected = jax.nn.gelu(proj_pre, approximate=False).astype(jnp.bfloat16)
    seq_embed = text_embed.at[dest_row].set(projected)
    grad_proj = cotangent[dest_row]
    proj_delta = (grad_proj.astype(jnp.float32) * gelu_slope(proj_pre)).astype(jnp.bfloat16)
    back_sum = jnp.dot(proj_delta, proj_weight.T, preferred_element_type=jnp.float32)
    merged_grad = norm_back(back_sum, proj_gain, merged_hat, merged_inv).astype(jnp.bfloat16)
    grad_out = merged_grad.reshape(PATCHES, VD)
    scaled_grad = (grad_out.astype(jnp.float32) * layer_scale).astype(jnp.bfloat16)
    hidden_grad = jnp.dot(scaled_grad, second_weight.T, preferred_element_type=jnp.float32)
    first_delta = (hidden_grad * gelu_slope(first_pre)).astype(jnp.bfloat16)
    normed_grad = jnp.dot(first_delta, first_weight.T, preferred_element_type=jnp.float32)
    grad_vision = (grad_out.astype(jnp.float32) + norm_back(normed_grad, vis_gain, patch_hat, patch_inv)).astype(jnp.bfloat16)
    return (seq_embed, grad_vision)
```

```python
import jax
import jax.numpy as jnp
from jax import lax
from jax.sharding import PartitionSpec as P

vis_eps = 1e-06
proj_eps = 1e-05
chunks = 2
images = 4
cores = 2


def layer_norm(values, scale_vec, epsilon):
    mean_val = jnp.mean(values, -1, keepdims=True)
    centred = values - mean_val
    inv_std = lax.rsqrt(jnp.mean(centred * centred, -1, keepdims=True) + epsilon)
    normed = centred * inv_std
    return (normed * scale_vec, normed, inv_std)


def norm_back(upstream, scale_vec, normed, inv_std):
    scaled = upstream * scale_vec
    return inv_std * (
        scaled
        - jnp.mean(scaled, -1, keepdims=True)
        - normed * jnp.mean(scaled * normed, -1, keepdims=True)
    )


def gelu_slope(values):
    cumul = 0.5 * (1.0 + lax.erf(values * 0.7071067811865476))
    dense = jnp.exp(-0.5 * values * values) * 0.3989422804014327
    return cumul + values * dense


def times_transposed(left, right):
    return lax.dot_general(
        left, right, (((1,), (1,)), ((), ())), preferred_element_type=jnp.float32
    )


class Line:
    def __init__(self):
        self.places = lax.axis_size("tp") // cores
        rank = lax.axis_index("tp")
        self.place = rank // cores
        self.core = rank % cores
        self.order = sorted(
            range(self.places), key=lambda k: max(k, self.places - k) if k else 0
        )
        self.swap_pairs = [
            (p * cores + c, p * cores + 1 - c) for p in range(self.places) for c in range(cores)
        ]

    def move(self, block, step, sources):
        pairs = [
            (p * cores + c, (p + step) * cores + c) for p in sources for c in range(cores)
        ]
        return lax.ppermute(block, "tp", pairs)

    def swap(self, block):
        return lax.ppermute(block, "tp", self.swap_pairs)

    def gather(self, block):
        n = self.places
        up, down = [block], [block]
        for s in range(1, n):
            up.append(self.move(up[-1], 1, range(s - 1, n - 1)))
            down.append(self.move(down[-1], -1, range(1, n - s + 1)))
        slots = [block] + [
            jnp.where(self.place >= k, up[k], down[n - k]) for k in range(1, n)
        ]
        mine = [slots[k] for k in self.order]
        head = [self.swap(m) for m in mine[:-2]]
        tail = self.swap(jnp.concatenate(mine[-2:], 0))
        return jnp.concatenate(mine + head + [tail], 0), (up[-1], down[-1])

    def scatter(self, partial):
        n = self.places
        half = partial.shape[0] // cores
        got = self.swap(partial[half:])
        both = partial[:half].astype(jnp.float32) + got.astype(jnp.float32)
        both = both.reshape(n, half // n, partial.shape[1])
        part = {k: both[i] for i, k in enumerate(self.order)}

        def travel(step):
            slot = lambda d: part[(-d * step) % n]
            total = slot(n - 1)
            for d in range(n - 1, 0, -1):
                sources = range(n - d) if step == 1 else range(d, n)
                came = self.move(total.astype(jnp.bfloat16), step, sources).astype(jnp.float32)
                total = came + slot(d - 1) if d > 1 else came
            return total

        return part[0] + travel(1) + travel(-1)


def per_device(
    vision_in,
    vis_gain,
    first_weight,
    second_weight,
    layer_scale,
    proj_gain,
    proj_weight,
    text_embed,
    dest_row,
    cotangent,
):
    line = Line()
    groups = lax.axis_size("grp")
    grp_rank = lax.axis_index("grp")
    seq_len, width = text_embed.shape
    merged_total = dest_row.shape[0] // groups
    image_rows = merged_total // images
    own_rows, vis_width = vision_in.shape
    merged_width = proj_gain.shape[0]
    fold = merged_width // vis_width
    merged_own = own_rows // fold
    rows = own_rows // chunks
    merged_rows = rows // fold

    starts = dest_row.reshape(groups, images, image_rows)[:, :, 0]
    start_seq = starts // seq_len
    start_pos = starts % seq_len
    mine_seq = lax.dynamic_index_in_dim(start_seq, grp_rank, 0, False)
    shift = (mine_seq - grp_rank) % groups
    matches = shift[None, :] == jnp.arange(groups)[:, None]
    image_of = jnp.argmax(matches, 1)
    used = jnp.any(matches, 1)
    spot = [start_pos[(grp_rank - s) % groups, image_of[s]] for s in range(groups)]
    span = jnp.arange(image_rows)

    picked = []
    for s in range(groups):
        block = jnp.take(cotangent, spot[s] + span, axis=0)
        if s:
            block = lax.ppermute(block, "grp", [(g, (g - s) % groups) for g in range(groups)])
        picked.append(block)
    returned = jnp.concatenate(picked, 0)

    ordering = jnp.array(line.order)
    held_place = (line.place - ordering) % line.places
    held_core = (line.core + jnp.arange(cores)) % cores
    held_rank = held_place[None, :] * cores + held_core[:, None]
    held_row = held_rank[:, :, None] * merged_own + jnp.arange(merged_rows)
    held_row = held_row.reshape(-1)
    natural = jnp.arange(merged_total)
    rank_of = natural // merged_own
    inside = natural % merged_own
    back_order = jnp.array([line.order.index(k) for k in range(line.places)])
    slot_of = jnp.take(back_order, (line.place - rank_of // cores) % line.places)
    far = (rank_of % cores + line.core) % cores
    row_in = (far * line.places + slot_of) * merged_rows + inside % merged_rows
    row_at = inside // merged_rows * (merged_total // chunks) + row_in

    x, hat, inv, normed = [], [], [], []
    for c in range(chunks):
        x.append(vision_in[c * rows : (c + 1) * rows].astype(jnp.float32))
        scaled, own_hat, own_inv = layer_norm(x[c], vis_gain, vis_eps)
        normed.append(scaled.astype(jnp.bfloat16))
        hat.append(own_hat)
        inv.append(own_inv)

    first_pre, merged_hat, merged_inv, merged_norm = [], [], [], []
    ends = None
    for c in range(chunks):
        block = normed[c]
        if ends is not None:
            block, _ = lax.optimization_barrier((block, ends))
        patches, ends = line.gather(block)
        first_pre.append(jnp.dot(patches, first_weight, preferred_element_type=jnp.float32))
        hidden = jax.nn.gelu(first_pre[c], approximate=False).astype(jnp.bfloat16)
        summed = line.scatter(
            jnp.dot(hidden, second_weight, preferred_element_type=jnp.float32).astype(jnp.bfloat16)
        )
        outputs = (x[c] + layer_scale * summed).astype(jnp.bfloat16)
        merged = outputs.reshape(merged_rows, merged_width).astype(jnp.float32)
        scaled, own_hat, own_inv = layer_norm(merged, proj_gain, proj_eps)
        merged_norm.append(scaled.astype(jnp.bfloat16))
        merged_hat.append(own_hat)
        merged_inv.append(own_inv)

    projected, own_grad = [], []
    for c in range(chunks):
        merged, _ = line.gather(merged_norm[c])
        proj_pre = jnp.dot(merged, proj_weight, preferred_element_type=jnp.float32)
        projected.append(jax.nn.gelu(proj_pre, approximate=False).astype(jnp.bfloat16))
        row = held_row + c * merged_rows
        from_row = jnp.take(shift, row // image_rows) * image_rows + row % image_rows
        grad_proj = jnp.take(returned, from_row, axis=0).astype(jnp.float32)
        proj_delta = (grad_proj * gelu_slope(proj_pre)).astype(jnp.bfloat16)
        back_sum = line.scatter(times_transposed(proj_delta, proj_weight).astype(jnp.bfloat16))
        merged_grad = norm_back(back_sum, proj_gain, merged_hat[c], merged_inv[c])
        own_grad.append(merged_grad.astype(jnp.bfloat16).reshape(rows, vis_width))

    projected = jnp.concatenate(projected, 0)
    seq_embed = text_embed
    for s in range(groups):
        block = jnp.take(projected, jnp.take(row_at, image_of[s] * image_rows + span), axis=0)
        if s:
            block = lax.ppermute(block, "grp", [(g, (g + s) % groups) for g in range(groups)])
        if groups > images:
            there = lax.dynamic_slice_in_dim(seq_embed, spot[s], image_rows, 0)
            block = jnp.where(used[s], block, there)
        seq_embed = lax.dynamic_update_slice_in_dim(seq_embed, block, spot[s], 0)

    grads = []
    for c in range(chunks):
        grad_float = own_grad[c].astype(jnp.float32)
        grad_out, _ = line.gather((grad_float * layer_scale).astype(jnp.bfloat16))
        hidden_grad = times_transposed(grad_out, second_weight)
        first_delta = (hidden_grad * gelu_slope(first_pre[c])).astype(jnp.bfloat16)
        normed_grad = line.scatter(times_transposed(first_delta, first_weight).astype(jnp.bfloat16))
        grads.append(grad_float + norm_back(normed_grad, vis_gain, hat[c], inv[c]))
    grad_vision = jnp.concatenate(grads, 0).astype(jnp.bfloat16)
    return (seq_embed, grad_vision)


def solution(mesh):
    placed = (
        P(("grp", "tp"), None),
        P(),
        P(None, "tp"),
        P("tp", None),
        P(),
        P(),
        P(None, "tp"),
        P("grp", "tp"),
        P(),
        P("grp", "tp"),
    )
    return jax.shard_map(
        per_device,
        mesh=mesh,
        in_specs=placed,
        out_specs=(P("grp", "tp"), P(("grp", "tp"), None)),
        check_vma=False,
    )
```

```python
import jax
import jax.numpy as jnp
from jax import lax
from jax.sharding import PartitionSpec as P

vis_eps = 1e-06
proj_eps = 1e-05
chunks = 2
images = 4
cores = 2


def layer_norm(values, scale_vec, epsilon):
    mean_val = jnp.mean(values, -1, keepdims=True)
    centred = values - mean_val
    inv_std = lax.rsqrt(jnp.mean(centred * centred, -1, keepdims=True) + epsilon)
    normed = centred * inv_std
    return (normed * scale_vec, normed, inv_std)


def norm_back(upstream, scale_vec, normed, inv_std):
    scaled = upstream * scale_vec
    return inv_std * (
        scaled
        - jnp.mean(scaled, -1, keepdims=True)
        - normed * jnp.mean(scaled * normed, -1, keepdims=True)
    )


def gelu_slope(values):
    cumul = 0.5 * (1.0 + lax.erf(values * 0.7071067811865476))
    dense = jnp.exp(-0.5 * values * values) * 0.3989422804014327
    return cumul + values * dense


def times_transposed(left, right):
    return lax.dot_general(
        left, right, (((1,), (1,)), ((), ())), preferred_element_type=jnp.float32
    )


class Line:
    def __init__(self):
        size = lax.axis_size("tp")
        rank = lax.axis_index("tp")
        self.stepped = size == 4 * cores
        if not self.stepped:
            self.ranks = jnp.arange(size)
            return
        place, core = rank // cores, rank % cores
        self.middle = jnp.logical_or(place == 1, place == 2)
        held = jnp.array([[0, 1, 2, 3], [1, 0, 2, 3], [2, 3, 1, 0], [3, 2, 1, 0]])[place]
        self.ranks = jnp.concatenate([held * cores + core, held * cores + 1 - core])

    def move(self, block, pairs):
        every = [(a * cores + c, b * cores + c) for a, b in pairs for c in range(cores)]
        return lax.ppermute(block, "tp", every)

    def swap(self, block):
        pairs = [(a, a + 1 - 2 * (a % cores)) for a in range(4 * cores)]
        return lax.ppermute(block, "tp", pairs)

    def outer(self, block):
        return self.move(block, [(0, 1), (1, 0), (2, 3), (3, 2)])

    def outward(self, block):
        return self.move(block, [(1, 0), (2, 3)])

    def inward(self, block):
        return self.move(block, [(0, 1), (3, 2)])

    def inner(self, block):
        return self.move(block, [(1, 2), (2, 1)])

    def gather(self, block):
        if not self.stepped:
            return (yield lax.all_gather(block, "tp", axis=0, tiled=True))
        first, near = yield self.outer(block), self.inner(block)
        second, cross, first, near = yield self.outward(near), self.inner(first), first, near
        middle = jnp.where(self.middle, near, second)
        head = self.swap(jnp.concatenate([block, first, middle], 0))
        third, cross, middle, head = yield self.outward(cross), cross, middle, head
        last = jnp.where(self.middle, cross, third)
        tail, last, head = yield self.swap(last), last, head
        return jnp.concatenate([block, first, middle, last, head, tail], 0)

    def scatter(self, partial):
        if not self.stepped:
            return (
                yield lax.psum_scatter(partial, "tp", scatter_dimension=0, tiled=True)
            ).astype(jnp.float32)
        half = partial.shape[0] // cores
        rows = half // 4
        got = yield self.swap(partial[half:])
        both = partial[:half].astype(jnp.float32) + got.astype(jnp.float32)
        part = [both[i * rows : (i + 1) * rows] for i in range(4)]
        sent = [p.astype(jnp.bfloat16) for p in part]
        came = yield self.inward(sent[3])
        third = part[3] + came.astype(jnp.float32)
        came, second = yield self.inner(third.astype(jnp.bfloat16)), self.inward(sent[2])
        first = (part[1] + came.astype(jnp.float32)).astype(jnp.bfloat16)
        middle = (part[2] + second.astype(jnp.float32)).astype(jnp.bfloat16)
        outer, inner = yield self.outer(first), self.inner(middle)
        return part[0] + outer.astype(jnp.float32) + inner.astype(jnp.float32)


def together(*works):
    results = [None] * len(works)
    replies = [None] * len(works)
    active = list(range(len(works)))
    while active:
        pending = {}
        for i in list(active):
            try:
                pending[i] = works[i].send(replies[i])
            except StopIteration as stop:
                results[i] = stop.value
                active.remove(i)
        if pending:
            done = [r for r in range(len(works)) if r not in pending]
            held = lax.optimization_barrier(([pending[i] for i in pending], [results[r] for r in done]))
            for i, reply in zip(pending, held[0]):
                replies[i] = reply
            for r, value in zip(done, held[1]):
                results[r] = value
    return results


def per_device(
    vision_in,
    vis_gain,
    first_weight,
    second_weight,
    layer_scale,
    proj_gain,
    proj_weight,
    text_embed,
    dest_row,
    cotangent,
):
    line = Line()
    groups = lax.axis_size("grp")
    grp_rank = lax.axis_index("grp")
    seq_len, width = text_embed.shape
    merged_total = dest_row.shape[0] // groups
    image_rows = merged_total // images
    own_rows, vis_width = vision_in.shape
    merged_width = proj_gain.shape[0]
    fold = merged_width // vis_width
    merged_own = own_rows // fold
    rows = own_rows // chunks
    merged_rows = rows // fold

    starts = dest_row.reshape(groups, images, image_rows)[:, :, 0]
    start_seq = starts // seq_len
    start_pos = starts % seq_len
    mine_seq = lax.dynamic_index_in_dim(start_seq, grp_rank, 0, False)
    shift = (mine_seq - grp_rank) % groups
    matches = shift[None, :] == jnp.arange(groups)[:, None]
    image_of = jnp.argmax(matches, 1)
    used = jnp.any(matches, 1)
    spot = [start_pos[(grp_rank - s) % groups, image_of[s]] for s in range(groups)]
    span = jnp.arange(image_rows)

    picked = []
    for s in range(groups):
        block = jnp.take(cotangent, spot[s] + span, axis=0)
        if s:
            block = lax.ppermute(block, "grp", [(g, (g - s) % groups) for g in range(groups)])
        picked.append(block)
    returned = jnp.concatenate(picked, 0)

    held_row = (line.ranks[:, None] * merged_own + jnp.arange(merged_rows)).reshape(-1)
    natural = jnp.arange(merged_total)
    rank_of = natural // merged_own
    inside = natural % merged_own
    block_of = jnp.argmax(line.ranks[None, :] == rank_of[:, None], 1)
    row_in = block_of * merged_rows + inside % merged_rows
    row_at = inside // merged_rows * (merged_total // chunks) + row_in

    x, hat, inv, normed = [], [], [], []
    for c in range(chunks):
        x.append(vision_in[c * rows : (c + 1) * rows].astype(jnp.float32))
        scaled, own_hat, own_inv = layer_norm(x[c], vis_gain, vis_eps)
        normed.append(scaled.astype(jnp.bfloat16))
        hat.append(own_hat)
        inv.append(own_inv)

    def vision_mlp(patches):
        pre = yield jnp.dot(patches, first_weight, preferred_element_type=jnp.float32)
        hidden = jax.nn.gelu(pre, approximate=False).astype(jnp.bfloat16)
        summed = jnp.dot(hidden, second_weight, preferred_element_type=jnp.float32)
        summed, pre = yield summed.astype(jnp.bfloat16), pre
        return summed, pre

    def merge(c, summed):
        outputs = (x[c] + layer_scale * summed).astype(jnp.bfloat16)
        merged = outputs.reshape(merged_rows, merged_width).astype(jnp.float32)
        scaled, own_hat, own_inv = layer_norm(merged, proj_gain, proj_eps)
        return scaled.astype(jnp.bfloat16), own_hat, own_inv

    def project(c, merged):
        row = held_row + c * merged_rows
        from_row = jnp.take(shift, row // image_rows) * image_rows + row % image_rows
        grad_proj = jnp.take(returned, from_row, axis=0).astype(jnp.float32)
        pre = jnp.dot(merged, proj_weight, preferred_element_type=jnp.float32)
        projected = jax.nn.gelu(pre, approximate=False).astype(jnp.bfloat16)
        delta = (grad_proj * gelu_slope(pre)).astype(jnp.bfloat16)
        delta, projected = yield delta, projected
        back = times_transposed(delta, proj_weight).astype(jnp.bfloat16)
        back, projected = yield back, projected
        return back, projected

    def unmerge(back_sum, own_hat, own_inv):
        merged_grad = norm_back(back_sum, proj_gain, own_hat, own_inv).astype(jnp.bfloat16)
        own_grad = merged_grad.reshape(rows, vis_width).astype(jnp.float32)
        return own_grad, (own_grad * layer_scale).astype(jnp.bfloat16)

    def vision_back(grad_out, pre):
        hidden_grad = times_transposed(grad_out, second_weight)
        delta = yield (hidden_grad * gelu_slope(pre)).astype(jnp.bfloat16)
        back = yield times_transposed(delta, first_weight).astype(jnp.bfloat16)
        return back

    def finish(c, own_grad, normed_grad):
        return own_grad + norm_back(normed_grad, vis_gain, hat[c], inv[c])

    (patches_a,) = together(line.gather(normed[0]))
    patches_a, normed[1] = lax.optimization_barrier((patches_a, normed[1]))
    (part_a, pre_a), patches_b = together(vision_mlp(patches_a), line.gather(normed[1]))
    summed_a, (part_b, pre_b) = together(line.scatter(part_a), vision_mlp(patches_b))
    mixed_a, mixed_hat_a, mixed_inv_a = merge(0, summed_a)
    summed_b, merged_a = together(line.scatter(part_b), line.gather(mixed_a))
    mixed_b, mixed_hat_b, mixed_inv_b = merge(1, summed_b)
    (back_a, projected_a), merged_b = together(project(0, merged_a), line.gather(mixed_b))
    back_a, (back_b, projected_b) = together(line.scatter(back_a), project(1, merged_b))

    projected = jnp.concatenate([projected_a, projected_b], 0)
    seq_embed = text_embed
    for s in range(groups):
        block = jnp.take(projected, jnp.take(row_at, image_of[s] * image_rows + span), axis=0)
        if s:
            block = lax.ppermute(block, "grp", [(g, (g + s) % groups) for g in range(groups)])
        if groups > images:
            there = lax.dynamic_slice_in_dim(seq_embed, spot[s], image_rows, 0)
            block = jnp.where(used[s], block, there)
        seq_embed = lax.dynamic_update_slice_in_dim(seq_embed, block, spot[s], 0)

    own_a, scaled_a = unmerge(back_a, mixed_hat_a, mixed_inv_a)
    back_b, grad_out_a = together(line.scatter(back_b), line.gather(scaled_a))
    own_b, scaled_b = unmerge(back_b, mixed_hat_b, mixed_inv_b)
    deep_a, grad_out_b = together(vision_back(grad_out_a, pre_a), line.gather(scaled_b))
    deep_a, deep_b = together(line.scatter(deep_a), vision_back(grad_out_b, pre_b))
    (deep_b,) = together(line.scatter(deep_b))
    grads = [finish(0, own_a, deep_a), finish(1, own_b, deep_b)]
    grad_vision = jnp.concatenate(grads, 0).astype(jnp.bfloat16)
    return (seq_embed, grad_vision)


def solution(mesh):
    placed = (
        P(("grp", "tp"), None),
        P(),
        P(None, "tp"),
        P("tp", None),
        P(),
        P(),
        P(None, "tp"),
        P("grp", "tp"),
        P(),
        P("grp", "tp"),
    )
    return jax.shard_map(
        per_device,
        mesh=mesh,
        in_specs=placed,
        out_specs=(P("grp", "tp"), P(("grp", "tp"), None)),
        check_vma=False,
    )
```

```python
import jax
import jax.numpy as jnp
from jax import lax
from jax.sharding import PartitionSpec as P

vis_eps = 1e-06
proj_eps = 1e-05
chunks = 2
images = 4
cores = 2


def layer_norm(values, scale_vec, epsilon):
    mean_val = jnp.mean(values, -1, keepdims=True)
    centred = values - mean_val
    inv_std = lax.rsqrt(jnp.mean(centred * centred, -1, keepdims=True) + epsilon)
    normed = centred * inv_std
    return (normed * scale_vec, normed, inv_std)


def norm_back(upstream, scale_vec, normed, inv_std):
    scaled = upstream * scale_vec
    return inv_std * (
        scaled
        - jnp.mean(scaled, -1, keepdims=True)
        - normed * jnp.mean(scaled * normed, -1, keepdims=True)
    )


def gelu_slope(values):
    cumul = 0.5 * (1.0 + lax.erf(values * 0.7071067811865476))
    dense = jnp.exp(-0.5 * values * values) * 0.3989422804014327
    return cumul + values * dense


def times_transposed(left, right):
    return lax.dot_general(
        left, right, (((1,), (1,)), ((), ())), preferred_element_type=jnp.float32
    )


def after(values, *tokens):
    return lax.optimization_barrier((values, tokens))[0]


class Whole:
    def gather(self, block):
        return lax.all_gather(block, "tp", axis=0, tiled=True)

    def scatter(self, partial):
        summed = lax.psum_scatter(partial, "tp", scatter_dimension=0, tiled=True)
        return summed.astype(jnp.float32)

    def by_rank(self, rows, size):
        return rows.reshape(size, -1, rows.shape[-1])

    def by_row(self, ranks):
        return ranks.reshape(-1, ranks.shape[-1])


class Rails:
    def __init__(self):
        size = lax.axis_size("tp")
        self.places = size // cores
        self.lead = lax.axis_index("tp") % cores == 0
        self.groups = [list(range(c, size, cores)) for c in range(cores)]
        self.pairs = [(a, a + 1 - 2 * (a % cores)) for a in range(size)]

    def exchange(self, blocks):
        return lax.all_to_all(
            blocks, "tp", split_axis=0, concat_axis=0, axis_index_groups=self.groups, tiled=True
        )

    def gather(self, block):
        mine = self.exchange(jnp.concatenate([block] * self.places, 0))
        other = lax.ppermute(mine, "tp", self.pairs)
        return jnp.concatenate(
            [jnp.where(self.lead, mine, other), jnp.where(self.lead, other, mine)], 0
        )

    def scatter(self, partial):
        half = partial.shape[0] // cores
        low, high = partial[:half], partial[half:]
        got = lax.ppermute(jnp.where(self.lead, high, low), "tp", self.pairs)
        mine = jnp.where(self.lead, low, high).astype(jnp.float32) + got.astype(jnp.float32)
        came = self.exchange(mine.astype(jnp.bfloat16)).astype(jnp.float32)
        return jnp.sum(came.reshape(self.places, half // self.places, -1), 0)

    def by_rank(self, rows, size):
        width = rows.shape[-1]
        split = rows.reshape(cores, self.places, -1, width)
        return jnp.swapaxes(split, 0, 1).reshape(size, -1, width)

    def by_row(self, ranks):
        size, _, width = ranks.shape
        split = ranks.reshape(self.places, cores, -1, width)
        return jnp.swapaxes(split, 0, 1).reshape(-1, width)


def per_device(
    vision_in,
    vis_gain,
    first_weight,
    second_weight,
    layer_scale,
    proj_gain,
    proj_weight,
    text_embed,
    dest_row,
    cotangent,
):
    moves = [Whole(), Rails()]
    groups = lax.axis_size("grp")
    size = lax.axis_size("tp")
    grp_rank = lax.axis_index("grp")
    seq_len, width = text_embed.shape
    merged_total = dest_row.shape[0] // groups
    image_rows = merged_total // images
    own_rows, vis_width = vision_in.shape
    merged_width = proj_gain.shape[0]
    fold = merged_width // vis_width
    rows = own_rows // chunks
    merged_rows = rows // fold

    x, hat, inv, normed = [], [], [], []
    for c in range(chunks):
        x.append(vision_in[c * rows : (c + 1) * rows].astype(jnp.float32))
        scaled, own_hat, own_inv = layer_norm(x[c], vis_gain, vis_eps)
        normed.append(scaled.astype(jnp.bfloat16))
        hat.append(own_hat)
        inv.append(own_inv)
    patches_a = moves[0].gather(normed[0])
    patches_b = moves[1].gather(normed[1])

    starts = dest_row.reshape(groups, images, image_rows)[:, :, 0]
    start_pos = starts % seq_len
    shift = starts[0] // seq_len
    matches = (shift[None, :] == jnp.arange(groups)[:, None]).astype(jnp.int32)
    image_of = jnp.sum(matches * jnp.arange(images), 1)
    used = jnp.sum(matches, 1) > 0
    source = (grp_rank - jnp.arange(groups)) % groups
    from_group = (source[:, None] == jnp.arange(groups)).astype(jnp.int32)
    spot = jnp.sum(matches[:, None, :] * from_group[:, :, None] * start_pos[None], (1, 2))

    picked = []
    for s in range(groups):
        block = lax.dynamic_slice_in_dim(cotangent, spot[s], image_rows, 0)
        if s:
            block = lax.ppermute(block, "grp", [(g, (g - s) % groups) for g in range(groups)])
        picked.append(block)
    returned = jnp.take(jnp.stack(picked), shift, axis=0).reshape(size, -1, width)
    grad_proj = [
        moves[c].by_row(returned[:, c * merged_rows : (c + 1) * merged_rows]) for c in range(chunks)
    ]

    def vision_mlp(patches):
        pre = jnp.dot(patches, first_weight, preferred_element_type=jnp.float32)
        hidden = jax.nn.gelu(pre, approximate=False).astype(jnp.bfloat16)
        summed = jnp.dot(hidden, second_weight, preferred_element_type=jnp.float32)
        return summed.astype(jnp.bfloat16), pre

    def merge(c, summed):
        outputs = (x[c] + layer_scale * summed).astype(jnp.bfloat16)
        merged = outputs.reshape(merged_rows, merged_width).astype(jnp.float32)
        scaled, own_hat, own_inv = layer_norm(merged, proj_gain, proj_eps)
        return scaled.astype(jnp.bfloat16), own_hat, own_inv

    def project(c, merged):
        pre = jnp.dot(merged, proj_weight, preferred_element_type=jnp.float32)
        projected = jax.nn.gelu(pre, approximate=False).astype(jnp.bfloat16)
        delta = (grad_proj[c].astype(jnp.float32) * gelu_slope(pre)).astype(jnp.bfloat16)
        return times_transposed(delta, proj_weight).astype(jnp.bfloat16), projected

    def unmerge(back_sum, own_hat, own_inv):
        merged_grad = norm_back(back_sum, proj_gain, own_hat, own_inv).astype(jnp.bfloat16)
        own_grad = merged_grad.reshape(rows, vis_width).astype(jnp.float32)
        return own_grad, (own_grad * layer_scale).astype(jnp.bfloat16)

    def vision_back(grad_out, pre):
        hidden_grad = times_transposed(grad_out, second_weight)
        delta = (hidden_grad * gelu_slope(pre)).astype(jnp.bfloat16)
        return times_transposed(delta, first_weight).astype(jnp.bfloat16)

    part_b, pre_b = vision_mlp(patches_b)
    summed_b = moves[1].scatter(part_b)
    part_a, pre_a = vision_mlp(after(patches_a, part_b))
    summed_a = moves[0].scatter(part_a)
    mixed_b, *stats_b = merge(1, after(summed_b, part_a))
    merged_b = moves[1].gather(mixed_b)
    mixed_a, *stats_a = merge(0, after(summed_a, mixed_b))
    merged_a = moves[0].gather(mixed_a)
    back_b, projected_b = project(1, after(merged_b, mixed_a))
    summed_b = moves[1].scatter(back_b)
    back_a, projected_a = project(0, after(merged_a, back_b))
    summed_a = moves[0].scatter(back_a)

    projected = jnp.concatenate(
        [moves[0].by_rank(projected_a, size), moves[1].by_rank(projected_b, size)], 1
    ).reshape(images, image_rows, width)
    seq_embed = text_embed
    for s in range(groups):
        block = lax.dynamic_index_in_dim(projected, image_of[s], 0, False)
        if s:
            block = lax.ppermute(block, "grp", [(g, (g + s) % groups) for g in range(groups)])
        if groups > images:
            there = lax.dynamic_slice_in_dim(seq_embed, spot[s], image_rows, 0)
            block = jnp.where(used[s], block, there)
        seq_embed = lax.dynamic_update_slice_in_dim(seq_embed, block, spot[s], 0)

    own_b, scaled_b = unmerge(after(summed_b, back_a), *stats_b)
    grad_out_b = moves[1].gather(scaled_b)
    own_a, scaled_a = unmerge(after(summed_a, scaled_b), *stats_a)
    grad_out_a = moves[0].gather(scaled_a)
    deep_b = vision_back(after(grad_out_b, scaled_a), pre_b)
    normed_b = moves[1].scatter(deep_b)
    deep_a = vision_back(after(grad_out_a, deep_b), pre_a)
    normed_a = moves[0].scatter(deep_a)
    normed_b, seq_embed = after((normed_b, seq_embed), deep_a)
    grads = [
        own_a + norm_back(normed_a, vis_gain, hat[0], inv[0]),
        own_b + norm_back(normed_b, vis_gain, hat[1], inv[1]),
    ]
    grad_vision = jnp.concatenate(grads, 0).astype(jnp.bfloat16)
    return (seq_embed, grad_vision)


def solution(mesh):
    placed = (
        P(("grp", "tp"), None),
        P(),
        P(None, "tp"),
        P("tp", None),
        P(),
        P(),
        P(None, "tp"),
        P("grp", "tp"),
        P(),
        P("grp", "tp"),
    )
    return jax.shard_map(
        per_device,
        mesh=mesh,
        in_specs=placed,
        out_specs=(P("grp", "tp"), P(("grp", "tp"), None)),
        check_vma=False,
    )
```

```python
import functools

import jax
import jax.numpy as jnp
from jax import lax
from jax.experimental import pallas as pl
from jax.experimental.pallas import tpu as pltpu
from jax.sharding import PartitionSpec as P

vis_eps = 1e-06
proj_eps = 1e-05
chunks = 2
images = 4
cores = 2


def layer_norm(values, scale_vec, epsilon):
    mean_val = jnp.mean(values, -1, keepdims=True)
    centred = values - mean_val
    inv_std = lax.rsqrt(jnp.mean(centred * centred, -1, keepdims=True) + epsilon)
    normed = centred * inv_std
    return (normed * scale_vec, normed, inv_std)


def norm_back(upstream, scale_vec, normed, inv_std):
    scaled = upstream * scale_vec
    return inv_std * (
        scaled
        - jnp.mean(scaled, -1, keepdims=True)
        - normed * jnp.mean(scaled * normed, -1, keepdims=True)
    )


def times_transposed(left, right):
    return lax.dot_general(
        left, right, (((1,), (1,)), ((), ())), preferred_element_type=jnp.float32
    )


def tile_of(length, most):
    return max(t for t in range(128, most + 1, 128) if length % t == 0)


def laid(pieces):
    if len(pieces) == 1:
        return pieces[0][...]
    if pieces[0].shape[0] % 16 == 0:
        return jnp.concatenate([p[...] for p in pieces], 0)
    return jnp.concatenate([p[...].astype(jnp.float32) for p in pieces], 0).astype(jnp.bfloat16)


def each_rows(total, body):
    step = 16 if total % 16 == 0 else total

    def run(i, _):
        body(pl.ds(pl.multiple_of(i * step, step), step))
        return 0

    lax.fori_loop(0, total // step, run, 0)


def forward_kernel(count, steps, *refs):
    pieces = refs[:count]
    first, second, out, slope, pre, hidden = refs[count:]
    i = pl.program_id(0)

    @pl.when(i == 0)
    def _():
        pre[...] = jnp.dot(laid(pieces), first[...], preferred_element_type=jnp.float32)

    @pl.when(jnp.logical_and(i > 0, i < steps))
    def _():
        pre[...] += jnp.dot(laid(pieces), first[...], preferred_element_type=jnp.float32)

    @pl.when(i == steps - 1)
    def _():
        def act(sel):
            u = pre[sel, :]
            cumul = 0.5 * (1.0 + lax.erf(u * 0.7071067811865476))
            dense = jnp.exp(-0.5 * u * u) * 0.3989422804014327
            hidden[sel, :] = (u * cumul).astype(jnp.bfloat16)
            slope[sel, :] = cumul + u * dense

        each_rows(pre.shape[0], act)

    @pl.when(i >= steps)
    def _():
        out[...] = jnp.dot(
            hidden[...], second[...], preferred_element_type=jnp.float32
        ).astype(jnp.bfloat16)


def backward_kernel(count, steps, *refs):
    pieces = refs[:count]
    first, second, slope, out, total, delta = refs[count:]
    i = pl.program_id(0)

    @pl.when(i == 0)
    def _():
        total[...] = times_transposed(laid(pieces), second[...])

    @pl.when(jnp.logical_and(i > 0, i < steps))
    def _():
        total[...] += times_transposed(laid(pieces), second[...])

    @pl.when(i == steps - 1)
    def _():
        def act(sel):
            delta[sel, :] = (total[sel, :] * slope[sel, :]).astype(jnp.bfloat16)

        each_rows(total.shape[0], act)

    @pl.when(i >= steps)
    def _():
        out[...] = times_transposed(delta[...], first[...]).astype(jnp.bfloat16)


def project_kernel(count, chunk, *refs):
    pieces = refs[:count]
    weight, upstream, projected, back, rows, total = refs[count:]
    i = pl.program_id(0)
    depth = weight.shape[0]

    @pl.when(i == 0)
    def _():
        total[...] = jnp.zeros_like(total)
        rows[...] = laid(pieces)

    def ahead(k, pre):
        sel = pl.ds(pl.multiple_of(k * chunk, 128), chunk)
        return pre + jnp.dot(rows[:, sel], weight[sel, :], preferred_element_type=jnp.float32)

    u = lax.fori_loop(0, depth // chunk, ahead, jnp.zeros(projected.shape, jnp.float32))
    cumul = 0.5 * (1.0 + lax.erf(u * 0.7071067811865476))
    dense = jnp.exp(-0.5 * u * u) * 0.3989422804014327
    projected[...] = (u * cumul).astype(jnp.bfloat16)
    delta = (upstream[...].astype(jnp.float32) * (cumul + u * dense)).astype(jnp.bfloat16)

    def behind(k, _):
        sel = pl.ds(pl.multiple_of(k * chunk, 128), chunk)
        total[:, sel] += times_transposed(delta, weight[sel, :])
        return 0

    lax.fori_loop(0, depth // chunk, behind, 0)

    @pl.when(i == pl.num_programs(0) - 1)
    def _():
        back[...] = total[...].astype(jnp.bfloat16)


def settings(limit):
    return pltpu.CompilerParams(
        vmem_limit_bytes=limit * 1024 * 1024, dimension_semantics=("arbitrary",)
    )


def vision_mlp(pieces, first, second):
    rows = sum(p.shape[0] for p in pieces)
    width, units = first.shape
    tile = tile_of(width, 640)
    steps = width // tile
    early = lambda i: jnp.minimum(i, steps - 1)
    late = lambda i: jnp.maximum(i - steps, 0)
    return pl.pallas_call(
        functools.partial(forward_kernel, len(pieces), steps),
        grid=(2 * steps,),
        in_specs=[pl.BlockSpec((p.shape[0], tile), lambda i: (0, early(i))) for p in pieces]
        + [
            pl.BlockSpec((tile, units), lambda i: (early(i), 0)),
            pl.BlockSpec((units, tile), lambda i: (0, late(i))),
        ],
        out_specs=[
            pl.BlockSpec((rows, tile), lambda i: (0, late(i))),
            pl.BlockSpec((rows, units), lambda i: (0, 0)),
        ],
        out_shape=[
            jax.ShapeDtypeStruct((rows, width), jnp.bfloat16),
            jax.ShapeDtypeStruct((rows, units), jnp.float32),
        ],
        scratch_shapes=[
            pltpu.VMEM((rows, units), jnp.float32),
            pltpu.VMEM((rows, units), jnp.bfloat16),
        ],
        compiler_params=settings(28),
        cost_estimate=pl.CostEstimate(
            flops=4 * rows * width * units,
            bytes_accessed=4 * width * units + 4 * rows * (width + units),
            transcendentals=2 * rows * units,
        ),
    )(*pieces, first, second)


def vision_back(pieces, first, second, slope):
    rows = sum(p.shape[0] for p in pieces)
    width, units = first.shape
    tile = tile_of(width, 640)
    steps = width // tile
    early = lambda i: jnp.minimum(i, steps - 1)
    late = lambda i: jnp.maximum(i - steps, 0)
    return pl.pallas_call(
        functools.partial(backward_kernel, len(pieces), steps),
        grid=(2 * steps,),
        in_specs=[pl.BlockSpec((p.shape[0], tile), lambda i: (0, early(i))) for p in pieces]
        + [
            pl.BlockSpec((tile, units), lambda i: (late(i), 0)),
            pl.BlockSpec((units, tile), lambda i: (0, early(i))),
            pl.BlockSpec((rows, units), lambda i: (0, 0)),
        ],
        out_specs=pl.BlockSpec((rows, tile), lambda i: (0, late(i))),
        out_shape=jax.ShapeDtypeStruct((rows, width), jnp.bfloat16),
        scratch_shapes=[
            pltpu.VMEM((rows, units), jnp.float32),
            pltpu.VMEM((rows, units), jnp.bfloat16),
        ],
        compiler_params=settings(28),
        cost_estimate=pl.CostEstimate(
            flops=4 * rows * width * units,
            bytes_accessed=4 * width * units + 4 * rows * (width + units),
            transcendentals=0,
        ),
    )(*pieces, first, second, slope)


def project(pieces, weight, upstream):
    rows = sum(p.shape[0] for p in pieces)
    depth, units = weight.shape
    tile = tile_of(units, 256)
    return pl.pallas_call(
        functools.partial(project_kernel, len(pieces), tile_of(depth, 2560)),
        grid=(units // tile,),
        in_specs=[pl.BlockSpec(p.shape, lambda i: (0, 0)) for p in pieces]
        + [
            pl.BlockSpec((depth, tile), lambda i: (0, i)),
            pl.BlockSpec((rows, tile), lambda i: (0, i)),
        ],
        out_specs=[
            pl.BlockSpec((rows, tile), lambda i: (0, i)),
            pl.BlockSpec((rows, depth), lambda i: (0, 0)),
        ],
        out_shape=[
            jax.ShapeDtypeStruct((rows, units), jnp.bfloat16),
            jax.ShapeDtypeStruct((rows, depth), jnp.bfloat16),
        ],
        scratch_shapes=[
            pltpu.VMEM((rows, depth), jnp.bfloat16),
            pltpu.VMEM((rows, depth), jnp.float32),
        ],
        compiler_params=settings(40),
        cost_estimate=pl.CostEstimate(
            flops=4 * rows * depth * units,
            bytes_accessed=2 * depth * units + 4 * rows * (depth + units),
            transcendentals=2 * rows * units,
        ),
    )(*pieces, weight, upstream)


def after(values, *tokens):
    return lax.optimization_barrier((values, tokens))[0]


class Whole:
    def gather(self, block):
        return [lax.all_gather(block, "tp", axis=0, tiled=True)]

    def scatter(self, partial):
        summed = lax.psum_scatter(partial, "tp", scatter_dimension=0, tiled=True)
        return summed.astype(jnp.float32)

    def by_rank(self, rows, size):
        return rows.reshape(size, -1, rows.shape[-1])

    def by_row(self, ranks):
        return ranks.reshape(-1, ranks.shape[-1])


class Direct:
    def __init__(self):
        self.size = lax.axis_size("tp")
        self.places = self.size // cores
        rank = lax.axis_index("tp")
        place, core = rank // cores, rank % cores
        back = (place - jnp.arange(self.places)) % self.places * cores
        self.ranks = jnp.concatenate([back + core, back + 1 - core])
        every = jnp.arange(self.size)
        far = (every + core) % cores * self.places
        self.blocks = far + (place - every // cores) % self.places
        self.pairs = [(a, a + 1 - 2 * (a % cores)) for a in range(self.size)]

    def shift(self, block, k):
        pairs = [(a, (a + k * cores) % self.size) for a in range(self.size)]
        return lax.ppermute(block, "tp", pairs)

    def gather(self, block):
        mine = [block] + [self.shift(block, k) for k in range(1, self.places)]
        other = [lax.ppermute(m, "tp", self.pairs) for m in mine]
        if block.shape[0] % 8:
            return [jnp.concatenate(mine + other, 0)]
        return mine + other

    def scatter(self, partial):
        half = partial.shape[0] // cores
        rows = half // self.places
        got = lax.ppermute(partial[half:], "tp", self.pairs)
        both = partial[:half].astype(jnp.float32) + got.astype(jnp.float32)
        total = both[:rows]
        for k in range(1, self.places):
            sent = both[k * rows : (k + 1) * rows].astype(jnp.bfloat16)
            total = total + self.shift(sent, -k).astype(jnp.float32)
        return total

    def by_rank(self, rows, size):
        return jnp.take(rows.reshape(size, -1, rows.shape[-1]), self.blocks, axis=0)

    def by_row(self, ranks):
        return jnp.take(ranks, self.ranks, axis=0).reshape(-1, ranks.shape[-1])


def per_device(
    vision_in,
    vis_gain,
    first_weight,
    second_weight,
    layer_scale,
    proj_gain,
    proj_weight,
    text_embed,
    dest_row,
    cotangent,
):
    moves = [Whole(), Direct()]
    groups = lax.axis_size("grp")
    size = lax.axis_size("tp")
    grp_rank = lax.axis_index("grp")
    seq_len, width = text_embed.shape
    merged_total = dest_row.shape[0] // groups
    image_rows = merged_total // images
    own_rows, vis_width = vision_in.shape
    merged_width = proj_gain.shape[0]
    fold = merged_width // vis_width
    rows = own_rows // chunks
    merged_rows = rows // fold

    x, hat, inv, normed = [], [], [], []
    for c in range(chunks):
        x.append(vision_in[c * rows : (c + 1) * rows].astype(jnp.float32))
        scaled, own_hat, own_inv = layer_norm(x[c], vis_gain, vis_eps)
        normed.append(scaled.astype(jnp.bfloat16))
        hat.append(own_hat)
        inv.append(own_inv)
    patches_a = moves[0].gather(normed[0])
    patches_b = moves[1].gather(normed[1])

    starts = dest_row.reshape(groups, images, image_rows)[:, :, 0]
    start_pos = starts % seq_len
    shift = starts[0] // seq_len
    matches = (shift[None, :] == jnp.arange(groups)[:, None]).astype(jnp.int32)
    image_of = jnp.sum(matches * jnp.arange(images), 1)
    used = jnp.sum(matches, 1) > 0
    source = (grp_rank - jnp.arange(groups)) % groups
    from_group = (source[:, None] == jnp.arange(groups)).astype(jnp.int32)
    spot = jnp.sum(matches[:, None, :] * from_group[:, :, None] * start_pos[None], (1, 2))

    picked = []
    for s in range(groups):
        block = lax.dynamic_slice_in_dim(cotangent, spot[s], image_rows, 0)
        if s:
            block = lax.ppermute(block, "grp", [(g, (g - s) % groups) for g in range(groups)])
        picked.append(block)
    returned = jnp.take(jnp.stack(picked), shift, axis=0).reshape(size, -1, width)
    grad_proj = [
        moves[c].by_row(returned[:, c * merged_rows : (c + 1) * merged_rows]) for c in range(chunks)
    ]

    def merge(c, summed):
        outputs = (x[c] + layer_scale * summed).astype(jnp.bfloat16)
        merged = outputs.reshape(merged_rows, merged_width).astype(jnp.float32)
        scaled, own_hat, own_inv = layer_norm(merged, proj_gain, proj_eps)
        return scaled.astype(jnp.bfloat16), own_hat, own_inv

    def unmerge(back_sum, own_hat, own_inv):
        merged_grad = norm_back(back_sum, proj_gain, own_hat, own_inv).astype(jnp.bfloat16)
        own_grad = merged_grad.reshape(rows, vis_width).astype(jnp.float32)
        return own_grad, (own_grad * layer_scale).astype(jnp.bfloat16)

    part_b, slope_b = vision_mlp(patches_b, first_weight, second_weight)
    summed_b = moves[1].scatter(part_b)
    patches_a = after(patches_a, part_b)
    part_a, slope_a = vision_mlp(patches_a, first_weight, second_weight)
    summed_a = moves[0].scatter(part_a)
    mixed_b, *stats_b = merge(1, after(summed_b, part_a))
    merged_b = moves[1].gather(mixed_b)
    mixed_a, *stats_a = merge(0, after(summed_a, mixed_b))
    merged_a = moves[0].gather(mixed_a)
    projected_b, back_b = project(after(merged_b, mixed_a), proj_weight, grad_proj[1])
    summed_b = moves[1].scatter(back_b)
    projected_a, back_a = project(after(merged_a, back_b), proj_weight, grad_proj[0])
    summed_a = moves[0].scatter(back_a)

    projected = jnp.concatenate(
        [moves[0].by_rank(projected_a, size), moves[1].by_rank(projected_b, size)], 1
    ).reshape(images, image_rows, width)
    seq_embed = text_embed
    for s in range(groups):
        block = lax.dynamic_index_in_dim(projected, image_of[s], 0, False)
        if s:
            block = lax.ppermute(block, "grp", [(g, (g + s) % groups) for g in range(groups)])
        if groups > images:
            there = lax.dynamic_slice_in_dim(seq_embed, spot[s], image_rows, 0)
            block = jnp.where(used[s], block, there)
        seq_embed = lax.dynamic_update_slice_in_dim(seq_embed, block, spot[s], 0)

    own_b, scaled_b = unmerge(after(summed_b, back_a), *stats_b)
    grad_out_b = moves[1].gather(scaled_b)
    own_a, scaled_a = unmerge(after(summed_a, scaled_b), *stats_a)
    grad_out_a = moves[0].gather(scaled_a)
    grad_out_b = after(grad_out_b, scaled_a)
    deep_b = vision_back(grad_out_b, first_weight, second_weight, slope_b)
    normed_b = moves[1].scatter(deep_b)
    grad_out_a = after(grad_out_a, deep_b)
    deep_a = vision_back(grad_out_a, first_weight, second_weight, slope_a)
    normed_a = moves[0].scatter(deep_a)
    normed_b, seq_embed = after((normed_b, seq_embed), deep_a)
    grads = [
        own_a + norm_back(normed_a, vis_gain, hat[0], inv[0]),
        own_b + norm_back(normed_b, vis_gain, hat[1], inv[1]),
    ]
    grad_vision = jnp.concatenate(grads, 0).astype(jnp.bfloat16)
    return (seq_embed, grad_vision)


def solution(mesh):
    placed = (
        P(("grp", "tp"), None),
        P(),
        P(None, "tp"),
        P("tp", None),
        P(),
        P(),
        P(None, "tp"),
        P("grp", "tp"),
        P(),
        P("grp", "tp"),
    )
    return jax.shard_map(
        per_device,
        mesh=mesh,
        in_specs=placed,
        out_specs=(P("grp", "tp"), P(("grp", "tp"), None)),
        check_vma=False,
    )
```

```python
import functools

import jax
import jax.numpy as jnp
from jax import lax
from jax.experimental import pallas as pl
from jax.experimental.pallas import tpu as pltpu
from jax.sharding import PartitionSpec as P

vis_eps = 1e-06
proj_eps = 1e-05
chunks = 2
images = 4
cores = 2


def layer_norm(values, scale_vec, epsilon):
    mean_val = jnp.mean(values, -1, keepdims=True)
    centred = values - mean_val
    inv_std = lax.rsqrt(jnp.mean(centred * centred, -1, keepdims=True) + epsilon)
    normed = centred * inv_std
    return (normed * scale_vec, normed, inv_std)


def norm_back(upstream, scale_vec, normed, inv_std):
    scaled = upstream * scale_vec
    return inv_std * (
        scaled
        - jnp.mean(scaled, -1, keepdims=True)
        - normed * jnp.mean(scaled * normed, -1, keepdims=True)
    )


def times_transposed(left, right):
    return lax.dot_general(
        left, right, (((1,), (1,)), ((), ())), preferred_element_type=jnp.float32
    )


def tile_of(length, most):
    return max(t for t in range(128, most + 1, 128) if length % t == 0)


def laid(pieces):
    if len(pieces) == 1:
        return pieces[0][...]
    if pieces[0].shape[0] % 16 == 0:
        return jnp.concatenate([p[...] for p in pieces], 0)
    return jnp.concatenate([p[...].astype(jnp.float32) for p in pieces], 0).astype(jnp.bfloat16)


def each_rows(total, body):
    step = 16 if total % 16 == 0 else total

    def run(i, _):
        body(pl.ds(pl.multiple_of(i * step, step), step))
        return 0

    lax.fori_loop(0, total // step, run, 0)


def forward_kernel(count, steps, *refs):
    pieces = refs[:count]
    first, second, near, far, slope, pre, hidden = refs[count:]
    i = pl.program_id(0)

    @pl.when(i == 0)
    def _():
        pre[...] = times_transposed(laid(pieces), first[...])

    @pl.when(jnp.logical_and(i > 0, i < steps))
    def _():
        pre[...] += times_transposed(laid(pieces), first[...])

    @pl.when(i == steps - 1)
    def _():
        def act(sel):
            u = pre[sel, :]
            cumul = 0.5 * (1.0 + lax.erf(u * 0.7071067811865476))
            dense = jnp.exp(-0.5 * u * u) * 0.3989422804014327
            hidden[sel, :] = (u * cumul).astype(jnp.bfloat16)
            slope[sel, :] = cumul + u * dense

        each_rows(pre.shape[0], act)

    @pl.when(i >= steps)
    def _():
        both = jnp.dot(hidden[...], second[...], preferred_element_type=jnp.float32)
        near[...] = both[: near.shape[0]].astype(jnp.bfloat16)
        far[...] = both[near.shape[0] :].astype(jnp.bfloat16)


def backward_kernel(count, steps, *refs):
    pieces = refs[:count]
    second, first, slope, near, far, total, delta = refs[count:]
    i = pl.program_id(0)

    @pl.when(i == 0)
    def _():
        total[...] = times_transposed(laid(pieces), second[...])

    @pl.when(jnp.logical_and(i > 0, i < steps))
    def _():
        total[...] += times_transposed(laid(pieces), second[...])

    @pl.when(i == steps - 1)
    def _():
        def act(sel):
            delta[sel, :] = (total[sel, :] * slope[sel, :]).astype(jnp.bfloat16)

        each_rows(total.shape[0], act)

    @pl.when(i >= steps)
    def _():
        both = jnp.dot(delta[...], first[...], preferred_element_type=jnp.float32)
        near[...] = both[: near.shape[0]].astype(jnp.bfloat16)
        far[...] = both[near.shape[0] :].astype(jnp.bfloat16)


def project_kernel(count, chunk, *refs):
    pieces = refs[:count]
    weight, upstream, projected, near, far, rows, total = refs[count:]
    i = pl.program_id(0)
    depth = weight.shape[0]

    @pl.when(i == 0)
    def _():
        total[...] = jnp.zeros_like(total)
        rows[...] = laid(pieces)

    def ahead(k, pre):
        sel = pl.ds(pl.multiple_of(k * chunk, 128), chunk)
        return pre + jnp.dot(rows[:, sel], weight[sel, :], preferred_element_type=jnp.float32)

    u = lax.fori_loop(0, depth // chunk, ahead, jnp.zeros(projected.shape, jnp.float32))
    cumul = 0.5 * (1.0 + lax.erf(u * 0.7071067811865476))
    dense = jnp.exp(-0.5 * u * u) * 0.3989422804014327
    projected[...] = (u * cumul).astype(jnp.bfloat16)
    delta = (upstream[...].astype(jnp.float32) * (cumul + u * dense)).astype(jnp.bfloat16)

    def behind(k, _):
        sel = pl.ds(pl.multiple_of(k * chunk, 128), chunk)
        total[:, sel] += times_transposed(delta, weight[sel, :])
        return 0

    lax.fori_loop(0, depth // chunk, behind, 0)

    @pl.when(i == pl.num_programs(0) - 1)
    def _():
        half = near.shape[0]
        near[...] = total[:half].astype(jnp.bfloat16)
        far[...] = total[half:].astype(jnp.bfloat16)


def settings():
    return pltpu.CompilerParams(
        vmem_limit_bytes=56 * 1024 * 1024, dimension_semantics=("arbitrary",)
    )


def vision_pass(kernel, pieces, early, late, slope=None):
    rows = sum(p.shape[0] for p in pieces)
    units, width = early.shape
    tile = tile_of(width, 640)
    steps = width // tile
    soon = lambda i: (0, jnp.minimum(i, steps - 1))
    then = lambda i: (0, jnp.maximum(i - steps, 0))
    slopes = pl.BlockSpec((rows, units), lambda i: (0, 0))
    sums = [pl.BlockSpec((rows // 2, tile), then)] * 2
    shapes = [jax.ShapeDtypeStruct((rows // 2, width), jnp.bfloat16)] * 2
    given = [] if slope is None else [slope]
    return pl.pallas_call(
        functools.partial(kernel, len(pieces), steps),
        grid=(2 * steps,),
        in_specs=[pl.BlockSpec((p.shape[0], tile), soon) for p in pieces]
        + [pl.BlockSpec((units, tile), soon), pl.BlockSpec((units, tile), then)]
        + [slopes] * len(given),
        out_specs=sums + [slopes] * (1 - len(given)),
        out_shape=shapes + [jax.ShapeDtypeStruct((rows, units), jnp.float32)] * (1 - len(given)),
        scratch_shapes=[
            pltpu.VMEM((rows, units), jnp.float32),
            pltpu.VMEM((rows, units), jnp.bfloat16),
        ],
        compiler_params=settings(),
        cost_estimate=pl.CostEstimate(
            flops=4 * rows * width * units,
            bytes_accessed=4 * width * units + 4 * rows * (width + units),
            transcendentals=2 * rows * units,
        ),
    )(*pieces, early, late, *given)


def project(pieces, weight, upstream):
    rows = sum(p.shape[0] for p in pieces)
    depth, units = weight.shape
    tile = tile_of(units, 256)
    return pl.pallas_call(
        functools.partial(project_kernel, len(pieces), tile_of(depth, 2560)),
        grid=(units // tile,),
        in_specs=[pl.BlockSpec(p.shape, lambda i: (0, 0)) for p in pieces]
        + [
            pl.BlockSpec((depth, tile), lambda i: (0, i)),
            pl.BlockSpec((rows, tile), lambda i: (0, i)),
        ],
        out_specs=[
            pl.BlockSpec((rows, tile), lambda i: (0, i)),
            pl.BlockSpec((rows // 2, depth), lambda i: (0, 0)),
            pl.BlockSpec((rows // 2, depth), lambda i: (0, 0)),
        ],
        out_shape=[jax.ShapeDtypeStruct((rows, units), jnp.bfloat16)]
        + [jax.ShapeDtypeStruct((rows // 2, depth), jnp.bfloat16)] * 2,
        scratch_shapes=[
            pltpu.VMEM((rows, depth), jnp.bfloat16),
            pltpu.VMEM((rows, depth), jnp.float32),
        ],
        compiler_params=settings(),
        cost_estimate=pl.CostEstimate(
            flops=4 * rows * depth * units,
            bytes_accessed=2 * depth * units + 4 * rows * (depth + units),
            transcendentals=2 * rows * units,
        ),
    )(*pieces, weight, upstream)


class Direct:
    def __init__(self):
        self.size = lax.axis_size("tp")
        self.places = self.size // cores
        rank = lax.axis_index("tp")
        place, core = rank // cores, rank % cores
        back = (place - jnp.arange(self.places)) % self.places * cores
        self.ranks = jnp.concatenate([back + core, back + 1 - core])
        every = jnp.arange(self.size)
        far = (every + core) % cores * self.places
        self.blocks = far + (place - every // cores) % self.places
        self.pairs = [(a, a + 1 - 2 * (a % cores)) for a in range(self.size)]

    def shift(self, block, k):
        pairs = [(a, (a + k * cores) % self.size) for a in range(self.size)]
        return lax.ppermute(block, "tp", pairs)

    def spread(self, block):
        return [block] + [self.shift(block, k) for k in range(1, self.places)]

    def gathered(self, mine):
        other = [lax.ppermute(m, "tp", self.pairs) for m in mine]
        if mine[0].shape[0] % 8:
            return [jnp.concatenate(mine + other, 0)]
        return mine + other

    def send(self, near, far):
        rows = near.shape[0] // self.places
        got = lax.ppermute(far, "tp", self.pairs)
        both = near.astype(jnp.float32) + got.astype(jnp.float32)
        cut = [both[k * rows : (k + 1) * rows] for k in range(self.places)]
        return cut[:1] + [
            self.shift(cut[k].astype(jnp.bfloat16), -k) for k in range(1, self.places)
        ]

    def summed(self, terms):
        return sum([t.astype(jnp.float32) for t in terms[1:]], terms[0])

    def by_rank(self, rows, size):
        return jnp.take(rows.reshape(size, -1, rows.shape[-1]), self.blocks, axis=0)

    def by_row(self, ranks):
        return jnp.take(ranks, self.ranks, axis=0).reshape(-1, ranks.shape[-1])


def per_device(
    vision_in,
    vis_gain,
    first_weight,
    second_weight,
    layer_scale,
    proj_gain,
    proj_weight,
    text_embed,
    dest_row,
    cotangent,
):
    moves = Direct()
    groups = lax.axis_size("grp")
    size = lax.axis_size("tp")
    grp_rank = lax.axis_index("grp")
    seq_len, width = text_embed.shape
    merged_total = dest_row.shape[0] // groups
    image_rows = merged_total // images
    own_rows, vis_width = vision_in.shape
    merged_width = proj_gain.shape[0]
    fold = merged_width // vis_width
    rows = own_rows // chunks
    merged_rows = rows // fold

    x, hat, inv, normed = [], [], [], []
    for c in range(chunks):
        x.append(vision_in[c * rows : (c + 1) * rows].astype(jnp.float32))
        scaled, own_hat, own_inv = layer_norm(x[c], vis_gain, vis_eps)
        normed.append(scaled.astype(jnp.bfloat16))
        hat.append(own_hat)
        inv.append(own_inv)
    tied = lax.optimization_barrier
    rail_b = moves.spread(normed[1])
    normed[0], rail_b = tied((normed[0], rail_b))
    rail_a = moves.spread(normed[0])
    patches_b = moves.gathered(rail_b)

    starts = dest_row.reshape(groups, images, image_rows)[:, :, 0]
    start_pos = starts % seq_len
    shift = starts[0] // seq_len
    matches = (shift[None, :] == jnp.arange(groups)[:, None]).astype(jnp.int32)
    image_of = jnp.sum(matches * jnp.arange(images), 1)
    used = jnp.sum(matches, 1) > 0
    source = (grp_rank - jnp.arange(groups)) % groups
    from_group = (source[:, None] == jnp.arange(groups)).astype(jnp.int32)
    spot = jnp.sum(matches[:, None, :] * from_group[:, :, None] * start_pos[None], (1, 2))

    picked = []
    for s in range(groups):
        block = lax.dynamic_slice_in_dim(cotangent, spot[s], image_rows, 0)
        if s:
            block = lax.ppermute(block, "grp", [(g, (g - s) % groups) for g in range(groups)])
        picked.append(block)
    returned = jnp.take(jnp.stack(picked), shift, axis=0).reshape(size, -1, width)
    grad_proj = [
        moves.by_row(returned[:, c * merged_rows : (c + 1) * merged_rows]) for c in range(chunks)
    ]

    def merge(c, summed):
        outputs = (x[c] + layer_scale * summed).astype(jnp.bfloat16)
        merged = outputs.reshape(merged_rows, merged_width).astype(jnp.float32)
        scaled, own_hat, own_inv = layer_norm(merged, proj_gain, proj_eps)
        return scaled.astype(jnp.bfloat16), own_hat, own_inv

    def unmerge(back_sum, own_hat, own_inv):
        merged_grad = norm_back(back_sum, proj_gain, own_hat, own_inv).astype(jnp.bfloat16)
        own_grad = merged_grad.reshape(rows, vis_width).astype(jnp.float32)
        return own_grad, (own_grad * layer_scale).astype(jnp.bfloat16)

    early, late = first_weight.T, second_weight
    near_b, far_b, slope_b = vision_pass(forward_kernel, patches_b, early, late)
    near_b, far_b, rail_a = tied((near_b, far_b, rail_a))
    patches_a = moves.gathered(rail_a)
    terms_b = moves.send(near_b, far_b)
    near_a, far_a, slope_a = vision_pass(forward_kernel, patches_a, early, late)
    near_a, far_a, terms_b = tied((near_a, far_a, terms_b))
    terms_a = moves.send(near_a, far_a)
    mixed_b, *stats_b = merge(1, moves.summed(terms_b))
    rail_b = moves.spread(mixed_b)
    rail_b, terms_a = tied((rail_b, terms_a))
    mixed_a, *stats_a = merge(0, moves.summed(terms_a))
    rail_a = moves.spread(mixed_a)
    merged_b = moves.gathered(rail_b)
    projected_b, near_b, far_b = project(merged_b, proj_weight, grad_proj[1])
    near_b, far_b, rail_a = tied((near_b, far_b, rail_a))
    merged_a = moves.gathered(rail_a)
    terms_b = moves.send(near_b, far_b)
    projected_a, near_a, far_a = project(merged_a, proj_weight, grad_proj[0])
    near_a, far_a, terms_b = tied((near_a, far_a, terms_b))
    terms_a = moves.send(near_a, far_a)

    projected = jnp.concatenate(
        [moves.by_rank(projected_a, size), moves.by_rank(projected_b, size)], 1
    ).reshape(images, image_rows, width)
    seq_embed = text_embed
    for s in range(groups):
        block = lax.dynamic_index_in_dim(projected, image_of[s], 0, False)
        if s:
            block = lax.ppermute(block, "grp", [(g, (g + s) % groups) for g in range(groups)])
        if groups > images:
            there = lax.dynamic_slice_in_dim(seq_embed, spot[s], image_rows, 0)
            block = jnp.where(used[s], block, there)
        seq_embed = lax.dynamic_update_slice_in_dim(seq_embed, block, spot[s], 0)

    own_b, scaled_b = unmerge(moves.summed(terms_b), *stats_b)
    rail_b = moves.spread(scaled_b)
    rail_b, terms_a = tied((rail_b, terms_a))
    own_a, scaled_a = unmerge(moves.summed(terms_a), *stats_a)
    rail_a = moves.spread(scaled_a)
    grad_out_b = moves.gathered(rail_b)
    near_b, far_b = vision_pass(backward_kernel, grad_out_b, late, early, slope_b)
    near_b, far_b, rail_a = tied((near_b, far_b, rail_a))
    grad_out_a = moves.gathered(rail_a)
    terms_b = moves.send(near_b, far_b)
    near_a, far_a = vision_pass(backward_kernel, grad_out_a, late, early, slope_a)
    near_a, far_a, terms_b, seq_embed = tied((near_a, far_a, terms_b, seq_embed))
    normed_a = moves.summed(moves.send(near_a, far_a))
    normed_b = moves.summed(terms_b)
    grads = [
        own_a + norm_back(normed_a, vis_gain, hat[0], inv[0]),
        own_b + norm_back(normed_b, vis_gain, hat[1], inv[1]),
    ]
    grad_vision = jnp.concatenate(grads, 0).astype(jnp.bfloat16)
    return (seq_embed, grad_vision)


def solution(mesh):
    placed = (
        P(("grp", "tp"), None),
        P(),
        P(None, "tp"),
        P("tp", None),
        P(),
        P(),
        P(None, "tp"),
        P("grp", "tp"),
        P(),
        P("grp", "tp"),
    )
    return jax.shard_map(
        per_device,
        mesh=mesh,
        in_specs=placed,
        out_specs=(P("grp", "tp"), P(("grp", "tp"), None)),
        check_vma=False,
    )
```

```python
import functools

import jax
import jax.numpy as jnp
from jax import lax
from jax.experimental import pallas as pl
from jax.experimental.pallas import tpu as pltpu
from jax.sharding import PartitionSpec as P

vis_eps = 1e-06
proj_eps = 1e-05
chunks = 2
images = 4
cores = 2


def layer_norm(values, scale_vec, epsilon):
    mean_val = jnp.mean(values, -1, keepdims=True)
    centred = values - mean_val
    inv_std = lax.rsqrt(jnp.mean(centred * centred, -1, keepdims=True) + epsilon)
    normed = centred * inv_std
    return (normed * scale_vec, normed, inv_std)


def norm_back(upstream, scale_vec, normed, inv_std):
    scaled = upstream * scale_vec
    return inv_std * (
        scaled
        - jnp.mean(scaled, -1, keepdims=True)
        - normed * jnp.mean(scaled * normed, -1, keepdims=True)
    )


def times_transposed(left, right):
    return lax.dot_general(
        left, right, (((1,), (1,)), ((), ())), preferred_element_type=jnp.float32
    )


def tile_of(length, most):
    return max(t for t in range(128, most + 1, 128) if length % t == 0)


def laid(pieces):
    if len(pieces) == 1:
        return pieces[0][...]
    if pieces[0].shape[0] % 16 == 0:
        return jnp.concatenate([p[...] for p in pieces], 0)
    return jnp.concatenate([p[...].astype(jnp.float32) for p in pieces], 0).astype(jnp.bfloat16)


def each_rows(total, body):
    step = 16 if total % 16 == 0 else total

    def run(i, _):
        body(pl.ds(pl.multiple_of(i * step, step), step))
        return 0

    lax.fori_loop(0, total // step, run, 0)


def fetch(source, held, sems):
    count, rows = held.shape[:2]
    for j in range(count):
        pltpu.make_async_copy(source.at[pl.ds(j * rows, rows)], held.at[j], sems.at[j]).start()


def arrive(source, held, sems, j):
    rows = held.shape[1]
    pltpu.make_async_copy(source.at[pl.ds(0, rows)], held.at[j], sems.at[j]).wait()


def vision_kernel(count, ahead, *refs):
    pieces = refs[:count]
    if ahead:
        early, late, near, far, slope = refs[count : count + 5]
    else:
        early, late, slope, near, far = refs[count : count + 5]
    first, second, rows, total, pre, hidden, first_sems, second_sems = refs[count + 5 :]
    fetch(early, first, first_sems)
    fetch(late, second, second_sems)
    rows[...] = laid(pieces)
    total[...] = jnp.zeros_like(total)
    tile = tile_of(rows.shape[1], 640)

    def block(j, _):
        arrive(early, first, first_sems, j)
        pre[...] = times_transposed(rows[...], first[j])

        def act(sel):
            u = pre[sel, :]
            if ahead:
                cumul = 0.5 * (1.0 + lax.erf(u * 0.7071067811865476))
                dense = jnp.exp(-0.5 * u * u) * 0.3989422804014327
                hidden[sel, :] = (u * cumul).astype(jnp.bfloat16)
                slope[j, sel, :] = cumul + u * dense
            else:
                hidden[sel, :] = (u * slope[j, sel, :]).astype(jnp.bfloat16)

        each_rows(pre.shape[0], act)
        arrive(late, second, second_sems, j)

        def columns(k, _):
            sel = pl.ds(pl.multiple_of(k * tile, 128), tile)
            total[:, sel] += jnp.dot(
                hidden[...], second[j, :, sel], preferred_element_type=jnp.float32
            )
            return 0

        lax.fori_loop(0, rows.shape[1] // tile, columns, 0)
        return 0

    lax.fori_loop(0, first.shape[0], block, 0)
    half = near.shape[0]
    near[...] = total[:half].astype(jnp.bfloat16)
    far[...] = total[half:].astype(jnp.bfloat16)


def project_kernel(count, *refs):
    pieces = refs[:count]
    weight, upstream, projected, near, far, held, rows, pre, delta, sems = refs[count:]
    fetch(weight, held, sems)
    rows[...] = laid(pieces)
    pre[...] = jnp.zeros_like(pre)
    chunk = held.shape[1]
    half = near.shape[0]

    def ahead(j, _):
        arrive(weight, held, sems, j)
        sel = pl.ds(pl.multiple_of(j * chunk, 128), chunk)
        pre[...] += jnp.dot(rows[:, sel], held[j], preferred_element_type=jnp.float32)
        return 0

    lax.fori_loop(0, held.shape[0], ahead, 0)

    def act(sel):
        u = pre[sel, :]
        cumul = 0.5 * (1.0 + lax.erf(u * 0.7071067811865476))
        dense = jnp.exp(-0.5 * u * u) * 0.3989422804014327
        projected[sel, :] = (u * cumul).astype(jnp.bfloat16)
        grad = upstream[sel, :].astype(jnp.float32)
        delta[sel, :] = (grad * (cumul + u * dense)).astype(jnp.bfloat16)

    each_rows(pre.shape[0], act)

    def behind(j, _):
        sel = pl.ds(pl.multiple_of(j * chunk, 128), chunk)
        back = times_transposed(delta[...], held[j]).astype(jnp.bfloat16)
        near[:, sel] = back[:half]
        far[:, sel] = back[half:]
        return 0

    lax.fori_loop(0, held.shape[0], behind, 0)


def settings():
    return pltpu.CompilerParams(vmem_limit_bytes=56 * 1024 * 1024)


def whole_blocks(count):
    return [pl.BlockSpec(memory_space=pltpu.VMEM)] * count


def vision_pass(pieces, early, late, slope=None):
    rows = sum(p.shape[0] for p in pieces)
    units, width = early.shape
    size = max(t for t in range(16, 401, 16) if units % t == 0)
    blocks = units // size
    given = [] if slope is None else [slope]
    slopes = [jax.ShapeDtypeStruct((blocks, rows, size), jnp.float32)] * (1 - len(given))
    return pl.pallas_call(
        functools.partial(vision_kernel, len(pieces), slope is None),
        in_specs=whole_blocks(len(pieces))
        + [pl.BlockSpec(memory_space=pl.ANY)] * 2
        + whole_blocks(len(given)),
        out_specs=whole_blocks(2 + len(slopes)),
        out_shape=[jax.ShapeDtypeStruct((rows // 2, width), jnp.bfloat16)] * 2 + slopes,
        scratch_shapes=[
            pltpu.VMEM((blocks, size, width), jnp.bfloat16),
            pltpu.VMEM((blocks, size, width), jnp.bfloat16),
            pltpu.VMEM((rows, width), jnp.bfloat16),
            pltpu.VMEM((rows, width), jnp.float32),
            pltpu.VMEM((rows, size), jnp.float32),
            pltpu.VMEM((rows, size), jnp.bfloat16),
            pltpu.SemaphoreType.DMA((blocks,)),
            pltpu.SemaphoreType.DMA((blocks,)),
        ],
        compiler_params=settings(),
        cost_estimate=pl.CostEstimate(
            flops=4 * rows * width * units,
            bytes_accessed=4 * width * units + 4 * rows * (width + units),
            transcendentals=2 * rows * units,
        ),
    )(*pieces, early, late, *given)


def project(pieces, weight, upstream):
    rows = sum(p.shape[0] for p in pieces)
    depth, units = weight.shape
    size = tile_of(depth, 1280)
    return pl.pallas_call(
        functools.partial(project_kernel, len(pieces)),
        in_specs=whole_blocks(len(pieces)) + [pl.BlockSpec(memory_space=pl.ANY)] + whole_blocks(1),
        out_specs=whole_blocks(3),
        out_shape=[jax.ShapeDtypeStruct((rows, units), jnp.bfloat16)]
        + [jax.ShapeDtypeStruct((rows // 2, depth), jnp.bfloat16)] * 2,
        scratch_shapes=[
            pltpu.VMEM((depth // size, size, units), jnp.bfloat16),
            pltpu.VMEM((rows, depth), jnp.bfloat16),
            pltpu.VMEM((rows, units), jnp.float32),
            pltpu.VMEM((rows, units), jnp.bfloat16),
            pltpu.SemaphoreType.DMA((depth // size,)),
        ],
        compiler_params=settings(),
        cost_estimate=pl.CostEstimate(
            flops=4 * rows * depth * units,
            bytes_accessed=2 * depth * units + 4 * rows * (depth + units),
            transcendentals=2 * rows * units,
        ),
    )(*pieces, weight, upstream)


class Direct:
    def __init__(self):
        self.size = lax.axis_size("tp")
        self.places = self.size // cores
        rank = lax.axis_index("tp")
        place, core = rank // cores, rank % cores
        back = (place - jnp.arange(self.places)) % self.places * cores
        self.ranks = jnp.concatenate([back + core, back + 1 - core])
        every = jnp.arange(self.size)
        far = (every + core) % cores * self.places
        self.blocks = far + (place - every // cores) % self.places
        self.pairs = [(a, a + 1 - 2 * (a % cores)) for a in range(self.size)]

    def shift(self, block, k):
        pairs = [(a, (a + k * cores) % self.size) for a in range(self.size)]
        return lax.ppermute(block, "tp", pairs)

    def spread(self, block):
        return [block] + [self.shift(block, k) for k in range(1, self.places)]

    def gathered(self, mine):
        other = [lax.ppermute(m, "tp", self.pairs) for m in mine]
        if mine[0].shape[0] % 8:
            return [jnp.concatenate(mine + other, 0)]
        return mine + other

    def send(self, near, far):
        rows = near.shape[0] // self.places
        got = lax.ppermute(far, "tp", self.pairs)
        both = near.astype(jnp.float32) + got.astype(jnp.float32)
        cut = [both[k * rows : (k + 1) * rows] for k in range(self.places)]
        return cut[:1] + [
            self.shift(cut[k].astype(jnp.bfloat16), -k) for k in range(1, self.places)
        ]

    def summed(self, terms):
        return sum([t.astype(jnp.float32) for t in terms[1:]], terms[0])

    def by_rank(self, rows, size):
        return jnp.take(rows.reshape(size, -1, rows.shape[-1]), self.blocks, axis=0)

    def by_row(self, ranks):
        return jnp.take(ranks, self.ranks, axis=0).reshape(-1, ranks.shape[-1])


def per_device(
    vision_in,
    vis_gain,
    first_weight,
    second_weight,
    layer_scale,
    proj_gain,
    proj_weight,
    text_embed,
    dest_row,
    cotangent,
):
    moves = Direct()
    groups = lax.axis_size("grp")
    size = lax.axis_size("tp")
    grp_rank = lax.axis_index("grp")
    seq_len, width = text_embed.shape
    merged_total = dest_row.shape[0] // groups
    image_rows = merged_total // images
    own_rows, vis_width = vision_in.shape
    merged_width = proj_gain.shape[0]
    fold = merged_width // vis_width
    rows = own_rows // chunks
    merged_rows = rows // fold

    x, hat, inv, normed = [], [], [], []
    for c in range(chunks):
        x.append(vision_in[c * rows : (c + 1) * rows].astype(jnp.float32))
        scaled, own_hat, own_inv = layer_norm(x[c], vis_gain, vis_eps)
        normed.append(scaled.astype(jnp.bfloat16))
        hat.append(own_hat)
        inv.append(own_inv)
    tied = lax.optimization_barrier
    rail_b = moves.spread(normed[1])
    normed[0], rail_b = tied((normed[0], rail_b))
    rail_a = moves.spread(normed[0])
    patches_b = moves.gathered(rail_b)

    starts = dest_row.reshape(groups, images, image_rows)[:, :, 0]
    start_pos = starts % seq_len
    shift = starts[0] // seq_len
    matches = (shift[None, :] == jnp.arange(groups)[:, None]).astype(jnp.int32)
    image_of = jnp.sum(matches * jnp.arange(images), 1)
    used = jnp.sum(matches, 1) > 0
    source = (grp_rank - jnp.arange(groups)) % groups
    from_group = (source[:, None] == jnp.arange(groups)).astype(jnp.int32)
    spot = jnp.sum(matches[:, None, :] * from_group[:, :, None] * start_pos[None], (1, 2))

    picked = []
    for s in range(groups):
        block = lax.dynamic_slice_in_dim(cotangent, spot[s], image_rows, 0)
        if s:
            block = lax.ppermute(block, "grp", [(g, (g - s) % groups) for g in range(groups)])
        picked.append(block)

    def grad_of(picked, c):
        returned = jnp.take(jnp.stack(picked), shift, axis=0).reshape(size, -1, width)
        return moves.by_row(returned[:, c * merged_rows : (c + 1) * merged_rows])

    def merge(c, summed):
        outputs = (x[c] + layer_scale * summed).astype(jnp.bfloat16)
        merged = outputs.reshape(merged_rows, merged_width).astype(jnp.float32)
        scaled, own_hat, own_inv = layer_norm(merged, proj_gain, proj_eps)
        return scaled.astype(jnp.bfloat16), own_hat, own_inv

    def unmerge(back_sum, own_hat, own_inv):
        merged_grad = norm_back(back_sum, proj_gain, own_hat, own_inv).astype(jnp.bfloat16)
        own_grad = merged_grad.reshape(rows, vis_width).astype(jnp.float32)
        return own_grad, (own_grad * layer_scale).astype(jnp.bfloat16)

    early, late = first_weight.T, second_weight
    near_b, far_b, slope_b = vision_pass(patches_b, early, late)
    near_b, far_b, rail_a = tied((near_b, far_b, rail_a))
    patches_a = moves.gathered(rail_a)
    terms_b = moves.send(near_b, far_b)
    near_a, far_a, slope_a = vision_pass(patches_a, early, late)
    near_a, far_a, terms_b, picked = tied((near_a, far_a, terms_b, picked))
    terms_a = moves.send(near_a, far_a)
    mixed_b, *stats_b = merge(1, moves.summed(terms_b))
    rail_b = moves.spread(mixed_b)
    rail_b, terms_a = tied((rail_b, terms_a))
    mixed_a, *stats_a = merge(0, moves.summed(terms_a))
    rail_a = moves.spread(mixed_a)
    merged_b = moves.gathered(rail_b)
    projected_b, near_b, far_b = project(merged_b, proj_weight, grad_of(picked, 1))
    near_b, far_b, rail_a = tied((near_b, far_b, rail_a))
    merged_a = moves.gathered(rail_a)
    terms_b = moves.send(near_b, far_b)
    projected_a, near_a, far_a = project(merged_a, proj_weight, grad_of(picked, 0))
    near_a, far_a, terms_b = tied((near_a, far_a, terms_b))
    terms_a = moves.send(near_a, far_a)

    projected = jnp.concatenate(
        [moves.by_rank(projected_a, size), moves.by_rank(projected_b, size)], 1
    ).reshape(images, image_rows, width)
    arrived = []
    for s in range(groups):
        block = lax.dynamic_index_in_dim(projected, image_of[s], 0, False)
        if s:
            block = lax.ppermute(block, "grp", [(g, (g + s) % groups) for g in range(groups)])
        arrived.append(block)

    def embed(text, arrived):
        for s in range(groups):
            block = arrived[s]
            if groups > images:
                there = lax.dynamic_slice_in_dim(text, spot[s], image_rows, 0)
                block = jnp.where(used[s], block, there)
            text = lax.dynamic_update_slice_in_dim(text, block, spot[s], 0)
        return text

    own_b, scaled_b = unmerge(moves.summed(terms_b), *stats_b)
    rail_b = moves.spread(scaled_b)
    rail_b, terms_a, arrived = tied((rail_b, terms_a, arrived))
    own_a, scaled_a = unmerge(moves.summed(terms_a), *stats_a)
    rail_a = moves.spread(scaled_a)
    grad_out_b = moves.gathered(rail_b)
    near_b, far_b = vision_pass(grad_out_b, late, early, slope_b)
    near_b, far_b, rail_a = tied((near_b, far_b, rail_a))
    grad_out_a = moves.gathered(rail_a)
    terms_b = moves.send(near_b, far_b)
    near_a, far_a = vision_pass(grad_out_a, late, early, slope_a)
    near_a, far_a, terms_b, text = tied((near_a, far_a, terms_b, text_embed))
    terms_a = moves.send(near_a, far_a)
    normed_b = moves.summed(terms_b)
    terms_a, seq_embed, normed_b = tied((terms_a, embed(text, arrived), normed_b))
    normed_a = moves.summed(terms_a)
    grads = [
        own_a + norm_back(normed_a, vis_gain, hat[0], inv[0]),
        own_b + norm_back(normed_b, vis_gain, hat[1], inv[1]),
    ]
    grad_vision = jnp.concatenate(grads, 0).astype(jnp.bfloat16)
    return (seq_embed, grad_vision)


def solution(mesh):
    placed = (
        P(("grp", "tp"), None),
        P(),
        P(None, "tp"),
        P("tp", None),
        P(),
        P(),
        P(None, "tp"),
        P("grp", "tp"),
        P(),
        P("grp", "tp"),
    )
    return jax.shard_map(
        per_device,
        mesh=mesh,
        in_specs=placed,
        out_specs=(P("grp", "tp"), P(("grp", "tp"), None)),
        check_vma=False,
    )
```

```python
import functools

import jax
import jax.numpy as jnp
from jax import lax
from jax.experimental import pallas as pl
from jax.experimental.pallas import tpu as pltpu
from jax.sharding import PartitionSpec as P

vis_eps = 1e-06
proj_eps = 1e-05
chunks = 2
images = 4
cores = 2


def layer_norm(values, scale_vec, epsilon):
    mean_val = jnp.mean(values, -1, keepdims=True)
    centred = values - mean_val
    inv_std = lax.rsqrt(jnp.mean(centred * centred, -1, keepdims=True) + epsilon)
    normed = centred * inv_std
    return (normed * scale_vec, normed, inv_std)


def norm_back(upstream, scale_vec, normed, inv_std):
    scaled = upstream * scale_vec
    return inv_std * (
        scaled
        - jnp.mean(scaled, -1, keepdims=True)
        - normed * jnp.mean(scaled * normed, -1, keepdims=True)
    )


def times_transposed(left, right):
    return lax.dot_general(
        left, right, (((1,), (1,)), ((), ())), preferred_element_type=jnp.float32
    )


def tile_of(length, most):
    return max(t for t in range(128, most + 1, 128) if length % t == 0)


def laid(pieces):
    if len(pieces) == 1:
        return pieces[0][...]
    if pieces[0].shape[0] % 16 == 0:
        return jnp.concatenate([p[...] for p in pieces], 0)
    return jnp.concatenate([p[...].astype(jnp.float32) for p in pieces], 0).astype(jnp.bfloat16)


def each_rows(total, body):
    step = 16 if total % 16 == 0 else total

    def run(i, _):
        body(pl.ds(pl.multiple_of(i * step, step), step))
        return 0

    lax.fori_loop(0, total // step, run, 0)


def fetch(source, held, sems):
    count, rows = held.shape[:2]
    for j in range(count):
        copy = pltpu.make_async_copy(source.at[pl.ds(j * rows, rows)], held.at[j], sems.at[j])
        copy.start(priority=j % 2)


def arrive(source, held, sems, j):
    rows = held.shape[1]
    pltpu.make_async_copy(source.at[pl.ds(0, rows)], held.at[j], sems.at[j]).wait()


def vision_kernel(count, ahead, *refs):
    pieces = refs[:count]
    if ahead:
        early, late, near, far, slope = refs[count : count + 5]
    else:
        early, late, slope, near, far = refs[count : count + 5]
    first, second, rows, total, pre, hidden, first_sems, second_sems = refs[count + 5 :]
    fetch(early, first, first_sems)
    fetch(late, second, second_sems)
    rows[...] = laid(pieces)
    total[...] = jnp.zeros_like(total)
    tile = tile_of(rows.shape[1], 640)

    def block(j, _):
        arrive(early, first, first_sems, j)
        pre[...] = times_transposed(rows[...], first[j])

        def act(sel):
            u = pre[sel, :]
            if ahead:
                cumul = 0.5 * (1.0 + lax.erf(u * 0.7071067811865476))
                dense = jnp.exp(-0.5 * u * u) * 0.3989422804014327
                hidden[sel, :] = (u * cumul).astype(jnp.bfloat16)
                slope[j, sel, :] = cumul + u * dense
            else:
                hidden[sel, :] = (u * slope[j, sel, :]).astype(jnp.bfloat16)

        each_rows(pre.shape[0], act)
        arrive(late, second, second_sems, j)

        def columns(k, _):
            sel = pl.ds(pl.multiple_of(k * tile, 128), tile)
            total[:, sel] += jnp.dot(
                hidden[...], second[j, :, sel], preferred_element_type=jnp.float32
            )
            return 0

        lax.fori_loop(0, rows.shape[1] // tile, columns, 0)
        return 0

    lax.fori_loop(0, first.shape[0], block, 0)
    half = near.shape[0]
    near[...] = total[:half].astype(jnp.bfloat16)
    far[...] = total[half:].astype(jnp.bfloat16)


def project_kernel(count, *refs):
    pieces = refs[:count]
    weight, upstream, projected, near, far, held, rows, pre, delta, sems = refs[count:]
    fetch(weight, held, sems)
    rows[...] = laid(pieces)
    pre[...] = jnp.zeros_like(pre)
    chunk = held.shape[1]
    half = near.shape[0]

    def ahead(j, _):
        arrive(weight, held, sems, j)
        sel = pl.ds(pl.multiple_of(j * chunk, 128), chunk)
        pre[...] += jnp.dot(rows[:, sel], held[j], preferred_element_type=jnp.float32)
        return 0

    lax.fori_loop(0, held.shape[0], ahead, 0)

    def act(sel):
        u = pre[sel, :]
        cumul = 0.5 * (1.0 + lax.erf(u * 0.7071067811865476))
        dense = jnp.exp(-0.5 * u * u) * 0.3989422804014327
        projected[sel, :] = (u * cumul).astype(jnp.bfloat16)
        grad = upstream[sel, :].astype(jnp.float32)
        delta[sel, :] = (grad * (cumul + u * dense)).astype(jnp.bfloat16)

    each_rows(pre.shape[0], act)

    def behind(j, _):
        sel = pl.ds(pl.multiple_of(j * chunk, 128), chunk)
        back = times_transposed(delta[...], held[j]).astype(jnp.bfloat16)
        near[:, sel] = back[:half]
        far[:, sel] = back[half:]
        return 0

    lax.fori_loop(0, held.shape[0], behind, 0)


def settings():
    return pltpu.CompilerParams(vmem_limit_bytes=56 * 1024 * 1024)


def whole_blocks(count):
    return [pl.BlockSpec(memory_space=pltpu.VMEM)] * count


def vision_pass(pieces, early, late, slope=None):
    rows = sum(p.shape[0] for p in pieces)
    units, width = early.shape
    size = max(t for t in range(16, 401, 16) if units % t == 0)
    blocks = units // size
    given = [] if slope is None else [slope]
    slopes = [jax.ShapeDtypeStruct((blocks, rows, size), jnp.float32)] * (1 - len(given))
    return pl.pallas_call(
        functools.partial(vision_kernel, len(pieces), slope is None),
        in_specs=whole_blocks(len(pieces))
        + [pl.BlockSpec(memory_space=pl.ANY)] * 2
        + whole_blocks(len(given)),
        out_specs=whole_blocks(2 + len(slopes)),
        out_shape=[jax.ShapeDtypeStruct((rows // 2, width), jnp.bfloat16)] * 2 + slopes,
        scratch_shapes=[
            pltpu.VMEM((blocks, size, width), jnp.bfloat16),
            pltpu.VMEM((blocks, size, width), jnp.bfloat16),
            pltpu.VMEM((rows, width), jnp.bfloat16),
            pltpu.VMEM((rows, width), jnp.float32),
            pltpu.VMEM((rows, size), jnp.float32),
            pltpu.VMEM((rows, size), jnp.bfloat16),
            pltpu.SemaphoreType.DMA((blocks,)),
            pltpu.SemaphoreType.DMA((blocks,)),
        ],
        compiler_params=settings(),
        cost_estimate=pl.CostEstimate(
            flops=4 * rows * width * units,
            bytes_accessed=4 * width * units + 4 * rows * (width + units),
            transcendentals=2 * rows * units,
        ),
    )(*pieces, early, late, *given)


def project(pieces, weight, upstream):
    rows = sum(p.shape[0] for p in pieces)
    depth, units = weight.shape
    size = tile_of(depth, 1280)
    return pl.pallas_call(
        functools.partial(project_kernel, len(pieces)),
        in_specs=whole_blocks(len(pieces)) + [pl.BlockSpec(memory_space=pl.ANY)] + whole_blocks(1),
        out_specs=whole_blocks(3),
        out_shape=[jax.ShapeDtypeStruct((rows, units), jnp.bfloat16)]
        + [jax.ShapeDtypeStruct((rows // 2, depth), jnp.bfloat16)] * 2,
        scratch_shapes=[
            pltpu.VMEM((depth // size, size, units), jnp.bfloat16),
            pltpu.VMEM((rows, depth), jnp.bfloat16),
            pltpu.VMEM((rows, units), jnp.float32),
            pltpu.VMEM((rows, units), jnp.bfloat16),
            pltpu.SemaphoreType.DMA((depth // size,)),
        ],
        compiler_params=settings(),
        cost_estimate=pl.CostEstimate(
            flops=4 * rows * depth * units,
            bytes_accessed=2 * depth * units + 4 * rows * (depth + units),
            transcendentals=2 * rows * units,
        ),
    )(*pieces, weight, upstream)


class Direct:
    def __init__(self):
        self.size = lax.axis_size("tp")
        self.places = self.size // cores
        rank = lax.axis_index("tp")
        place, core = rank // cores, rank % cores
        back = (place - jnp.arange(self.places)) % self.places * cores
        self.ranks = jnp.concatenate([back + core, back + 1 - core])
        every = jnp.arange(self.size)
        far = (every + core) % cores * self.places
        self.blocks = far + (place - every // cores) % self.places
        self.pairs = [(a, a + 1 - 2 * (a % cores)) for a in range(self.size)]

    def shift(self, block, k):
        pairs = [(a, (a + k * cores) % self.size) for a in range(self.size)]
        return lax.ppermute(block, "tp", pairs)

    def spread(self, block):
        return [block] + [self.shift(block, k) for k in range(1, self.places)]

    def gathered(self, mine):
        other = [lax.ppermute(m, "tp", self.pairs) for m in mine]
        if mine[0].shape[0] % 8:
            return [jnp.concatenate(mine + other, 0)]
        return mine + other

    def send(self, near, far):
        rows = near.shape[0] // self.places
        got = lax.ppermute(far, "tp", self.pairs)
        both = near.astype(jnp.float32) + got.astype(jnp.float32)
        cut = [both[k * rows : (k + 1) * rows] for k in range(self.places)]
        return cut[:1] + [
            self.shift(cut[k].astype(jnp.bfloat16), -k) for k in range(1, self.places)
        ]

    def summed(self, terms):
        return sum([t.astype(jnp.float32) for t in terms[1:]], terms[0])

    def by_rank(self, rows, size):
        return jnp.take(rows.reshape(size, -1, rows.shape[-1]), self.blocks, axis=0, mode="clip")

    def by_row(self, ranks):
        return jnp.take(ranks, self.ranks, axis=0, mode="clip").reshape(-1, ranks.shape[-1])


def per_device(
    vision_in,
    vis_gain,
    first_weight,
    second_weight,
    layer_scale,
    proj_gain,
    proj_weight,
    text_embed,
    dest_row,
    cotangent,
):
    moves = Direct()
    groups = lax.axis_size("grp")
    size = lax.axis_size("tp")
    grp_rank = lax.axis_index("grp")
    seq_len, width = text_embed.shape
    merged_total = dest_row.shape[0] // groups
    image_rows = merged_total // images
    own_rows, vis_width = vision_in.shape
    merged_width = proj_gain.shape[0]
    fold = merged_width // vis_width
    rows = own_rows // chunks
    merged_rows = rows // fold

    x, hat, inv, normed = [], [], [], []
    for c in range(chunks):
        x.append(vision_in[c * rows : (c + 1) * rows].astype(jnp.float32))
        scaled, own_hat, own_inv = layer_norm(x[c], vis_gain, vis_eps)
        normed.append(scaled.astype(jnp.bfloat16))
        hat.append(own_hat)
        inv.append(own_inv)
    tied = lax.optimization_barrier
    rail_b = moves.spread(normed[1])

    starts = dest_row.reshape(groups, images, image_rows)[:, :, 0]
    start_pos = starts % seq_len
    shift = starts[0] // seq_len
    matches = (shift[None, :] == jnp.arange(groups)[:, None]).astype(jnp.int32)
    image_of = jnp.sum(matches * jnp.arange(images), 1)
    used = jnp.sum(matches, 1) > 0
    source = (grp_rank - jnp.arange(groups)) % groups
    from_group = (source[:, None] == jnp.arange(groups)).astype(jnp.int32)
    spot = jnp.sum(matches[:, None, :] * from_group[:, :, None] * start_pos[None], (1, 2))

    span = jnp.arange(image_rows)
    picked = jnp.take(cotangent, (spot[:, None] + span).reshape(-1), axis=0, mode="clip")
    picked = [picked[s * image_rows : (s + 1) * image_rows] for s in range(groups)]
    for s in range(1, groups):
        pairs = [(g, (g - s) % groups) for g in range(groups)]
        picked[s] = lax.ppermute(picked[s], "grp", pairs)

    normed[0], rail_b, picked = tied((normed[0], rail_b, picked))
    rail_a = moves.spread(normed[0])
    patches_b = moves.gathered(rail_b)

    def grad_of(picked, c):
        returned = jnp.take(jnp.stack(picked), shift, axis=0, mode="clip").reshape(size, -1, width)
        return moves.by_row(returned[:, c * merged_rows : (c + 1) * merged_rows])

    def merge(c, summed):
        outputs = (x[c] + layer_scale * summed).astype(jnp.bfloat16)
        merged = outputs.reshape(merged_rows, merged_width).astype(jnp.float32)
        scaled, own_hat, own_inv = layer_norm(merged, proj_gain, proj_eps)
        return scaled.astype(jnp.bfloat16), own_hat, own_inv

    def unmerge(back_sum, own_hat, own_inv):
        merged_grad = norm_back(back_sum, proj_gain, own_hat, own_inv).astype(jnp.bfloat16)
        own_grad = merged_grad.reshape(rows, vis_width).astype(jnp.float32)
        return own_grad, (own_grad * layer_scale).astype(jnp.bfloat16)

    early, late = first_weight.T, second_weight
    near_b, far_b, slope_b = vision_pass(patches_b, early, late)
    near_b, far_b, rail_a = tied((near_b, far_b, rail_a))
    patches_a = moves.gathered(rail_a)
    terms_b = moves.send(near_b, far_b)
    near_a, far_a, slope_a = vision_pass(patches_a, early, late)
    near_a, far_a, terms_b, picked = tied((near_a, far_a, terms_b, picked))
    terms_a = moves.send(near_a, far_a)
    mixed_b, *stats_b = merge(1, moves.summed(terms_b))
    rail_b = moves.spread(mixed_b)
    rail_b, terms_a = tied((rail_b, terms_a))
    mixed_a, *stats_a = merge(0, moves.summed(terms_a))
    rail_a = moves.spread(mixed_a)
    merged_b = moves.gathered(rail_b)
    projected_b, near_b, far_b = project(merged_b, proj_weight, grad_of(picked, 1))
    near_b, far_b, rail_a = tied((near_b, far_b, rail_a))
    merged_a = moves.gathered(rail_a)
    terms_b = moves.send(near_b, far_b)
    projected_a, near_a, far_a = project(merged_a, proj_weight, grad_of(picked, 0))
    near_a, far_a, terms_b, projected_a, projected_b = tied(
        (near_a, far_a, terms_b, projected_a, projected_b)
    )
    terms_a = moves.send(near_a, far_a)

    projected = jnp.concatenate(
        [moves.by_rank(projected_a, size), moves.by_rank(projected_b, size)], 1
    ).reshape(images, image_rows, width)
    chosen = jnp.take(projected, image_of, axis=0, mode="clip")
    arrived = [chosen[s] for s in range(groups)]
    for s in range(1, groups):
        pairs = [(g, (g + s) % groups) for g in range(groups)]
        arrived[s] = lax.ppermute(arrived[s], "grp", pairs)

    def embed(text, arrived):
        goes_to = jnp.where(used[:, None], spot[:, None] + span, seq_len).reshape(-1)
        picks = jnp.arange(seq_len)[:, None] == goes_to[None, :]
        placed = jnp.dot(
            picks.astype(jnp.bfloat16),
            jnp.concatenate(arrived, 0),
            preferred_element_type=jnp.float32,
        ).astype(jnp.bfloat16)
        return jnp.where(jnp.any(picks, 1, keepdims=True), placed, text)

    own_b, scaled_b = unmerge(moves.summed(terms_b), *stats_b)
    rail_b = moves.spread(scaled_b)
    rail_b, terms_a, arrived = tied((rail_b, terms_a, arrived))
    own_a, scaled_a = unmerge(moves.summed(terms_a), *stats_a)
    rail_a = moves.spread(scaled_a)
    grad_out_b = moves.gathered(rail_b)
    near_b, far_b = vision_pass(grad_out_b, late, early, slope_b)
    near_b, far_b, rail_a = tied((near_b, far_b, rail_a))
    grad_out_a = moves.gathered(rail_a)
    terms_b = moves.send(near_b, far_b)
    near_a, far_a = vision_pass(grad_out_a, late, early, slope_a)
    near_a, far_a, terms_b, arrived = tied((near_a, far_a, terms_b, arrived))
    terms_a = moves.send(near_a, far_a)
    normed_b = moves.summed(terms_b)
    terms_a, seq_embed, normed_b = tied((terms_a, embed(text_embed, arrived), normed_b))
    normed_a = moves.summed(terms_a)
    grads = [
        own_a + norm_back(normed_a, vis_gain, hat[0], inv[0]),
        own_b + norm_back(normed_b, vis_gain, hat[1], inv[1]),
    ]
    grad_vision = jnp.concatenate(grads, 0).astype(jnp.bfloat16)
    return (seq_embed, grad_vision)


def solution(mesh):
    placed = (
        P(("grp", "tp"), None),
        P(),
        P(None, "tp"),
        P("tp", None),
        P(),
        P(),
        P(None, "tp"),
        P("grp", "tp"),
        P(),
        P("grp", "tp"),
    )
    return jax.shard_map(
        per_device,
        mesh=mesh,
        in_specs=placed,
        out_specs=(P("grp", "tp"), P(("grp", "tp"), None)),
        check_vma=False,
    )
```

```python
import functools

import jax
import jax.numpy as jnp
from jax import lax
from jax.experimental import pallas as pl
from jax.experimental.pallas import tpu as pltpu
from jax.sharding import PartitionSpec as P

vis_eps = 1e-06
proj_eps = 1e-05
chunks = 2
images = 4
cores = 2


def layer_norm(values, scale_vec, epsilon):
    mean_val = jnp.mean(values, -1, keepdims=True)
    centred = values - mean_val
    inv_std = lax.rsqrt(jnp.mean(centred * centred, -1, keepdims=True) + epsilon)
    normed = centred * inv_std
    return (normed * scale_vec, normed, inv_std)


def norm_back(upstream, scale_vec, normed, inv_std):
    scaled = upstream * scale_vec
    return inv_std * (
        scaled
        - jnp.mean(scaled, -1, keepdims=True)
        - normed * jnp.mean(scaled * normed, -1, keepdims=True)
    )


def times_transposed(left, right):
    return lax.dot_general(
        left, right, (((1,), (1,)), ((), ())), preferred_element_type=jnp.float32
    )


def tile_of(length, most):
    return max(t for t in range(128, most + 1, 128) if length % t == 0)


def laid(pieces):
    if len(pieces) == 1:
        return pieces[0][...]
    if pieces[0].shape[0] % 16 == 0:
        return jnp.concatenate([p[...] for p in pieces], 0)
    return jnp.concatenate([p[...].astype(jnp.float32) for p in pieces], 0).astype(jnp.bfloat16)


def each_rows(total, body):
    step = 16 if total % 16 == 0 else total

    def run(i, _):
        body(pl.ds(pl.multiple_of(i * step, step), step))
        return 0

    lax.fori_loop(0, total // step, run, 0)


def fetch(source, held, sems, j):
    count, rows = held.shape[:2]

    @pl.when(j < count)
    def _():
        start = pl.multiple_of(j * rows, 16)
        pltpu.make_async_copy(source.at[pl.ds(start, rows)], held.at[j], sems.at[j]).start()


def arrive(source, held, sems, j):
    rows = held.shape[1]
    pltpu.make_async_copy(source.at[pl.ds(0, rows)], held.at[j], sems.at[j]).wait()


def vision_kernel(count, ahead, *refs):
    pieces = refs[:count]
    if ahead:
        early, late, near, far, slope = refs[count : count + 5]
    else:
        early, late, slope, near, far = refs[count : count + 5]
    first, second, rows, total, pre, hidden, first_sems, second_sems = refs[count + 5 :]
    fetch(early, first, first_sems, 0)
    fetch(late, second, second_sems, 0)
    rows[...] = laid(pieces)
    total[...] = jnp.zeros_like(total)
    tile = tile_of(rows.shape[1], 640)

    def block(j, _):
        arrive(early, first, first_sems, j)
        fetch(early, first, first_sems, j + 1)
        pre[...] = times_transposed(rows[...], first[j])

        def act(sel):
            u = pre[sel, :]
            if ahead:
                cumul = 0.5 * (1.0 + lax.erf(u * 0.7071067811865476))
                dense = jnp.exp(-0.5 * u * u) * 0.3989422804014327
                hidden[sel, :] = (u * cumul).astype(jnp.bfloat16)
                slope[j, sel, :] = cumul + u * dense
            else:
                hidden[sel, :] = (u * slope[j, sel, :]).astype(jnp.bfloat16)

        each_rows(pre.shape[0], act)
        arrive(late, second, second_sems, j)
        fetch(late, second, second_sems, j + 1)

        def columns(k, _):
            sel = pl.ds(pl.multiple_of(k * tile, 128), tile)
            total[:, sel] += jnp.dot(
                hidden[...], second[j, :, sel], preferred_element_type=jnp.float32
            )
            return 0

        lax.fori_loop(0, rows.shape[1] // tile, columns, 0)
        return 0

    lax.fori_loop(0, first.shape[0], block, 0)
    half = near.shape[0]
    near[...] = total[:half].astype(jnp.bfloat16)
    far[...] = total[half:].astype(jnp.bfloat16)


def project_kernel(count, *refs):
    pieces = refs[:count]
    weight, upstream, projected, near, far, held, rows, pre, delta, sems = refs[count:]
    for j in range(3):
        fetch(weight, held, sems, j)
    rows[...] = laid(pieces)
    pre[...] = jnp.zeros_like(pre)
    chunk = held.shape[1]
    half = near.shape[0]

    def ahead(j, _):
        arrive(weight, held, sems, j)
        fetch(weight, held, sems, j + 3)
        sel = pl.ds(pl.multiple_of(j * chunk, 128), chunk)
        pre[...] += jnp.dot(rows[:, sel], held[j], preferred_element_type=jnp.float32)
        return 0

    lax.fori_loop(0, held.shape[0], ahead, 0)

    def act(sel):
        u = pre[sel, :]
        cumul = 0.5 * (1.0 + lax.erf(u * 0.7071067811865476))
        dense = jnp.exp(-0.5 * u * u) * 0.3989422804014327
        projected[sel, :] = (u * cumul).astype(jnp.bfloat16)
        grad = upstream[sel, :].astype(jnp.float32)
        delta[sel, :] = (grad * (cumul + u * dense)).astype(jnp.bfloat16)

    each_rows(pre.shape[0], act)

    def behind(j, _):
        sel = pl.ds(pl.multiple_of(j * chunk, 128), chunk)
        back = times_transposed(delta[...], held[j]).astype(jnp.bfloat16)
        near[:, sel] = back[:half]
        far[:, sel] = back[half:]
        return 0

    lax.fori_loop(0, held.shape[0], behind, 0)


def settings():
    return pltpu.CompilerParams(vmem_limit_bytes=56 * 1024 * 1024)


def whole_blocks(count):
    return [pl.BlockSpec(memory_space=pltpu.VMEM)] * count


def vision_pass(pieces, early, late, slope=None):
    rows = sum(p.shape[0] for p in pieces)
    units, width = early.shape
    size = max(t for t in range(16, 401, 16) if units % t == 0)
    blocks = units // size
    given = [] if slope is None else [slope]
    slopes = [jax.ShapeDtypeStruct((blocks, rows, size), jnp.float32)] * (1 - len(given))
    return pl.pallas_call(
        functools.partial(vision_kernel, len(pieces), slope is None),
        in_specs=whole_blocks(len(pieces))
        + [pl.BlockSpec(memory_space=pl.ANY)] * 2
        + whole_blocks(len(given)),
        out_specs=whole_blocks(2 + len(slopes)),
        out_shape=[jax.ShapeDtypeStruct((rows // 2, width), jnp.bfloat16)] * 2 + slopes,
        scratch_shapes=[
            pltpu.VMEM((blocks, size, width), jnp.bfloat16),
            pltpu.VMEM((blocks, size, width), jnp.bfloat16),
            pltpu.VMEM((rows, width), jnp.bfloat16),
            pltpu.VMEM((rows, width), jnp.float32),
            pltpu.VMEM((rows, size), jnp.float32),
            pltpu.VMEM((rows, size), jnp.bfloat16),
            pltpu.SemaphoreType.DMA((blocks,)),
            pltpu.SemaphoreType.DMA((blocks,)),
        ],
        compiler_params=settings(),
        cost_estimate=pl.CostEstimate(
            flops=4 * rows * width * units,
            bytes_accessed=4 * width * units + 4 * rows * (width + units),
            transcendentals=2 * rows * units,
        ),
    )(*pieces, early, late, *given)


def project(pieces, weight, upstream):
    rows = sum(p.shape[0] for p in pieces)
    depth, units = weight.shape
    size = tile_of(depth, 1280)
    return pl.pallas_call(
        functools.partial(project_kernel, len(pieces)),
        in_specs=whole_blocks(len(pieces)) + [pl.BlockSpec(memory_space=pl.ANY)] + whole_blocks(1),
        out_specs=whole_blocks(3),
        out_shape=[jax.ShapeDtypeStruct((rows, units), jnp.bfloat16)]
        + [jax.ShapeDtypeStruct((rows // 2, depth), jnp.bfloat16)] * 2,
        scratch_shapes=[
            pltpu.VMEM((depth // size, size, units), jnp.bfloat16),
            pltpu.VMEM((rows, depth), jnp.bfloat16),
            pltpu.VMEM((rows, units), jnp.float32),
            pltpu.VMEM((rows, units), jnp.bfloat16),
            pltpu.SemaphoreType.DMA((depth // size,)),
        ],
        compiler_params=settings(),
        cost_estimate=pl.CostEstimate(
            flops=4 * rows * depth * units,
            bytes_accessed=2 * depth * units + 4 * rows * (depth + units),
            transcendentals=2 * rows * units,
        ),
    )(*pieces, weight, upstream)


class Direct:
    def __init__(self):
        self.size = lax.axis_size("tp")
        self.places = self.size // cores
        rank = lax.axis_index("tp")
        place, core = rank // cores, rank % cores
        partner = (place ^ jnp.arange(self.places)) * cores
        self.ranks = jnp.concatenate([partner + core, partner + 1 - core])
        every = jnp.arange(self.size)
        self.blocks = (every + core) % cores * self.places + (every // cores ^ place)
        self.pairs = [(a, a + 1 - 2 * (a % cores)) for a in range(self.size)]

    def shift(self, block, k):
        pairs = [(a, (a // cores ^ k) * cores + a % cores) for a in range(self.size)]
        return lax.ppermute(block, "tp", pairs)

    def spread(self, block):
        return [block] + [self.shift(block, k) for k in range(1, self.places)]

    def gathered(self, mine):
        other = [lax.ppermute(m, "tp", self.pairs) for m in mine]
        if mine[0].shape[0] % 8:
            return [jnp.concatenate(mine + other, 0)]
        return mine + other

    def send(self, near, far):
        rows = near.shape[0] // self.places
        got = lax.ppermute(far, "tp", self.pairs)
        both = near.astype(jnp.float32) + got.astype(jnp.float32)
        cut = [both[k * rows : (k + 1) * rows] for k in range(self.places)]
        return cut[:1] + [
            self.shift(cut[k].astype(jnp.bfloat16), k) for k in range(1, self.places)
        ]

    def summed(self, terms):
        return sum([t.astype(jnp.float32) for t in terms[1:]], terms[0])

    def by_rank(self, rows, size):
        return jnp.take(rows.reshape(size, -1, rows.shape[-1]), self.blocks, axis=0, mode="clip")

    def by_row(self, ranks):
        return jnp.take(ranks, self.ranks, axis=0, mode="clip").reshape(-1, ranks.shape[-1])


def per_device(
    vision_in,
    vis_gain,
    first_weight,
    second_weight,
    layer_scale,
    proj_gain,
    proj_weight,
    text_embed,
    dest_row,
    cotangent,
):
    moves = Direct()
    groups = lax.axis_size("grp")
    size = lax.axis_size("tp")
    grp_rank = lax.axis_index("grp")
    seq_len, width = text_embed.shape
    merged_total = dest_row.shape[0] // groups
    image_rows = merged_total // images
    own_rows, vis_width = vision_in.shape
    merged_width = proj_gain.shape[0]
    fold = merged_width // vis_width
    rows = own_rows // chunks
    merged_rows = rows // fold

    x, hat, inv, normed = [], [], [], []
    for c in range(chunks):
        x.append(vision_in[c * rows : (c + 1) * rows].astype(jnp.float32))
        scaled, own_hat, own_inv = layer_norm(x[c], vis_gain, vis_eps)
        normed.append(scaled.astype(jnp.bfloat16))
        hat.append(own_hat)
        inv.append(own_inv)
    tied = lax.optimization_barrier
    rail_b = moves.spread(normed[1])

    starts = dest_row.reshape(groups, images, image_rows)[:, :, 0]
    start_pos = starts % seq_len
    shift = starts[0] // seq_len
    matches = (shift[None, :] == jnp.arange(groups)[:, None]).astype(jnp.int32)
    image_of = jnp.sum(matches * jnp.arange(images), 1)
    used = jnp.sum(matches, 1) > 0
    source = (grp_rank - jnp.arange(groups)) % groups
    from_group = (source[:, None] == jnp.arange(groups)).astype(jnp.int32)
    spot = jnp.sum(matches[:, None, :] * from_group[:, :, None] * start_pos[None], (1, 2))

    span = jnp.arange(image_rows)
    picked = jnp.take(cotangent, (spot[:, None] + span).reshape(-1), axis=0, mode="clip")
    picked = [picked[s * image_rows : (s + 1) * image_rows] for s in range(groups)]
    for s in range(1, groups):
        pairs = [(g, (g - s) % groups) for g in range(groups)]
        picked[s] = lax.ppermute(picked[s], "grp", pairs)

    normed[0], rail_b, picked = tied((normed[0], rail_b, picked))
    rail_a = moves.spread(normed[0])
    patches_b = moves.gathered(rail_b)

    def grad_of(picked, c):
        returned = jnp.take(jnp.stack(picked), shift, axis=0, mode="clip").reshape(size, -1, width)
        return moves.by_row(returned[:, c * merged_rows : (c + 1) * merged_rows])

    def merge(c, summed):
        outputs = (x[c] + layer_scale * summed).astype(jnp.bfloat16)
        merged = outputs.reshape(merged_rows, merged_width).astype(jnp.float32)
        scaled, own_hat, own_inv = layer_norm(merged, proj_gain, proj_eps)
        return scaled.astype(jnp.bfloat16), own_hat, own_inv

    def unmerge(back_sum, own_hat, own_inv):
        merged_grad = norm_back(back_sum, proj_gain, own_hat, own_inv).astype(jnp.bfloat16)
        own_grad = merged_grad.reshape(rows, vis_width).astype(jnp.float32)
        return own_grad, (own_grad * layer_scale).astype(jnp.bfloat16)

    early, late = first_weight.T, second_weight
    near_b, far_b, slope_b = vision_pass(patches_b, early, late)
    near_b, far_b, rail_a = tied((near_b, far_b, rail_a))
    patches_a = moves.gathered(rail_a)
    terms_b = moves.send(near_b, far_b)
    near_a, far_a, slope_a = vision_pass(patches_a, early, late)
    near_a, far_a, terms_b, picked = tied((near_a, far_a, terms_b, picked))
    terms_a = moves.send(near_a, far_a)
    mixed_b, *stats_b = merge(1, moves.summed(terms_b))
    rail_b = moves.spread(mixed_b)
    rail_b, terms_a = tied((rail_b, terms_a))
    mixed_a, *stats_a = merge(0, moves.summed(terms_a))
    rail_a = moves.spread(mixed_a)
    merged_b = moves.gathered(rail_b)
    projected_b, near_b, far_b = project(merged_b, proj_weight, grad_of(picked, 1))
    near_b, far_b, rail_a = tied((near_b, far_b, rail_a))
    merged_a = moves.gathered(rail_a)
    terms_b = moves.send(near_b, far_b)
    projected_a, near_a, far_a = project(merged_a, proj_weight, grad_of(picked, 0))
    near_a, far_a, terms_b, projected_a, projected_b = tied(
        (near_a, far_a, terms_b, projected_a, projected_b)
    )
    terms_a = moves.send(near_a, far_a)

    projected = jnp.concatenate(
        [moves.by_rank(projected_a, size), moves.by_rank(projected_b, size)], 1
    ).reshape(images, image_rows, width)
    chosen = jnp.take(projected, image_of, axis=0, mode="clip")
    arrived = [chosen[s] for s in range(groups)]
    for s in range(1, groups):
        pairs = [(g, (g + s) % groups) for g in range(groups)]
        arrived[s] = lax.ppermute(arrived[s], "grp", pairs)

    def embed(text, arrived):
        goes_to = jnp.where(used[:, None], spot[:, None] + span, seq_len).reshape(-1)
        picks = jnp.arange(seq_len)[:, None] == goes_to[None, :]
        placed = jnp.dot(
            picks.astype(jnp.bfloat16),
            jnp.concatenate(arrived, 0),
            preferred_element_type=jnp.float32,
        ).astype(jnp.bfloat16)
        return jnp.where(jnp.any(picks, 1, keepdims=True), placed, text)

    own_b, scaled_b = unmerge(moves.summed(terms_b), *stats_b)
    rail_b = moves.spread(scaled_b)
    rail_b, terms_a, arrived = tied((rail_b, terms_a, arrived))
    own_a, scaled_a = unmerge(moves.summed(terms_a), *stats_a)
    rail_a = moves.spread(scaled_a)
    grad_out_b = moves.gathered(rail_b)
    near_b, far_b = vision_pass(grad_out_b, late, early, slope_b)
    near_b, far_b, rail_a = tied((near_b, far_b, rail_a))
    grad_out_a = moves.gathered(rail_a)
    terms_b = moves.send(near_b, far_b)
    near_a, far_a = vision_pass(grad_out_a, late, early, slope_a)
    near_a, far_a, terms_b, arrived = tied((near_a, far_a, terms_b, arrived))
    terms_a = moves.send(near_a, far_a)
    normed_b = moves.summed(terms_b)
    terms_a, seq_embed, normed_b = tied((terms_a, embed(text_embed, arrived), normed_b))
    normed_a = moves.summed(terms_a)
    grads = [
        own_a + norm_back(normed_a, vis_gain, hat[0], inv[0]),
        own_b + norm_back(normed_b, vis_gain, hat[1], inv[1]),
    ]
    grad_vision = jnp.concatenate(grads, 0).astype(jnp.bfloat16)
    return (seq_embed, grad_vision)


def solution(mesh):
    placed = (
        P(("grp", "tp"), None),
        P(),
        P(None, "tp"),
        P("tp", None),
        P(),
        P(),
        P(None, "tp"),
        P("grp", "tp"),
        P(),
        P("grp", "tp"),
    )
    return jax.shard_map(
        per_device,
        mesh=mesh,
        in_specs=placed,
        out_specs=(P("grp", "tp"), P(("grp", "tp"), None)),
        check_vma=False,
    )
```

```python
import functools

import jax
import jax.numpy as jnp
from jax import lax
from jax.experimental import pallas as pl
from jax.experimental.pallas import tpu as pltpu
from jax.sharding import PartitionSpec as P

vis_eps = 1e-06
proj_eps = 1e-05
chunks = 2
images = 4
cores = 2


def layer_norm(values, scale_vec, epsilon):
    mean_val = jnp.mean(values, -1, keepdims=True)
    centred = values - mean_val
    inv_std = lax.rsqrt(jnp.mean(centred * centred, -1, keepdims=True) + epsilon)
    normed = centred * inv_std
    return (normed * scale_vec, normed, inv_std)


def norm_back(upstream, scale_vec, normed, inv_std):
    scaled = upstream * scale_vec
    return inv_std * (
        scaled
        - jnp.mean(scaled, -1, keepdims=True)
        - normed * jnp.mean(scaled * normed, -1, keepdims=True)
    )


def times_transposed(left, right):
    return lax.dot_general(
        left, right, (((1,), (1,)), ((), ())), preferred_element_type=jnp.float32
    )


def tile_of(length, most):
    return max(t for t in range(128, most + 1, 128) if length % t == 0)


def laid(pieces):
    if len(pieces) == 1:
        return pieces[0][...]
    if pieces[0].shape[0] % 16 == 0:
        return jnp.concatenate([p[...] for p in pieces], 0)
    return jnp.concatenate([p[...].astype(jnp.float32) for p in pieces], 0).astype(jnp.bfloat16)


def each_rows(total, body):
    step = 32 if total % 32 == 0 else total

    def run(i, _):
        body(pl.ds(pl.multiple_of(i * step, step), step))
        return 0

    lax.fori_loop(0, total // step, run, 0)


def block_start(total, rows, j):
    return pl.multiple_of(jnp.minimum(j * rows, total - rows), 16)


def fetch(source, held, sems, j):
    count, rows = held.shape[:2]

    @pl.when(j < count)
    def _():
        part = source.at[pl.ds(block_start(source.shape[0], rows, j), rows)]
        pltpu.make_async_copy(part, held.at[j], sems.at[j]).start()


def arrive(source, held, sems, j):
    rows = held.shape[1]
    pltpu.make_async_copy(source.at[pl.ds(0, rows)], held.at[j], sems.at[j]).wait()


def vision_kernel(count, ahead, *refs):
    pieces = refs[:count]
    if ahead:
        early, late, near, far, slope = refs[count : count + 5]
    else:
        early, late, slope, near, far = refs[count : count + 5]
    first, second, rows, total, pre, hidden, first_sems, second_sems = refs[count + 5 :]
    fetch(early, first, first_sems, 0)
    fetch(late, second, second_sems, 0)
    rows[...] = laid(pieces)
    total[...] = jnp.zeros_like(total)
    size = first.shape[1]
    width = rows.shape[1]
    tile = min(1280, width)
    spans = [(k, min(tile, width - k)) for k in range(0, width, tile)]

    def block(j, _):
        arrive(early, first, first_sems, j)
        fetch(early, first, first_sems, j + 1)
        pre[...] = times_transposed(rows[...], first[j])
        repeated = j * size - jnp.minimum(j * size, early.shape[0] - size)

        def act(sel):
            u = pre[sel, :]
            if ahead:
                fresh = lax.broadcasted_iota(jnp.int32, u.shape, 1) >= repeated
                cumul = 0.5 * (1.0 + lax.erf(u * 0.7071067811865476))
                dense = jnp.exp(-0.5 * u * u) * 0.3989422804014327
                hidden[sel, :] = jnp.where(fresh, u * cumul, 0.0).astype(jnp.bfloat16)
                slope[j, sel, :] = jnp.where(fresh, cumul + u * dense, 0.0)
            else:
                hidden[sel, :] = (u * slope[j, sel, :]).astype(jnp.bfloat16)

        each_rows(pre.shape[0], act)
        arrive(late, second, second_sems, j)
        fetch(late, second, second_sems, j + 1)
        for k, length in spans:
            total[:, k : k + length] += jnp.dot(
                hidden[...], second[j, :, k : k + length], preferred_element_type=jnp.float32
            )
        return 0

    lax.fori_loop(0, first.shape[0], block, 0)
    half = near.shape[0]
    near[...] = total[:half].astype(jnp.bfloat16)
    far[...] = total[half:].astype(jnp.bfloat16)


def project_kernel(count, *refs):
    pieces = refs[:count]
    weight, upstream, projected, delta, held, rows, pre, sems = refs[count:]
    for j in range(3):
        fetch(weight, held, sems, j)
    rows[...] = laid(pieces)
    pre[...] = jnp.zeros_like(pre)
    chunk = held.shape[1]

    def ahead(j, _):
        arrive(weight, held, sems, j)
        fetch(weight, held, sems, j + 3)
        sel = pl.ds(pl.multiple_of(j * chunk, 128), chunk)
        pre[...] += jnp.dot(rows[:, sel], held[j], preferred_element_type=jnp.float32)
        return 0

    lax.fori_loop(0, held.shape[0], ahead, 0)

    def act(sel):
        u = pre[sel, :]
        cumul = 0.5 * (1.0 + lax.erf(u * 0.7071067811865476))
        dense = jnp.exp(-0.5 * u * u) * 0.3989422804014327
        projected[sel, :] = (u * cumul).astype(jnp.bfloat16)
        grad = upstream[sel, :].astype(jnp.float32)
        delta[sel, :] = (grad * (cumul + u * dense)).astype(jnp.bfloat16)

    each_rows(pre.shape[0], act)


def project_back_kernel(delta, weight, near, far, held, sems):
    for j in range(3):
        fetch(weight, held, sems, j)
    chunk = held.shape[1]
    half = near.shape[0]

    def behind(j, _):
        arrive(weight, held, sems, j)
        fetch(weight, held, sems, j + 3)
        sel = pl.ds(pl.multiple_of(j * chunk, 128), chunk)
        back = times_transposed(delta[...], held[j]).astype(jnp.bfloat16)
        near[:, sel] = back[:half]
        far[:, sel] = back[half:]
        return 0

    lax.fori_loop(0, held.shape[0], behind, 0)


def settings():
    return pltpu.CompilerParams(vmem_limit_bytes=56 * 1024 * 1024)


def whole_blocks(count):
    return [pl.BlockSpec(memory_space=pltpu.VMEM)] * count


def vision_pass(pieces, early, late, slope=None):
    rows = sum(p.shape[0] for p in pieces)
    units, width = early.shape
    size = min(256, units)
    blocks = -(-units // size)
    given = [] if slope is None else [slope]
    slopes = [jax.ShapeDtypeStruct((blocks, rows, size), jnp.float32)] * (1 - len(given))
    return pl.pallas_call(
        functools.partial(vision_kernel, len(pieces), slope is None),
        in_specs=whole_blocks(len(pieces))
        + [pl.BlockSpec(memory_space=pl.ANY)] * 2
        + whole_blocks(len(given)),
        out_specs=whole_blocks(2 + len(slopes)),
        out_shape=[jax.ShapeDtypeStruct((rows // 2, width), jnp.bfloat16)] * 2 + slopes,
        scratch_shapes=[
            pltpu.VMEM((blocks, size, width), jnp.bfloat16),
            pltpu.VMEM((blocks, size, width), jnp.bfloat16),
            pltpu.VMEM((rows, width), jnp.bfloat16),
            pltpu.VMEM((rows, width), jnp.float32),
            pltpu.VMEM((rows, size), jnp.float32),
            pltpu.VMEM((rows, size), jnp.bfloat16),
            pltpu.SemaphoreType.DMA((blocks,)),
            pltpu.SemaphoreType.DMA((blocks,)),
        ],
        compiler_params=settings(),
        cost_estimate=pl.CostEstimate(
            flops=4 * rows * width * units,
            bytes_accessed=4 * width * units + 4 * rows * (width + units),
            transcendentals=2 * rows * units,
        ),
    )(*pieces, early, late, *given)


def weight_cost(rows, depth, units):
    return pl.CostEstimate(
        flops=2 * rows * depth * units,
        bytes_accessed=2 * depth * units + 4 * rows * (depth + units),
        transcendentals=2 * rows * units,
    )


def project(pieces, weight, upstream):
    rows = sum(p.shape[0] for p in pieces)
    depth, units = weight.shape
    size = tile_of(depth, 1280)
    return pl.pallas_call(
        functools.partial(project_kernel, len(pieces)),
        in_specs=whole_blocks(len(pieces)) + [pl.BlockSpec(memory_space=pl.ANY)] + whole_blocks(1),
        out_specs=whole_blocks(2),
        out_shape=[jax.ShapeDtypeStruct((rows, units), jnp.bfloat16)] * 2,
        scratch_shapes=[
            pltpu.VMEM((depth // size, size, units), jnp.bfloat16),
            pltpu.VMEM((rows, depth), jnp.bfloat16),
            pltpu.VMEM((rows, units), jnp.float32),
            pltpu.SemaphoreType.DMA((depth // size,)),
        ],
        compiler_params=settings(),
        cost_estimate=weight_cost(rows, depth, units),
    )(*pieces, weight, upstream)


def project_back(delta, weight):
    rows = delta.shape[0]
    depth, units = weight.shape
    size = tile_of(depth, 1280)
    return pl.pallas_call(
        project_back_kernel,
        in_specs=whole_blocks(1) + [pl.BlockSpec(memory_space=pl.ANY)],
        out_specs=whole_blocks(2),
        out_shape=[jax.ShapeDtypeStruct((rows // 2, depth), jnp.bfloat16)] * 2,
        scratch_shapes=[
            pltpu.VMEM((depth // size, size, units), jnp.bfloat16),
            pltpu.SemaphoreType.DMA((depth // size,)),
        ],
        compiler_params=settings(),
        cost_estimate=weight_cost(rows, depth, units),
    )(delta, weight)


class Direct:
    def __init__(self):
        self.size = lax.axis_size("tp")
        self.places = self.size // cores
        rank = lax.axis_index("tp")
        place, core = rank // cores, rank % cores
        partner = (place ^ jnp.arange(self.places)) * cores
        self.ranks = jnp.concatenate([partner + core, partner + 1 - core])
        every = jnp.arange(self.size)
        self.blocks = (every + core) % cores * self.places + (every // cores ^ place)
        self.pairs = [(a, a + 1 - 2 * (a % cores)) for a in range(self.size)]

    def shift(self, block, k):
        pairs = [(a, (a // cores ^ k) * cores + a % cores) for a in range(self.size)]
        return lax.ppermute(block, "tp", pairs)

    def spread(self, block):
        return [block] + [self.shift(block, k) for k in range(1, self.places)]

    def gathered(self, mine):
        other = [lax.ppermute(m, "tp", self.pairs) for m in mine]
        if mine[0].shape[0] % 8:
            return [jnp.concatenate(mine + other, 0)]
        return mine + other

    def combine(self, near, far):
        rows = near.shape[0] // self.places
        got = lax.ppermute(far, "tp", self.pairs)
        both = near.astype(jnp.float32) + got.astype(jnp.float32)
        cut = [both[k * rows : (k + 1) * rows] for k in range(self.places)]
        return cut[:1] + [c.astype(jnp.bfloat16) for c in cut[1:]]

    def send(self, cut):
        return cut[:1] + [self.shift(cut[k], k) for k in range(1, self.places)]

    def summed(self, terms):
        return sum([t.astype(jnp.float32) for t in terms[1:]], terms[0])

    def by_rank(self, rows, size):
        return jnp.take(rows.reshape(size, -1, rows.shape[-1]), self.blocks, axis=0, mode="clip")

    def by_row(self, ranks):
        return jnp.take(ranks, self.ranks, axis=0, mode="clip").reshape(-1, ranks.shape[-1])


def per_device(
    vision_in,
    vis_gain,
    first_weight,
    second_weight,
    layer_scale,
    proj_gain,
    proj_weight,
    text_embed,
    dest_row,
    cotangent,
):
    moves = Direct()
    groups = lax.axis_size("grp")
    size = lax.axis_size("tp")
    grp_rank = lax.axis_index("grp")
    seq_len, width = text_embed.shape
    merged_total = dest_row.shape[0] // groups
    image_rows = merged_total // images
    own_rows, vis_width = vision_in.shape
    merged_width = proj_gain.shape[0]
    fold = merged_width // vis_width
    rows = own_rows // chunks
    merged_rows = rows // fold

    x, hat, inv, normed = [], [], [], []
    for c in range(chunks):
        x.append(vision_in[c * rows : (c + 1) * rows].astype(jnp.float32))
        scaled, own_hat, own_inv = layer_norm(x[c], vis_gain, vis_eps)
        normed.append(scaled.astype(jnp.bfloat16))
        hat.append(own_hat)
        inv.append(own_inv)
    tied = lax.optimization_barrier
    rail_b = moves.spread(normed[1])

    starts = dest_row.reshape(groups, images, image_rows)[:, :, 0]
    start_pos = starts % seq_len
    shift = starts[0] // seq_len
    matches = (shift[None, :] == jnp.arange(groups)[:, None]).astype(jnp.int32)
    image_of = jnp.sum(matches * jnp.arange(images), 1)
    used = jnp.sum(matches, 1) > 0
    source = (grp_rank - jnp.arange(groups)) % groups
    from_group = (source[:, None] == jnp.arange(groups)).astype(jnp.int32)
    spot = jnp.sum(matches[:, None, :] * from_group[:, :, None] * start_pos[None], (1, 2))

    span = jnp.arange(image_rows)
    picked = jnp.take(cotangent, (spot[:, None] + span).reshape(-1), axis=0, mode="clip")
    picked = [picked[s * image_rows : (s + 1) * image_rows] for s in range(groups)]
    for s in range(1, groups):
        pairs = [(g, (g - s) % groups) for g in range(groups)]
        picked[s] = lax.ppermute(picked[s], "grp", pairs)

    normed[0], rail_b, picked = tied((normed[0], rail_b, picked))
    rail_a = moves.spread(normed[0])
    patches_b = moves.gathered(rail_b)

    def grad_of(picked, c):
        returned = jnp.take(jnp.stack(picked), shift, axis=0, mode="clip").reshape(size, -1, width)
        return moves.by_row(returned[:, c * merged_rows : (c + 1) * merged_rows])

    def merge(c, summed):
        outputs = (x[c] + layer_scale * summed).astype(jnp.bfloat16)
        merged = outputs.reshape(merged_rows, merged_width).astype(jnp.float32)
        scaled, own_hat, own_inv = layer_norm(merged, proj_gain, proj_eps)
        return scaled.astype(jnp.bfloat16), own_hat, own_inv

    def unmerge(back_sum, own_hat, own_inv):
        merged_grad = norm_back(back_sum, proj_gain, own_hat, own_inv).astype(jnp.bfloat16)
        own_grad = merged_grad.reshape(rows, vis_width).astype(jnp.float32)
        return own_grad, (own_grad * layer_scale).astype(jnp.bfloat16)

    early, late = first_weight.T, second_weight
    near_b, far_b, slope_b = vision_pass(patches_b, early, late)
    near_b, far_b, rail_a = tied((near_b, far_b, rail_a))
    patches_a = moves.gathered(rail_a)
    terms_b = moves.send(moves.combine(near_b, far_b))
    near_a, far_a, slope_a = vision_pass(patches_a, early, late)
    near_a, far_a, terms_b, picked = tied((near_a, far_a, terms_b, picked))
    mixed_b, *stats_b = merge(1, moves.summed(terms_b))
    rail_b = moves.spread(mixed_b)
    near_a, far_a, mixed_b = tied((near_a, far_a, mixed_b))
    terms_a = moves.send(moves.combine(near_a, far_a))
    merged_b = moves.gathered(rail_b)
    projected_b, delta_b = project(merged_b, proj_weight, grad_of(picked, 1))
    projected_b, delta_b, terms_a = tied((projected_b, delta_b, terms_a))
    mixed_a, *stats_a = merge(0, moves.summed(terms_a))
    rail_a = moves.spread(mixed_a)
    delta_b, mixed_a = tied((delta_b, mixed_a))
    near_b, far_b = project_back(delta_b, proj_weight)
    near_b, far_b, rail_a = tied((near_b, far_b, rail_a))
    terms_b = moves.send(moves.combine(near_b, far_b))
    merged_a = moves.gathered(rail_a)
    projected_a, delta_a = project(merged_a, proj_weight, grad_of(picked, 0))
    projected_a, delta_a, terms_b = tied((projected_a, delta_a, terms_b))
    own_b, scaled_b = unmerge(moves.summed(terms_b), *stats_b)
    rail_b = moves.spread(scaled_b)
    delta_a, scaled_b = tied((delta_a, scaled_b))
    near_a, far_a = project_back(delta_a, proj_weight)
    near_a, far_a, rail_b = tied((near_a, far_a, rail_b))
    terms_a = moves.send(moves.combine(near_a, far_a))
    grad_out_b = moves.gathered(rail_b)
    near_b, far_b = vision_pass(grad_out_b, late, early, slope_b)
    near_b, far_b, terms_a, projected_a, projected_b = tied(
        (near_b, far_b, terms_a, projected_a, projected_b)
    )
    own_a, scaled_a = unmerge(moves.summed(terms_a), *stats_a)
    rail_a = moves.spread(scaled_a)
    near_b, far_b, scaled_a, projected_a, projected_b = tied(
        (near_b, far_b, scaled_a, projected_a, projected_b)
    )
    cut_b = moves.combine(near_b, far_b)

    projected = jnp.concatenate(
        [moves.by_rank(projected_a, size), moves.by_rank(projected_b, size)], 1
    ).reshape(images, image_rows, width)
    chosen = jnp.take(projected, image_of, axis=0, mode="clip")
    arrived = [chosen[s] for s in range(groups)]
    for s in range(1, groups):
        pairs = [(g, (g + s) % groups) for g in range(groups)]
        arrived[s] = lax.ppermute(arrived[s], "grp", pairs)

    def embed(text, arrived):
        goes_to = jnp.where(used[:, None], spot[:, None] + span, seq_len).reshape(-1)
        picks = jnp.arange(seq_len)[:, None] == goes_to[None, :]
        placed = jnp.dot(
            picks.astype(jnp.bfloat16),
            jnp.concatenate(arrived, 0),
            preferred_element_type=jnp.float32,
        ).astype(jnp.bfloat16)
        return jnp.where(jnp.any(picks, 1, keepdims=True), placed, text)

    cut_b, rail_a, arrived = tied((cut_b, rail_a, arrived))
    terms_b = moves.send(cut_b)
    grad_out_a = moves.gathered(rail_a)
    near_a, far_a = vision_pass(grad_out_a, late, early, slope_a)
    near_a, far_a, terms_b, arrived = tied((near_a, far_a, terms_b, arrived))
    terms_a = moves.send(moves.combine(near_a, far_a))
    normed_b = moves.summed(terms_b)
    terms_a, seq_embed, normed_b = tied((terms_a, embed(text_embed, arrived), normed_b))
    normed_a = moves.summed(terms_a)
    grads = [
        own_a + norm_back(normed_a, vis_gain, hat[0], inv[0]),
        own_b + norm_back(normed_b, vis_gain, hat[1], inv[1]),
    ]
    grad_vision = jnp.concatenate(grads, 0).astype(jnp.bfloat16)
    return (seq_embed, grad_vision)


def solution(mesh):
    placed = (
        P(("grp", "tp"), None),
        P(),
        P(None, "tp"),
        P("tp", None),
        P(),
        P(),
        P(None, "tp"),
        P("grp", "tp"),
        P(),
        P("grp", "tp"),
    )
    return jax.shard_map(
        per_device,
        mesh=mesh,
        in_specs=placed,
        out_specs=(P("grp", "tp"), P(("grp", "tp"), None)),
        check_vma=False,
    )
```

```python
import functools

import jax
import jax.numpy as jnp
from jax import lax
from jax.experimental import pallas as pl
from jax.experimental.pallas import tpu as pltpu
from jax.sharding import PartitionSpec as P

vis_eps = 1e-06
proj_eps = 1e-05
chunks = 2
images = 4
cores = 2


def layer_norm(values, scale_vec, epsilon):
    mean_val = jnp.mean(values, -1, keepdims=True)
    centred = values - mean_val
    inv_std = lax.rsqrt(jnp.mean(centred * centred, -1, keepdims=True) + epsilon)
    normed = centred * inv_std
    return (normed * scale_vec, normed, inv_std)


def norm_back(upstream, scale_vec, normed, inv_std):
    scaled = upstream * scale_vec
    return inv_std * (
        scaled
        - jnp.mean(scaled, -1, keepdims=True)
        - normed * jnp.mean(scaled * normed, -1, keepdims=True)
    )


def times_transposed(left, right):
    return lax.dot_general(
        left, right, (((1,), (1,)), ((), ())), preferred_element_type=jnp.float32
    )


def tile_of(length, most):
    return max(t for t in range(128, most + 1, 128) if length % t == 0)


def laid(pieces):
    if len(pieces) == 1:
        return pieces[0][...]
    if pieces[0].shape[0] % 16 == 0:
        return jnp.concatenate([p[...] for p in pieces], 0)
    return jnp.concatenate([p[...].astype(jnp.float32) for p in pieces], 0).astype(jnp.bfloat16)


def each_rows(total, body):
    step = 32 if total % 32 == 0 else total

    def run(i, _):
        body(pl.ds(pl.multiple_of(i * step, step), step))
        return 0

    lax.fori_loop(0, total // step, run, 0)


def block_start(total, rows, j):
    return pl.multiple_of(jnp.minimum(j * rows, total - rows), 16)


def fetch(source, held, sems, j):
    count, rows = held.shape[:2]

    @pl.when(j < count)
    def _():
        part = source.at[pl.ds(block_start(source.shape[0], rows, j), rows)]
        pltpu.make_async_copy(part, held.at[j], sems.at[j]).start()


def arrive(source, held, sems, j):
    rows = held.shape[1]
    pltpu.make_async_copy(source.at[pl.ds(0, rows)], held.at[j], sems.at[j]).wait()


def vision_kernel(count, ahead, *refs):
    pieces = refs[:count]
    if ahead:
        early, late, near, far, slope = refs[count : count + 5]
    else:
        early, late, slope, near, far = refs[count : count + 5]
    first, second, rows, pre, hidden, first_sems, second_sems = refs[count + 5 :]
    blocks, size, width = first.shape
    for j in range(blocks):
        fetch(early, first, first_sems, j)
    rows[...] = laid(pieces)

    def block(j, _):
        arrive(early, first, first_sems, j)
        fetch(late, second, second_sems, j)
        pre[...] = times_transposed(rows[...], first[j])
        repeated = j * size - jnp.minimum(j * size, early.shape[0] - size)
        place = pl.ds(pl.multiple_of(j * size, min(size, 128)), size)

        def act(sel):
            u = pre[sel, :]
            if ahead:
                fresh = lax.broadcasted_iota(jnp.int32, u.shape, 1) >= repeated
                cumul = 0.5 * (1.0 + lax.erf(u * 0.7071067811865476))
                dense = jnp.exp(-0.5 * u * u) * 0.3989422804014327
                hidden[sel, place] = jnp.where(fresh, u * cumul, 0.0).astype(jnp.bfloat16)
                slope[j, sel, :] = jnp.where(fresh, cumul + u * dense, 0.0)
            else:
                hidden[sel, place] = (u * slope[j, sel, :]).astype(jnp.bfloat16)

        each_rows(pre.shape[0], act)
        return 0

    lax.fori_loop(0, blocks, block, 0)
    for j in range(blocks):
        arrive(late, second, second_sems, j)
    half = near.shape[0]
    tile = min(1280, width)
    for k in range(0, width, tile):
        span = slice(k, min(k + tile, width))
        held = second[:, :, span]
        both = jnp.dot(
            hidden[...],
            held.reshape(blocks * size, held.shape[2]),
            preferred_element_type=jnp.float32,
        ).astype(jnp.bfloat16)
        near[:, span] = both[:half]
        far[:, span] = both[half:]


def project_kernel(count, *refs):
    pieces = refs[:count]
    weight, upstream, projected, delta, held, rows, pre, sems = refs[count:]
    for j in range(3):
        fetch(weight, held, sems, j)
    rows[...] = laid(pieces)
    pre[...] = jnp.zeros_like(pre)
    chunk = held.shape[1]

    def ahead(j, _):
        arrive(weight, held, sems, j)
        fetch(weight, held, sems, j + 3)
        sel = pl.ds(pl.multiple_of(j * chunk, 128), chunk)
        pre[...] += jnp.dot(rows[:, sel], held[j], preferred_element_type=jnp.float32)
        return 0

    lax.fori_loop(0, held.shape[0], ahead, 0)

    def act(sel):
        u = pre[sel, :]
        cumul = 0.5 * (1.0 + lax.erf(u * 0.7071067811865476))
        dense = jnp.exp(-0.5 * u * u) * 0.3989422804014327
        projected[sel, :] = (u * cumul).astype(jnp.bfloat16)
        grad = upstream[sel, :].astype(jnp.float32)
        delta[sel, :] = (grad * (cumul + u * dense)).astype(jnp.bfloat16)

    each_rows(pre.shape[0], act)


def project_back_kernel(delta, weight, near, far, held, sems):
    for j in range(3):
        fetch(weight, held, sems, j)
    chunk = held.shape[1]
    half = near.shape[0]

    def behind(j, _):
        arrive(weight, held, sems, j)
        fetch(weight, held, sems, j + 3)
        sel = pl.ds(pl.multiple_of(j * chunk, 128), chunk)
        back = times_transposed(delta[...], held[j]).astype(jnp.bfloat16)
        near[:, sel] = back[:half]
        far[:, sel] = back[half:]
        return 0

    lax.fori_loop(0, held.shape[0], behind, 0)


def settings():
    return pltpu.CompilerParams(vmem_limit_bytes=56 * 1024 * 1024)


def whole_blocks(count):
    return [pl.BlockSpec(memory_space=pltpu.VMEM)] * count


def vision_pass(pieces, early, late, slope=None):
    rows = sum(p.shape[0] for p in pieces)
    units, width = early.shape
    size = min(256, units)
    blocks = -(-units // size)
    given = [] if slope is None else [slope]
    slopes = [jax.ShapeDtypeStruct((blocks, rows, size), jnp.float32)] * (1 - len(given))
    return pl.pallas_call(
        functools.partial(vision_kernel, len(pieces), slope is None),
        in_specs=whole_blocks(len(pieces))
        + [pl.BlockSpec(memory_space=pl.ANY)] * 2
        + whole_blocks(len(given)),
        out_specs=whole_blocks(2 + len(slopes)),
        out_shape=[jax.ShapeDtypeStruct((rows // 2, width), jnp.bfloat16)] * 2 + slopes,
        scratch_shapes=[
            pltpu.VMEM((blocks, size, width), jnp.bfloat16),
            pltpu.VMEM((blocks, size, width), jnp.bfloat16),
            pltpu.VMEM((rows, width), jnp.bfloat16),
            pltpu.VMEM((rows, size), jnp.float32),
            pltpu.VMEM((rows, blocks * size), jnp.bfloat16),
            pltpu.SemaphoreType.DMA((blocks,)),
            pltpu.SemaphoreType.DMA((blocks,)),
        ],
        compiler_params=settings(),
        cost_estimate=pl.CostEstimate(
            flops=4 * rows * width * units,
            bytes_accessed=4 * width * units + 4 * rows * (width + units),
            transcendentals=2 * rows * units,
        ),
    )(*pieces, early, late, *given)


def weight_cost(rows, depth, units):
    return pl.CostEstimate(
        flops=2 * rows * depth * units,
        bytes_accessed=2 * depth * units + 4 * rows * (depth + units),
        transcendentals=2 * rows * units,
    )


def project(pieces, weight, upstream):
    rows = sum(p.shape[0] for p in pieces)
    depth, units = weight.shape
    size = tile_of(depth, 1280)
    return pl.pallas_call(
        functools.partial(project_kernel, len(pieces)),
        in_specs=whole_blocks(len(pieces)) + [pl.BlockSpec(memory_space=pl.ANY)] + whole_blocks(1),
        out_specs=whole_blocks(2),
        out_shape=[jax.ShapeDtypeStruct((rows, units), jnp.bfloat16)] * 2,
        scratch_shapes=[
            pltpu.VMEM((depth // size, size, units), jnp.bfloat16),
            pltpu.VMEM((rows, depth), jnp.bfloat16),
            pltpu.VMEM((rows, units), jnp.float32),
            pltpu.SemaphoreType.DMA((depth // size,)),
        ],
        compiler_params=settings(),
        cost_estimate=weight_cost(rows, depth, units),
    )(*pieces, weight, upstream)


def project_back(delta, weight):
    rows = delta.shape[0]
    depth, units = weight.shape
    size = tile_of(depth, 1280)
    return pl.pallas_call(
        project_back_kernel,
        in_specs=whole_blocks(1) + [pl.BlockSpec(memory_space=pl.ANY)],
        out_specs=whole_blocks(2),
        out_shape=[jax.ShapeDtypeStruct((rows // 2, depth), jnp.bfloat16)] * 2,
        scratch_shapes=[
            pltpu.VMEM((depth // size, size, units), jnp.bfloat16),
            pltpu.SemaphoreType.DMA((depth // size,)),
        ],
        compiler_params=settings(),
        cost_estimate=weight_cost(rows, depth, units),
    )(delta, weight)


class Direct:
    def __init__(self):
        self.size = lax.axis_size("tp")
        self.places = self.size // cores
        rank = lax.axis_index("tp")
        place, core = rank // cores, rank % cores
        partner = (place ^ jnp.arange(self.places)) * cores
        self.ranks = jnp.concatenate([partner + core, partner + 1 - core])
        every = jnp.arange(self.size)
        self.blocks = (every + core) % cores * self.places + (every // cores ^ place)
        self.pairs = [(a, a + 1 - 2 * (a % cores)) for a in range(self.size)]

    def shift(self, block, k):
        pairs = [(a, (a // cores ^ k) * cores + a % cores) for a in range(self.size)]
        return lax.ppermute(block, "tp", pairs)

    def spread(self, block):
        return [block] + [self.shift(block, k) for k in range(1, self.places)]

    def gathered(self, mine):
        other = [lax.ppermute(m, "tp", self.pairs) for m in mine]
        if mine[0].shape[0] % 8:
            return [jnp.concatenate(mine + other, 0)]
        return mine + other

    def combine(self, near, far):
        rows = near.shape[0] // self.places
        got = lax.ppermute(far, "tp", self.pairs)
        both = near.astype(jnp.float32) + got.astype(jnp.float32)
        cut = [both[k * rows : (k + 1) * rows] for k in range(self.places)]
        return cut[:1] + [c.astype(jnp.bfloat16) for c in cut[1:]]

    def send(self, cut):
        return cut[:1] + [self.shift(cut[k], k) for k in range(1, self.places)]

    def summed(self, terms):
        return sum([t.astype(jnp.float32) for t in terms[1:]], terms[0])

    def by_rank(self, rows, size):
        return jnp.take(rows.reshape(size, -1, rows.shape[-1]), self.blocks, axis=0, mode="clip")

    def by_row(self, ranks):
        return jnp.take(ranks, self.ranks, axis=0, mode="clip").reshape(-1, ranks.shape[-1])


def per_device(
    vision_in,
    vis_gain,
    first_weight,
    second_weight,
    layer_scale,
    proj_gain,
    proj_weight,
    text_embed,
    dest_row,
    cotangent,
):
    moves = Direct()
    groups = lax.axis_size("grp")
    size = lax.axis_size("tp")
    grp_rank = lax.axis_index("grp")
    seq_len, width = text_embed.shape
    merged_total = dest_row.shape[0] // groups
    image_rows = merged_total // images
    own_rows, vis_width = vision_in.shape
    merged_width = proj_gain.shape[0]
    fold = merged_width // vis_width
    rows = own_rows // chunks
    merged_rows = rows // fold

    x, hat, inv, normed = [], [], [], []
    for c in range(chunks):
        x.append(vision_in[c * rows : (c + 1) * rows].astype(jnp.float32))
        scaled, own_hat, own_inv = layer_norm(x[c], vis_gain, vis_eps)
        normed.append(scaled.astype(jnp.bfloat16))
        hat.append(own_hat)
        inv.append(own_inv)
    tied = lax.optimization_barrier
    rail_b = moves.spread(normed[1])

    starts = dest_row.reshape(groups, images, image_rows)[:, :, 0]
    start_pos = starts % seq_len
    shift = starts[0] // seq_len
    matches = (shift[None, :] == jnp.arange(groups)[:, None]).astype(jnp.int32)
    image_of = jnp.sum(matches * jnp.arange(images), 1)
    used = jnp.sum(matches, 1) > 0
    source = (grp_rank - jnp.arange(groups)) % groups
    from_group = (source[:, None] == jnp.arange(groups)).astype(jnp.int32)
    spot = jnp.sum(matches[:, None, :] * from_group[:, :, None] * start_pos[None], (1, 2))

    span = jnp.arange(image_rows)
    picked = jnp.take(cotangent, (spot[:, None] + span).reshape(-1), axis=0, mode="clip")
    picked = [picked[s * image_rows : (s + 1) * image_rows] for s in range(groups)]
    for s in range(1, groups):
        pairs = [(g, (g - s) % groups) for g in range(groups)]
        picked[s] = lax.ppermute(picked[s], "grp", pairs)

    normed[0], rail_b, picked = tied((normed[0], rail_b, picked))
    rail_a = moves.spread(normed[0])
    patches_b = moves.gathered(rail_b)

    def grad_of(picked, c):
        returned = jnp.take(jnp.stack(picked), shift, axis=0, mode="clip").reshape(size, -1, width)
        return moves.by_row(returned[:, c * merged_rows : (c + 1) * merged_rows])

    def merge(c, summed):
        outputs = (x[c] + layer_scale * summed).astype(jnp.bfloat16)
        merged = outputs.reshape(merged_rows, merged_width).astype(jnp.float32)
        scaled, own_hat, own_inv = layer_norm(merged, proj_gain, proj_eps)
        return scaled.astype(jnp.bfloat16), own_hat, own_inv

    def unmerge(back_sum, own_hat, own_inv):
        merged_grad = norm_back(back_sum, proj_gain, own_hat, own_inv).astype(jnp.bfloat16)
        own_grad = merged_grad.reshape(rows, vis_width).astype(jnp.float32)
        return own_grad, (own_grad * layer_scale).astype(jnp.bfloat16)

    early, late = first_weight.T, second_weight
    near_b, far_b, slope_b = vision_pass(patches_b, early, late)
    near_b, far_b, rail_a = tied((near_b, far_b, rail_a))
    patches_a = moves.gathered(rail_a)
    terms_b = moves.send(moves.combine(near_b, far_b))
    near_a, far_a, slope_a = vision_pass(patches_a, early, late)
    near_a, far_a, terms_b, picked = tied((near_a, far_a, terms_b, picked))
    mixed_b, *stats_b = merge(1, moves.summed(terms_b))
    rail_b = moves.spread(mixed_b)
    near_a, far_a, mixed_b = tied((near_a, far_a, mixed_b))
    cut_a, rail_b, upstream = tied(
        (moves.combine(near_a, far_a), rail_b, [grad_of(picked, c) for c in range(chunks)])
    )
    terms_a = moves.send(cut_a)
    merged_b = moves.gathered(rail_b)
    projected_b, delta_b = project(merged_b, proj_weight, upstream[1])
    projected_b, delta_b, terms_a = tied((projected_b, delta_b, terms_a))
    mixed_a, *stats_a = merge(0, moves.summed(terms_a))
    rail_a = moves.spread(mixed_a)
    delta_b, mixed_a = tied((delta_b, mixed_a))
    near_b, far_b = project_back(delta_b, proj_weight)
    near_b, far_b, rail_a = tied((near_b, far_b, rail_a))
    terms_b = moves.send(moves.combine(near_b, far_b))
    merged_a = moves.gathered(rail_a)
    projected_a, delta_a = project(merged_a, proj_weight, upstream[0])
    projected_a, delta_a, terms_b = tied((projected_a, delta_a, terms_b))
    own_b, scaled_b = unmerge(moves.summed(terms_b), *stats_b)
    rail_b = moves.spread(scaled_b)
    delta_a, scaled_b = tied((delta_a, scaled_b))
    near_a, far_a = project_back(delta_a, proj_weight)
    near_a, far_a, rail_b = tied((near_a, far_a, rail_b))
    terms_a = moves.send(moves.combine(near_a, far_a))
    grad_out_b = moves.gathered(rail_b)
    near_b, far_b = vision_pass(grad_out_b, late, early, slope_b)
    near_b, far_b, terms_a, projected_a, projected_b = tied(
        (near_b, far_b, terms_a, projected_a, projected_b)
    )
    own_a, scaled_a = unmerge(moves.summed(terms_a), *stats_a)
    rail_a = moves.spread(scaled_a)
    near_b, far_b, scaled_a, projected_a, projected_b = tied(
        (near_b, far_b, scaled_a, projected_a, projected_b)
    )
    cut_b = moves.combine(near_b, far_b)

    projected = jnp.concatenate(
        [moves.by_rank(projected_a, size), moves.by_rank(projected_b, size)], 1
    ).reshape(images, image_rows, width)
    chosen = jnp.take(projected, image_of, axis=0, mode="clip")
    arrived = [chosen[s] for s in range(groups)]
    for s in range(1, groups):
        pairs = [(g, (g + s) % groups) for g in range(groups)]
        arrived[s] = lax.ppermute(arrived[s], "grp", pairs)

    def embed(text, arrived):
        goes_to = jnp.where(used[:, None], spot[:, None] + span, seq_len).reshape(-1)
        picks = jnp.arange(seq_len)[:, None] == goes_to[None, :]
        placed = jnp.dot(
            picks.astype(jnp.bfloat16),
            jnp.concatenate(arrived, 0),
            preferred_element_type=jnp.float32,
        ).astype(jnp.bfloat16)
        return jnp.where(jnp.any(picks, 1, keepdims=True), placed, text)

    cut_b, rail_a, arrived = tied((cut_b, rail_a, arrived))
    terms_b = moves.send(cut_b)
    grad_out_a = moves.gathered(rail_a)
    near_a, far_a = vision_pass(grad_out_a, late, early, slope_a)
    near_a, far_a, terms_b, arrived = tied((near_a, far_a, terms_b, arrived))
    terms_a = moves.send(moves.combine(near_a, far_a))
    normed_b = moves.summed(terms_b)
    terms_a, seq_embed, normed_b = tied((terms_a, embed(text_embed, arrived), normed_b))
    normed_a = moves.summed(terms_a)
    grads = [
        own_a + norm_back(normed_a, vis_gain, hat[0], inv[0]),
        own_b + norm_back(normed_b, vis_gain, hat[1], inv[1]),
    ]
    grad_vision = jnp.concatenate(grads, 0).astype(jnp.bfloat16)
    return (seq_embed, grad_vision)


def solution(mesh):
    placed = (
        P(("grp", "tp"), None),
        P(),
        P(None, "tp"),
        P("tp", None),
        P(),
        P(),
        P(None, "tp"),
        P("grp", "tp"),
        P(),
        P("grp", "tp"),
    )
    return jax.shard_map(
        per_device,
        mesh=mesh,
        in_specs=placed,
        out_specs=(P("grp", "tp"), P(("grp", "tp"), None)),
        check_vma=False,
    )
```

```python
import functools

import jax
import jax.numpy as jnp
from jax import lax
from jax.experimental import pallas as pl
from jax.experimental.pallas import tpu as pltpu
from jax.sharding import PartitionSpec as P

vis_eps = 1e-06
proj_eps = 1e-05
chunks = 2
images = 4
cores = 2


def layer_norm(values, scale_vec, epsilon):
    mean_val = jnp.mean(values, -1, keepdims=True)
    centred = values - mean_val
    inv_std = lax.rsqrt(jnp.mean(centred * centred, -1, keepdims=True) + epsilon)
    normed = centred * inv_std
    return (normed * scale_vec, normed, inv_std)


def norm_back(upstream, scale_vec, normed, inv_std):
    scaled = upstream * scale_vec
    return inv_std * (
        scaled
        - jnp.mean(scaled, -1, keepdims=True)
        - normed * jnp.mean(scaled * normed, -1, keepdims=True)
    )


def times_transposed(left, right):
    return lax.dot_general(
        left, right, (((1,), (1,)), ((), ())), preferred_element_type=jnp.float32
    )


def tile_of(length, most):
    return max(t for t in range(128, most + 1, 128) if length % t == 0)


def laid(pieces):
    if len(pieces) == 1:
        return pieces[0][...]
    if pieces[0].shape[0] % 16 == 0:
        return jnp.concatenate([p[...] for p in pieces], 0)
    return jnp.concatenate([p[...].astype(jnp.float32) for p in pieces], 0).astype(jnp.bfloat16)


def each_rows(total, body):
    step = 32 if total % 32 == 0 else total

    def run(i, _):
        body(pl.ds(pl.multiple_of(i * step, step), step))
        return 0

    lax.fori_loop(0, total // step, run, 0)


def block_start(total, rows, j):
    return pl.multiple_of(jnp.minimum(j * rows, total - rows), 16)


def fetch(source, held, sems, j):
    count, rows = held.shape[:2]

    @pl.when(j < count)
    def _():
        part = source.at[pl.ds(block_start(source.shape[0], rows, j), rows)]
        pltpu.make_async_copy(part, held.at[j], sems.at[j]).start()


def arrive(source, held, sems, j):
    rows = held.shape[1]
    pltpu.make_async_copy(source.at[pl.ds(0, rows)], held.at[j], sems.at[j]).wait()


def vision_kernel(count, ahead, *refs):
    pieces = refs[:count]
    if ahead:
        early, late, near, far, slope = refs[count : count + 5]
    else:
        early, late, slope, near, far = refs[count : count + 5]
    first, second, rows, pre, hidden, first_sems, second_sems = refs[count + 5 :]
    blocks, size, width = first.shape
    for j in range(blocks):
        fetch(early, first, first_sems, j)
    rows[...] = laid(pieces)

    def block(j, _):
        arrive(early, first, first_sems, j)
        fetch(late, second, second_sems, j)
        pre[...] = times_transposed(rows[...], first[j])
        repeated = j * size - jnp.minimum(j * size, early.shape[0] - size)
        place = pl.ds(pl.multiple_of(j * size, min(size, 128)), size)

        def act(sel):
            u = pre[sel, :]
            if ahead:
                fresh = lax.broadcasted_iota(jnp.int32, u.shape, 1) >= repeated
                cumul = 0.5 * (1.0 + lax.erf(u * 0.7071067811865476))
                dense = jnp.exp(-0.5 * u * u) * 0.3989422804014327
                hidden[sel, place] = jnp.where(fresh, u * cumul, 0.0).astype(jnp.bfloat16)
                slope[j, sel, :] = jnp.where(fresh, cumul + u * dense, 0.0)
            else:
                hidden[sel, place] = (u * slope[j, sel, :]).astype(jnp.bfloat16)

        each_rows(pre.shape[0], act)
        return 0

    lax.fori_loop(0, blocks, block, 0)
    for j in range(blocks):
        arrive(late, second, second_sems, j)
    half = near.shape[0]
    tile = min(1280, width)
    for k in range(0, width, tile):
        span = slice(k, min(k + tile, width))
        held = second[:, :, span]
        both = jnp.dot(
            hidden[...],
            held.reshape(blocks * size, held.shape[2]),
            preferred_element_type=jnp.float32,
        ).astype(jnp.bfloat16)
        near[:, span] = both[:half]
        far[:, span] = both[half:]


def project_kernel(count, *refs):
    pieces = refs[:count]
    weight, upstream, projected, delta, held, rows, pre, sems = refs[count:]
    for j in range(3):
        fetch(weight, held, sems, j)
    rows[...] = laid(pieces)
    pre[...] = jnp.zeros_like(pre)
    chunk = held.shape[1]

    def ahead(j, _):
        arrive(weight, held, sems, j)
        fetch(weight, held, sems, j + 3)
        sel = pl.ds(pl.multiple_of(j * chunk, 128), chunk)
        pre[...] += jnp.dot(rows[:, sel], held[j], preferred_element_type=jnp.float32)
        return 0

    lax.fori_loop(0, held.shape[0], ahead, 0)

    def act(sel):
        u = pre[sel, :]
        cumul = 0.5 * (1.0 + lax.erf(u * 0.7071067811865476))
        dense = jnp.exp(-0.5 * u * u) * 0.3989422804014327
        projected[sel, :] = (u * cumul).astype(jnp.bfloat16)
        grad = upstream[sel, :].astype(jnp.float32)
        delta[sel, :] = (grad * (cumul + u * dense)).astype(jnp.bfloat16)

    each_rows(pre.shape[0], act)


def project_back_kernel(delta, weight, near, far, held, sems):
    for j in range(3):
        fetch(weight, held, sems, j)
    chunk = held.shape[1]
    half = near.shape[0]

    def behind(j, _):
        arrive(weight, held, sems, j)
        fetch(weight, held, sems, j + 3)
        sel = pl.ds(pl.multiple_of(j * chunk, 128), chunk)
        back = times_transposed(delta[...], held[j]).astype(jnp.bfloat16)
        near[:, sel] = back[:half]
        far[:, sel] = back[half:]
        return 0

    lax.fori_loop(0, held.shape[0], behind, 0)


def entry_kernel(source, gain, *normed):
    rows = normed[0].shape[0]
    for c, out in enumerate(normed):
        values = source[c * rows : (c + 1) * rows].astype(jnp.float32)
        out[...] = layer_norm(values, gain[...], vis_eps)[0].astype(jnp.bfloat16)


def entry_norm(source, gain):
    rows, width = source.shape
    return pl.pallas_call(
        entry_kernel,
        in_specs=whole_blocks(2),
        out_specs=whole_blocks(chunks),
        out_shape=[jax.ShapeDtypeStruct((rows // chunks, width), jnp.bfloat16)] * chunks,
        cost_estimate=pl.CostEstimate(
            flops=8 * rows * width, bytes_accessed=4 * rows * width, transcendentals=rows
        ),
    )(source, gain.reshape(1, width))


def settings():
    return pltpu.CompilerParams(vmem_limit_bytes=56 * 1024 * 1024)


def whole_blocks(count):
    return [pl.BlockSpec(memory_space=pltpu.VMEM)] * count


def vision_pass(pieces, early, late, slope=None):
    rows = sum(p.shape[0] for p in pieces)
    units, width = early.shape
    size = min(256, units)
    blocks = -(-units // size)
    given = [] if slope is None else [slope]
    slopes = [jax.ShapeDtypeStruct((blocks, rows, size), jnp.float32)] * (1 - len(given))
    return pl.pallas_call(
        functools.partial(vision_kernel, len(pieces), slope is None),
        in_specs=whole_blocks(len(pieces))
        + [pl.BlockSpec(memory_space=pl.ANY)] * 2
        + whole_blocks(len(given)),
        out_specs=whole_blocks(2 + len(slopes)),
        out_shape=[jax.ShapeDtypeStruct((rows // 2, width), jnp.bfloat16)] * 2 + slopes,
        scratch_shapes=[
            pltpu.VMEM((blocks, size, width), jnp.bfloat16),
            pltpu.VMEM((blocks, size, width), jnp.bfloat16),
            pltpu.VMEM((rows, width), jnp.bfloat16),
            pltpu.VMEM((rows, size), jnp.float32),
            pltpu.VMEM((rows, blocks * size), jnp.bfloat16),
            pltpu.SemaphoreType.DMA((blocks,)),
            pltpu.SemaphoreType.DMA((blocks,)),
        ],
        compiler_params=settings(),
        cost_estimate=pl.CostEstimate(
            flops=4 * rows * width * units,
            bytes_accessed=4 * width * units + 4 * rows * (width + units),
            transcendentals=2 * rows * units,
        ),
    )(*pieces, early, late, *given)


def weight_cost(rows, depth, units):
    return pl.CostEstimate(
        flops=2 * rows * depth * units,
        bytes_accessed=2 * depth * units + 4 * rows * (depth + units),
        transcendentals=2 * rows * units,
    )


def project(pieces, weight, upstream):
    rows = sum(p.shape[0] for p in pieces)
    depth, units = weight.shape
    size = tile_of(depth, 1280)
    return pl.pallas_call(
        functools.partial(project_kernel, len(pieces)),
        in_specs=whole_blocks(len(pieces)) + [pl.BlockSpec(memory_space=pl.ANY)] + whole_blocks(1),
        out_specs=whole_blocks(2),
        out_shape=[jax.ShapeDtypeStruct((rows, units), jnp.bfloat16)] * 2,
        scratch_shapes=[
            pltpu.VMEM((depth // size, size, units), jnp.bfloat16),
            pltpu.VMEM((rows, depth), jnp.bfloat16),
            pltpu.VMEM((rows, units), jnp.float32),
            pltpu.SemaphoreType.DMA((depth // size,)),
        ],
        compiler_params=settings(),
        cost_estimate=weight_cost(rows, depth, units),
    )(*pieces, weight, upstream)


def project_back(delta, weight):
    rows = delta.shape[0]
    depth, units = weight.shape
    size = tile_of(depth, 1280)
    return pl.pallas_call(
        project_back_kernel,
        in_specs=whole_blocks(1) + [pl.BlockSpec(memory_space=pl.ANY)],
        out_specs=whole_blocks(2),
        out_shape=[jax.ShapeDtypeStruct((rows // 2, depth), jnp.bfloat16)] * 2,
        scratch_shapes=[
            pltpu.VMEM((depth // size, size, units), jnp.bfloat16),
            pltpu.SemaphoreType.DMA((depth // size,)),
        ],
        compiler_params=settings(),
        cost_estimate=weight_cost(rows, depth, units),
    )(delta, weight)


class Direct:
    def __init__(self):
        self.size = lax.axis_size("tp")
        self.places = self.size // cores
        rank = lax.axis_index("tp")
        place, core = rank // cores, rank % cores
        partner = (place ^ jnp.arange(self.places)) * cores
        self.ranks = jnp.concatenate([partner + core, partner + 1 - core])
        every = jnp.arange(self.size)
        self.blocks = (every + core) % cores * self.places + (every // cores ^ place)
        self.pairs = [(a, a + 1 - 2 * (a % cores)) for a in range(self.size)]

    def shift(self, block, k):
        pairs = [(a, (a // cores ^ k) * cores + a % cores) for a in range(self.size)]
        return lax.ppermute(block, "tp", pairs)

    def spread(self, block):
        return [block] + [self.shift(block, k) for k in range(1, self.places)]

    def gathered(self, mine):
        other = [lax.ppermute(m, "tp", self.pairs) for m in mine]
        if mine[0].shape[0] % 8:
            return [jnp.concatenate(mine + other, 0)]
        return mine + other

    def combine(self, near, far):
        rows = near.shape[0] // self.places
        got = lax.ppermute(far, "tp", self.pairs)
        both = near.astype(jnp.float32) + got.astype(jnp.float32)
        cut = [both[k * rows : (k + 1) * rows] for k in range(self.places)]
        return cut[:1] + [c.astype(jnp.bfloat16) for c in cut[1:]]

    def send(self, cut):
        return cut[:1] + [self.shift(cut[k], k) for k in range(1, self.places)]

    def summed(self, terms):
        return sum([t.astype(jnp.float32) for t in terms[1:]], terms[0])

    def by_rank(self, rows, size):
        return jnp.take(rows.reshape(size, -1, rows.shape[-1]), self.blocks, axis=0, mode="clip")

    def by_row(self, ranks):
        return jnp.take(ranks, self.ranks, axis=0, mode="clip").reshape(-1, ranks.shape[-1])


def per_device(
    vision_in,
    vis_gain,
    first_weight,
    second_weight,
    layer_scale,
    proj_gain,
    proj_weight,
    text_embed,
    dest_row,
    cotangent,
):
    moves = Direct()
    groups = lax.axis_size("grp")
    size = lax.axis_size("tp")
    grp_rank = lax.axis_index("grp")
    seq_len, width = text_embed.shape
    merged_total = dest_row.shape[0] // groups
    image_rows = merged_total // images
    own_rows, vis_width = vision_in.shape
    merged_width = proj_gain.shape[0]
    fold = merged_width // vis_width
    rows = own_rows // chunks
    merged_rows = rows // fold

    normed = list(entry_norm(vision_in, vis_gain))
    x = [vision_in[c * rows : (c + 1) * rows].astype(jnp.float32) for c in range(chunks)]

    tied = lax.optimization_barrier
    rail_b = moves.spread(normed[1])

    starts = dest_row.reshape(groups, images, image_rows)[:, :, 0]
    start_pos = starts % seq_len
    shift = starts[0] // seq_len
    matches = (shift[None, :] == jnp.arange(groups)[:, None]).astype(jnp.int32)
    image_of = jnp.sum(matches * jnp.arange(images), 1)
    used = jnp.sum(matches, 1) > 0
    source = (grp_rank - jnp.arange(groups)) % groups
    from_group = (source[:, None] == jnp.arange(groups)).astype(jnp.int32)
    spot = jnp.sum(matches[:, None, :] * from_group[:, :, None] * start_pos[None], (1, 2))

    span = jnp.arange(image_rows)
    picked = jnp.take(cotangent, (spot[:, None] + span).reshape(-1), axis=0, mode="clip")
    picked = [picked[s * image_rows : (s + 1) * image_rows] for s in range(groups)]
    for s in range(1, groups):
        pairs = [(g, (g - s) % groups) for g in range(groups)]
        picked[s] = lax.ppermute(picked[s], "grp", pairs)

    normed[0], rail_b, picked = tied((normed[0], rail_b, picked))
    rail_a = moves.spread(normed[0])
    patches_b = moves.gathered(rail_b)

    def grad_of(picked, c):
        returned = jnp.take(jnp.stack(picked), shift, axis=0, mode="clip").reshape(size, -1, width)
        return moves.by_row(returned[:, c * merged_rows : (c + 1) * merged_rows])

    def merge(c, summed):
        outputs = (x[c] + layer_scale * summed).astype(jnp.bfloat16)
        merged = outputs.reshape(merged_rows, merged_width).astype(jnp.float32)
        scaled, own_hat, own_inv = layer_norm(merged, proj_gain, proj_eps)
        return scaled.astype(jnp.bfloat16), own_hat, own_inv

    def unmerge(back_sum, own_hat, own_inv):
        merged_grad = norm_back(back_sum, proj_gain, own_hat, own_inv).astype(jnp.bfloat16)
        own_grad = merged_grad.reshape(rows, vis_width).astype(jnp.float32)
        return own_grad, (own_grad * layer_scale).astype(jnp.bfloat16)

    early, late = first_weight.T, second_weight
    near_b, far_b, slope_b = vision_pass(patches_b, early, late)
    near_b, far_b, rail_a = tied((near_b, far_b, rail_a))
    patches_a = moves.gathered(rail_a)
    terms_b = moves.send(moves.combine(near_b, far_b))
    near_a, far_a, slope_a = vision_pass(patches_a, early, late)
    near_a, far_a, terms_b, picked = tied((near_a, far_a, terms_b, picked))
    mixed_b, *stats_b = merge(1, moves.summed(terms_b))
    rail_b = moves.spread(mixed_b)
    near_a, far_a, mixed_b = tied((near_a, far_a, mixed_b))
    cut_a, upstream = tied(
        (moves.combine(near_a, far_a), [grad_of(picked, c) for c in range(chunks)])
    )
    terms_a = moves.send(cut_a)
    rail_b, terms_a[1] = tied((rail_b, terms_a[1]))
    merged_b = moves.gathered(rail_b)
    projected_b, delta_b = project(merged_b, proj_weight, upstream[1])
    projected_b, delta_b, terms_a = tied((projected_b, delta_b, terms_a))
    mixed_a, *stats_a = merge(0, moves.summed(terms_a))
    rail_a = moves.spread(mixed_a)
    delta_b, mixed_a = tied((delta_b, mixed_a))
    near_b, far_b = project_back(delta_b, proj_weight)
    near_b, far_b, rail_a = tied((near_b, far_b, rail_a))
    terms_b = moves.send(moves.combine(near_b, far_b))
    merged_a = moves.gathered(rail_a)
    projected_a, delta_a = project(merged_a, proj_weight, upstream[0])
    projected_a, delta_a, terms_b = tied((projected_a, delta_a, terms_b))
    own_b, scaled_b = unmerge(moves.summed(terms_b), *stats_b)
    rail_b = moves.spread(scaled_b)
    delta_a, scaled_b = tied((delta_a, scaled_b))
    near_a, far_a = project_back(delta_a, proj_weight)
    near_a, far_a, rail_b = tied((near_a, far_a, rail_b))
    terms_a = moves.send(moves.combine(near_a, far_a))
    grad_out_b = moves.gathered(rail_b)
    near_b, far_b = vision_pass(grad_out_b, late, early, slope_b)
    near_b, far_b, terms_a, projected_a, projected_b = tied(
        (near_b, far_b, terms_a, projected_a, projected_b)
    )
    own_a, scaled_a = unmerge(moves.summed(terms_a), *stats_a)
    rail_a = moves.spread(scaled_a)
    near_b, far_b, scaled_a, projected_a, projected_b = tied(
        (near_b, far_b, scaled_a, projected_a, projected_b)
    )
    cut_b = moves.combine(near_b, far_b)

    projected = jnp.concatenate(
        [moves.by_rank(projected_a, size), moves.by_rank(projected_b, size)], 1
    ).reshape(images, image_rows, width)
    chosen = jnp.take(projected, image_of, axis=0, mode="clip")
    arrived = [chosen[s] for s in range(groups)]
    for s in range(1, groups):
        pairs = [(g, (g + s) % groups) for g in range(groups)]
        arrived[s] = lax.ppermute(arrived[s], "grp", pairs)

    def embed(text, arrived):
        goes_to = jnp.where(used[:, None], spot[:, None] + span, seq_len).reshape(-1)
        picks = jnp.arange(seq_len)[:, None] == goes_to[None, :]
        placed = jnp.dot(
            picks.astype(jnp.bfloat16),
            jnp.concatenate(arrived, 0),
            preferred_element_type=jnp.float32,
        ).astype(jnp.bfloat16)
        return jnp.where(jnp.any(picks, 1, keepdims=True), placed, text)

    cut_b, rail_a, arrived = tied((cut_b, rail_a, arrived))
    terms_b = moves.send(cut_b)
    grad_out_a = moves.gathered(rail_a)
    near_a, far_a = vision_pass(grad_out_a, late, early, slope_a)
    near_a, far_a, terms_b, arrived = tied((near_a, far_a, terms_b, arrived))
    terms_a = moves.send(moves.combine(near_a, far_a))
    normed_b = moves.summed(terms_b)
    terms_a, seq_embed, normed_b = tied((terms_a, embed(text_embed, arrived), normed_b))
    normed_a = moves.summed(terms_a)
    parts = [layer_norm(x[c], vis_gain, vis_eps) for c in range(chunks)]
    grads = [
        own_a + norm_back(normed_a, vis_gain, parts[0][1], parts[0][2]),
        own_b + norm_back(normed_b, vis_gain, parts[1][1], parts[1][2]),
    ]
    grad_vision = jnp.concatenate(grads, 0).astype(jnp.bfloat16)
    return (seq_embed, grad_vision)


def solution(mesh):
    placed = (
        P(("grp", "tp"), None),
        P(),
        P(None, "tp"),
        P("tp", None),
        P(),
        P(),
        P(None, "tp"),
        P("grp", "tp"),
        P(),
        P("grp", "tp"),
    )
    return jax.shard_map(
        per_device,
        mesh=mesh,
        in_specs=placed,
        out_specs=(P("grp", "tp"), P(("grp", "tp"), None)),
        check_vma=False,
    )
```

```python
import functools

import jax
import jax.numpy as jnp
from jax import lax
from jax.experimental import pallas as pl
from jax.experimental.pallas import tpu as pltpu
from jax.sharding import PartitionSpec as P

vis_eps = 1e-06
proj_eps = 1e-05
chunks = 2
images = 4
cores = 2


def layer_norm(values, scale_vec, epsilon):
    mean_val = jnp.mean(values, -1, keepdims=True)
    centred = values - mean_val
    inv_std = lax.rsqrt(jnp.mean(centred * centred, -1, keepdims=True) + epsilon)
    normed = centred * inv_std
    return (normed * scale_vec, normed, inv_std)


def norm_back(upstream, scale_vec, normed, inv_std):
    scaled = upstream * scale_vec
    return inv_std * (
        scaled
        - jnp.mean(scaled, -1, keepdims=True)
        - normed * jnp.mean(scaled * normed, -1, keepdims=True)
    )


def times_transposed(left, right):
    return lax.dot_general(
        left, right, (((1,), (1,)), ((), ())), preferred_element_type=jnp.float32
    )


def tile_of(length, most):
    return max(t for t in range(128, most + 1, 128) if length % t == 0)


def laid(pieces):
    if len(pieces) == 1:
        return pieces[0][...]
    if pieces[0].shape[0] % 16 == 0:
        return jnp.concatenate([p[...] for p in pieces], 0)
    return jnp.concatenate([p[...].astype(jnp.float32) for p in pieces], 0).astype(jnp.bfloat16)


def each_rows(total, body):
    step = 32 if total % 32 == 0 else total

    def run(i, _):
        body(pl.ds(pl.multiple_of(i * step, step), step))
        return 0

    lax.fori_loop(0, total // step, run, 0)


def block_start(total, rows, j):
    return pl.multiple_of(jnp.minimum(j * rows, total - rows), 16)


def fetch(source, held, sems, j):
    count, rows = held.shape[:2]

    @pl.when(j < count)
    def _():
        part = source.at[pl.ds(block_start(source.shape[0], rows, j), rows)]
        pltpu.make_async_copy(part, held.at[j], sems.at[j]).start()


def arrive(source, held, sems, j):
    rows = held.shape[1]
    pltpu.make_async_copy(source.at[pl.ds(0, rows)], held.at[j], sems.at[j]).wait()


def vision_kernel(count, ahead, *refs):
    pieces = refs[:count]
    if ahead:
        early, late, near, far, slope = refs[count : count + 5]
    else:
        early, late, slope, near, far = refs[count : count + 5]
    first, second, rows, pre, hidden, first_sems, second_sems = refs[count + 5 :]
    blocks, size, width = first.shape
    for j in range(blocks):
        fetch(early, first, first_sems, j)
    rows[...] = laid(pieces)

    def block(j, _):
        arrive(early, first, first_sems, j)
        fetch(late, second, second_sems, j)
        pre[...] = times_transposed(rows[...], first[j])
        repeated = j * size - jnp.minimum(j * size, early.shape[0] - size)
        place = pl.ds(pl.multiple_of(j * size, min(size, 128)), size)

        def act(sel):
            u = pre[sel, :]
            if ahead:
                fresh = lax.broadcasted_iota(jnp.int32, u.shape, 1) >= repeated
                cumul = 0.5 * (1.0 + lax.erf(u * 0.7071067811865476))
                dense = jnp.exp(-0.5 * u * u) * 0.3989422804014327
                hidden[sel, place] = jnp.where(fresh, u * cumul, 0.0).astype(jnp.bfloat16)
                slope[j, sel, :] = jnp.where(fresh, cumul + u * dense, 0.0)
            else:
                hidden[sel, place] = (u * slope[j, sel, :]).astype(jnp.bfloat16)

        each_rows(pre.shape[0], act)
        return 0

    lax.fori_loop(0, blocks, block, 0)
    for j in range(blocks):
        arrive(late, second, second_sems, j)
    half = near.shape[0]
    tile = min(1280, width)
    for k in range(0, width, tile):
        span = slice(k, min(k + tile, width))
        held = second[:, :, span]
        both = jnp.dot(
            hidden[...],
            held.reshape(blocks * size, held.shape[2]),
            preferred_element_type=jnp.float32,
        ).astype(jnp.bfloat16)
        near[:, span] = both[:half]
        far[:, span] = both[half:]


def project_kernel(count, *refs):
    pieces = refs[:count]
    weight, upstream, projected, delta, held, rows, pre, sems = refs[count:]
    for j in range(3):
        fetch(weight, held, sems, j)
    rows[...] = laid(pieces)
    pre[...] = jnp.zeros_like(pre)
    chunk = held.shape[1]

    def ahead(j, _):
        arrive(weight, held, sems, j)
        fetch(weight, held, sems, j + 3)
        sel = pl.ds(pl.multiple_of(j * chunk, 128), chunk)
        pre[...] += jnp.dot(rows[:, sel], held[j], preferred_element_type=jnp.float32)
        return 0

    lax.fori_loop(0, held.shape[0], ahead, 0)

    def act(sel):
        u = pre[sel, :]
        cumul = 0.5 * (1.0 + lax.erf(u * 0.7071067811865476))
        dense = jnp.exp(-0.5 * u * u) * 0.3989422804014327
        projected[sel, :] = (u * cumul).astype(jnp.bfloat16)
        grad = upstream[sel, :].astype(jnp.float32)
        delta[sel, :] = (grad * (cumul + u * dense)).astype(jnp.bfloat16)

    each_rows(pre.shape[0], act)


def project_back_kernel(delta, weight, near, far, held, sems):
    for j in range(3):
        fetch(weight, held, sems, j)
    chunk = held.shape[1]
    half = near.shape[0]

    def behind(j, _):
        arrive(weight, held, sems, j)
        fetch(weight, held, sems, j + 3)
        sel = pl.ds(pl.multiple_of(j * chunk, 128), chunk)
        back = times_transposed(delta[...], held[j]).astype(jnp.bfloat16)
        near[:, sel] = back[:half]
        far[:, sel] = back[half:]
        return 0

    lax.fori_loop(0, held.shape[0], behind, 0)


def entry_kernel(source, gain, *normed):
    rows = normed[0].shape[0]
    for c, out in enumerate(normed):
        values = source[c * rows : (c + 1) * rows].astype(jnp.float32)
        out[...] = layer_norm(values, gain[...][None, :], vis_eps)[0].astype(jnp.bfloat16)


def entry_norm(source, gain):
    rows, width = source.shape
    return pl.pallas_call(
        entry_kernel,
        in_specs=whole_blocks(2),
        out_specs=whole_blocks(chunks),
        out_shape=[jax.ShapeDtypeStruct((rows // chunks, width), jnp.bfloat16)] * chunks,
        cost_estimate=pl.CostEstimate(
            flops=8 * rows * width, bytes_accessed=4 * rows * width, transcendentals=rows
        ),
    )(source, gain)


def settings():
    return pltpu.CompilerParams(vmem_limit_bytes=56 * 1024 * 1024)


def whole_blocks(count):
    return [pl.BlockSpec(memory_space=pltpu.VMEM)] * count


def vision_pass(pieces, early, late, slope=None):
    rows = sum(p.shape[0] for p in pieces)
    units, width = early.shape
    size = min(256, units)
    blocks = -(-units // size)
    given = [] if slope is None else [slope]
    slopes = [jax.ShapeDtypeStruct((blocks, rows, size), jnp.float32)] * (1 - len(given))
    return pl.pallas_call(
        functools.partial(vision_kernel, len(pieces), slope is None),
        in_specs=whole_blocks(len(pieces))
        + [pl.BlockSpec(memory_space=pl.ANY)] * 2
        + whole_blocks(len(given)),
        out_specs=whole_blocks(2 + len(slopes)),
        out_shape=[jax.ShapeDtypeStruct((rows // 2, width), jnp.bfloat16)] * 2 + slopes,
        scratch_shapes=[
            pltpu.VMEM((blocks, size, width), jnp.bfloat16),
            pltpu.VMEM((blocks, size, width), jnp.bfloat16),
            pltpu.VMEM((rows, width), jnp.bfloat16),
            pltpu.VMEM((rows, size), jnp.float32),
            pltpu.VMEM((rows, blocks * size), jnp.bfloat16),
            pltpu.SemaphoreType.DMA((blocks,)),
            pltpu.SemaphoreType.DMA((blocks,)),
        ],
        compiler_params=settings(),
        cost_estimate=pl.CostEstimate(
            flops=4 * rows * width * units,
            bytes_accessed=4 * width * units + 4 * rows * (width + units),
            transcendentals=2 * rows * units,
        ),
    )(*pieces, early, late, *given)


def weight_cost(rows, depth, units):
    return pl.CostEstimate(
        flops=2 * rows * depth * units,
        bytes_accessed=2 * depth * units + 4 * rows * (depth + units),
        transcendentals=2 * rows * units,
    )


def project(pieces, weight, upstream):
    rows = sum(p.shape[0] for p in pieces)
    depth, units = weight.shape
    size = tile_of(depth, 1280)
    return pl.pallas_call(
        functools.partial(project_kernel, len(pieces)),
        in_specs=whole_blocks(len(pieces)) + [pl.BlockSpec(memory_space=pl.ANY)] + whole_blocks(1),
        out_specs=whole_blocks(2),
        out_shape=[jax.ShapeDtypeStruct((rows, units), jnp.bfloat16)] * 2,
        scratch_shapes=[
            pltpu.VMEM((depth // size, size, units), jnp.bfloat16),
            pltpu.VMEM((rows, depth), jnp.bfloat16),
            pltpu.VMEM((rows, units), jnp.float32),
            pltpu.SemaphoreType.DMA((depth // size,)),
        ],
        compiler_params=settings(),
        cost_estimate=weight_cost(rows, depth, units),
    )(*pieces, weight, upstream)


def project_back(delta, weight):
    rows = delta.shape[0]
    depth, units = weight.shape
    size = tile_of(depth, 1280)
    return pl.pallas_call(
        project_back_kernel,
        in_specs=whole_blocks(1) + [pl.BlockSpec(memory_space=pl.ANY)],
        out_specs=whole_blocks(2),
        out_shape=[jax.ShapeDtypeStruct((rows // 2, depth), jnp.bfloat16)] * 2,
        scratch_shapes=[
            pltpu.VMEM((depth // size, size, units), jnp.bfloat16),
            pltpu.SemaphoreType.DMA((depth // size,)),
        ],
        compiler_params=settings(),
        cost_estimate=weight_cost(rows, depth, units),
    )(delta, weight)


class Direct:
    def __init__(self):
        self.size = lax.axis_size("tp")
        self.places = self.size // cores
        rank = lax.axis_index("tp")
        place, core = rank // cores, rank % cores
        partner = (place ^ jnp.arange(self.places)) * cores
        self.ranks = jnp.concatenate([partner + core, partner + 1 - core])
        every = jnp.arange(self.size)
        self.blocks = (every + core) % cores * self.places + (every // cores ^ place)
        self.pairs = [(a, a + 1 - 2 * (a % cores)) for a in range(self.size)]

    def shift(self, block, k):
        pairs = [(a, (a // cores ^ k) * cores + a % cores) for a in range(self.size)]
        return lax.ppermute(block, "tp", pairs)

    def spread(self, block):
        return [block] + [self.shift(block, k) for k in range(1, self.places)]

    def gathered(self, mine):
        other = [lax.ppermute(m, "tp", self.pairs) for m in mine]
        if mine[0].shape[0] % 8:
            return [jnp.concatenate(mine + other, 0)]
        return mine + other

    def combine(self, near, far):
        rows = near.shape[0] // self.places
        got = lax.ppermute(far, "tp", self.pairs)
        both = near.astype(jnp.float32) + got.astype(jnp.float32)
        cut = [both[k * rows : (k + 1) * rows] for k in range(self.places)]
        return cut[:1] + [c.astype(jnp.bfloat16) for c in cut[1:]]

    def send(self, cut):
        return cut[:1] + [self.shift(cut[k], k) for k in range(1, self.places)]

    def summed(self, terms):
        return sum([t.astype(jnp.float32) for t in terms[1:]], terms[0])

    def by_rank(self, rows, size):
        return jnp.take(rows.reshape(size, -1, rows.shape[-1]), self.blocks, axis=0, mode="clip")

    def by_row(self, ranks):
        return jnp.take(ranks, self.ranks, axis=0, mode="clip").reshape(-1, ranks.shape[-1])


def per_device(
    vision_in,
    vis_gain,
    first_weight,
    second_weight,
    layer_scale,
    proj_gain,
    proj_weight,
    text_embed,
    dest_row,
    cotangent,
):
    moves = Direct()
    groups = lax.axis_size("grp")
    size = lax.axis_size("tp")
    grp_rank = lax.axis_index("grp")
    seq_len, width = text_embed.shape
    merged_total = dest_row.shape[0] // groups
    image_rows = merged_total // images
    own_rows, vis_width = vision_in.shape
    merged_width = proj_gain.shape[0]
    fold = merged_width // vis_width
    rows = own_rows // chunks
    merged_rows = rows // fold

    normed = list(entry_norm(vision_in, vis_gain))
    x = [vision_in[c * rows : (c + 1) * rows].astype(jnp.float32) for c in range(chunks)]

    tied = lax.optimization_barrier
    rail_b = moves.spread(normed[1])

    starts = dest_row.reshape(groups, images, image_rows)[:, :, 0]
    start_pos = starts % seq_len
    shift = starts[0] // seq_len
    matches = (shift[None, :] == jnp.arange(groups)[:, None]).astype(jnp.int32)
    image_of = jnp.sum(matches * jnp.arange(images), 1)
    used = jnp.sum(matches, 1) > 0
    source = (grp_rank - jnp.arange(groups)) % groups
    from_group = (source[:, None] == jnp.arange(groups)).astype(jnp.int32)
    spot = jnp.sum(matches[:, None, :] * from_group[:, :, None] * start_pos[None], (1, 2))

    span = jnp.arange(image_rows)
    picked = jnp.take(cotangent, (spot[:, None] + span).reshape(-1), axis=0, mode="clip")
    picked = [picked[s * image_rows : (s + 1) * image_rows] for s in range(groups)]
    for s in range(1, groups):
        pairs = [(g, (g - s) % groups) for g in range(groups)]
        picked[s] = lax.ppermute(picked[s], "grp", pairs)

    normed[0], rail_b, picked = tied((normed[0], rail_b, picked))
    rail_a = moves.spread(normed[0])
    patches_b = moves.gathered(rail_b)

    def grad_of(picked, c):
        returned = jnp.take(jnp.stack(picked), shift, axis=0, mode="clip").reshape(size, -1, width)
        return moves.by_row(returned[:, c * merged_rows : (c + 1) * merged_rows])

    def merge(c, summed):
        outputs = (x[c] + layer_scale * summed).astype(jnp.bfloat16)
        merged = outputs.reshape(merged_rows, merged_width).astype(jnp.float32)
        scaled, own_hat, own_inv = layer_norm(merged, proj_gain, proj_eps)
        return scaled.astype(jnp.bfloat16), own_hat, own_inv

    def unmerge(back_sum, own_hat, own_inv):
        merged_grad = norm_back(back_sum, proj_gain, own_hat, own_inv).astype(jnp.bfloat16)
        own_grad = merged_grad.reshape(rows, vis_width).astype(jnp.float32)
        return own_grad, (own_grad * layer_scale).astype(jnp.bfloat16)

    early, late = first_weight.T, second_weight
    near_b, far_b, slope_b = vision_pass(patches_b, early, late)
    near_b, far_b, rail_a = tied((near_b, far_b, rail_a))
    patches_a = moves.gathered(rail_a)
    terms_b = moves.send(moves.combine(near_b, far_b))
    near_a, far_a, slope_a = vision_pass(patches_a, early, late)
    near_a, terms_b, picked = tied((near_a, terms_b, picked))
    mixed_b, *stats_b = merge(1, moves.summed(terms_b))
    rail_b = moves.spread(mixed_b)
    near_a, mixed_b = tied((near_a, mixed_b))
    cut_a, upstream = tied(
        (moves.combine(near_a, far_a), [grad_of(picked, c) for c in range(chunks)])
    )
    terms_a = moves.send(cut_a)
    rail_b, terms_a[1] = tied((rail_b, terms_a[1]))
    merged_b = moves.gathered(rail_b)
    projected_b, delta_b = project(merged_b, proj_weight, upstream[1])
    projected_b, delta_b, terms_a = tied((projected_b, delta_b, terms_a))
    mixed_a, *stats_a = merge(0, moves.summed(terms_a))
    rail_a = moves.spread(mixed_a)
    delta_b, mixed_a = tied((delta_b, mixed_a))
    near_b, far_b = project_back(delta_b, proj_weight)
    near_b, far_b, rail_a = tied((near_b, far_b, rail_a))
    terms_b = moves.send(moves.combine(near_b, far_b))
    merged_a = moves.gathered(rail_a)
    projected_a, delta_a = project(merged_a, proj_weight, upstream[0])
    projected_a, delta_a, terms_b = tied((projected_a, delta_a, terms_b))
    own_b, scaled_b = unmerge(moves.summed(terms_b), *stats_b)
    rail_b = moves.spread(scaled_b)
    delta_a, scaled_b = tied((delta_a, scaled_b))
    near_a, far_a = project_back(delta_a, proj_weight)
    near_a, far_a, rail_b = tied((near_a, far_a, rail_b))
    terms_a = moves.send(moves.combine(near_a, far_a))
    grad_out_b = moves.gathered(rail_b)
    near_b, far_b = vision_pass(grad_out_b, late, early, slope_b)
    near_b, terms_a, projected_a, projected_b = tied((near_b, terms_a, projected_a, projected_b))
    own_a, scaled_a = unmerge(moves.summed(terms_a), *stats_a)
    rail_a = moves.spread(scaled_a)
    near_b, scaled_a, projected_a, projected_b = tied((near_b, scaled_a, projected_a, projected_b))
    cut_b = moves.combine(near_b, far_b)

    projected = jnp.concatenate(
        [moves.by_rank(projected_a, size), moves.by_rank(projected_b, size)], 1
    ).reshape(images, image_rows, width)
    chosen = jnp.take(projected, image_of, axis=0, mode="clip")
    arrived = [chosen[s] for s in range(groups)]
    for s in range(1, groups):
        pairs = [(g, (g + s) % groups) for g in range(groups)]
        arrived[s] = lax.ppermute(arrived[s], "grp", pairs)

    def embed(text, arrived):
        goes_to = jnp.where(used[:, None], spot[:, None] + span, seq_len).reshape(-1)
        picks = jnp.arange(seq_len)[:, None] == goes_to[None, :]
        placed = jnp.dot(
            picks.astype(jnp.bfloat16),
            jnp.concatenate(arrived, 0),
            preferred_element_type=jnp.float32,
        ).astype(jnp.bfloat16)
        return jnp.where(jnp.any(picks, 1, keepdims=True), placed, text)

    cut_b, rail_a, arrived = tied((cut_b, rail_a, arrived))
    terms_b = moves.send(cut_b)
    grad_out_a = moves.gathered(rail_a)
    near_a, far_a = vision_pass(grad_out_a, late, early, slope_a)
    near_a, terms_b, arrived = tied((near_a, terms_b, arrived))
    terms_a = moves.send(moves.combine(near_a, far_a))
    normed_b = moves.summed(terms_b)
    terms_a, seq_embed, normed_b = tied((terms_a, embed(text_embed, arrived), normed_b))
    normed_a = moves.summed(terms_a)
    parts = [layer_norm(x[c], vis_gain, vis_eps) for c in range(chunks)]
    grads = [
        own_a + norm_back(normed_a, vis_gain, parts[0][1], parts[0][2]),
        own_b + norm_back(normed_b, vis_gain, parts[1][1], parts[1][2]),
    ]
    grad_vision = jnp.concatenate(grads, 0).astype(jnp.bfloat16)
    return (seq_embed, grad_vision)


def solution(mesh):
    placed = (
        P(("grp", "tp"), None),
        P(),
        P(None, "tp"),
        P("tp", None),
        P(),
        P(),
        P(None, "tp"),
        P("grp", "tp"),
        P(),
        P("grp", "tp"),
    )
    return jax.shard_map(
        per_device,
        mesh=mesh,
        in_specs=placed,
        out_specs=(P("grp", "tp"), P(("grp", "tp"), None)),
        check_vma=False,
    )
```

```python
import functools

import jax
import jax.numpy as jnp
from jax import lax
from jax.experimental import pallas as pl
from jax.experimental.pallas import tpu as pltpu
from jax.sharding import PartitionSpec as P

vis_eps = 1e-06
proj_eps = 1e-05
chunks = 2
images = 4
cores = 2


def layer_norm(values, scale_vec, epsilon):
    mean_val = jnp.mean(values, -1, keepdims=True)
    centred = values - mean_val
    inv_std = lax.rsqrt(jnp.mean(centred * centred, -1, keepdims=True) + epsilon)
    normed = centred * inv_std
    return (normed * scale_vec, normed, inv_std)


def norm_back(upstream, scale_vec, normed, inv_std):
    scaled = upstream * scale_vec
    return inv_std * (
        scaled
        - jnp.mean(scaled, -1, keepdims=True)
        - normed * jnp.mean(scaled * normed, -1, keepdims=True)
    )


def times_transposed(left, right):
    return lax.dot_general(
        left, right, (((1,), (1,)), ((), ())), preferred_element_type=jnp.float32
    )


def tile_of(length, most):
    return max(t for t in range(128, most + 1, 128) if length % t == 0)


def laid(pieces):
    if len(pieces) == 1:
        return pieces[0][...]
    if pieces[0].shape[0] % 16 == 0:
        return jnp.concatenate([p[...] for p in pieces], 0)
    return jnp.concatenate([p[...].astype(jnp.float32) for p in pieces], 0).astype(jnp.bfloat16)


def each_rows(total, body):
    step = 32 if total % 32 == 0 else total

    def run(i, _):
        body(pl.ds(pl.multiple_of(i * step, step), step))
        return 0

    lax.fori_loop(0, total // step, run, 0)


def block_start(total, rows, j):
    return pl.multiple_of(jnp.minimum(j * rows, total - rows), 16)


def fetch(source, held, sems, j):
    count, rows = held.shape[:2]

    @pl.when(j < count)
    def _():
        part = source.at[pl.ds(block_start(source.shape[0], rows, j), rows)]
        pltpu.make_async_copy(part, held.at[j], sems.at[j]).start()


def arrive(source, held, sems, j):
    rows = held.shape[1]
    pltpu.make_async_copy(source.at[pl.ds(0, rows)], held.at[j], sems.at[j]).wait()


def vision_kernel(count, ahead, *refs):
    pieces = refs[:count]
    if ahead:
        early, late, near, far, slope = refs[count : count + 5]
    else:
        early, late, slope, near, far = refs[count : count + 5]
    first, second, rows, pre, hidden, first_sems, second_sems = refs[count + 5 :]
    blocks, size, width = first.shape
    for j in range(blocks):
        fetch(early, first, first_sems, j)
    rows[...] = laid(pieces)

    def block(j, _):
        arrive(early, first, first_sems, j)
        fetch(late, second, second_sems, j)
        pre[...] = times_transposed(rows[...], first[j])
        repeated = j * size - jnp.minimum(j * size, early.shape[0] - size)
        place = pl.ds(pl.multiple_of(j * size, min(size, 128)), size)

        def act(sel):
            u = pre[sel, :]
            if ahead:
                fresh = lax.broadcasted_iota(jnp.int32, u.shape, 1) >= repeated
                cumul = 0.5 * (1.0 + lax.erf(u * 0.7071067811865476))
                dense = jnp.exp(-0.5 * u * u) * 0.3989422804014327
                hidden[sel, place] = jnp.where(fresh, u * cumul, 0.0).astype(jnp.bfloat16)
                slope[j, sel, :] = jnp.where(fresh, cumul + u * dense, 0.0)
            else:
                hidden[sel, place] = (u * slope[j, sel, :]).astype(jnp.bfloat16)

        each_rows(pre.shape[0], act)
        return 0

    lax.fori_loop(0, blocks, block, 0)
    for j in range(blocks):
        arrive(late, second, second_sems, j)
    half = near.shape[0]
    tile = min(1280, width)
    for k in range(0, width, tile):
        span = slice(k, min(k + tile, width))
        held = second[:, :, span]
        both = jnp.dot(
            hidden[...],
            held.reshape(blocks * size, held.shape[2]),
            preferred_element_type=jnp.float32,
        ).astype(jnp.bfloat16)
        near[:, span] = both[:half]
        far[:, span] = both[half:]


def project_kernel(count, *refs):
    pieces = refs[:count]
    weight, upstream, projected, delta, held, rows, pre, sems = refs[count:]
    for j in range(3):
        fetch(weight, held, sems, j)
    rows[...] = laid(pieces)
    pre[...] = jnp.zeros_like(pre)
    chunk = held.shape[1]

    def ahead(j, _):
        arrive(weight, held, sems, j)
        fetch(weight, held, sems, j + 3)
        sel = pl.ds(pl.multiple_of(j * chunk, 128), chunk)
        pre[...] += jnp.dot(rows[:, sel], held[j], preferred_element_type=jnp.float32)
        return 0

    lax.fori_loop(0, held.shape[0], ahead, 0)

    def act(sel):
        u = pre[sel, :]
        cumul = 0.5 * (1.0 + lax.erf(u * 0.7071067811865476))
        dense = jnp.exp(-0.5 * u * u) * 0.3989422804014327
        projected[sel, :] = (u * cumul).astype(jnp.bfloat16)
        grad = upstream[sel, :].astype(jnp.float32)
        delta[sel, :] = (grad * (cumul + u * dense)).astype(jnp.bfloat16)

    each_rows(pre.shape[0], act)


def project_back_kernel(delta, weight, near, far, held, sems):
    for j in range(3):
        fetch(weight, held, sems, j)
    chunk = held.shape[1]
    half = near.shape[0]

    def behind(j, _):
        arrive(weight, held, sems, j)
        fetch(weight, held, sems, j + 3)
        sel = pl.ds(pl.multiple_of(j * chunk, 128), chunk)
        back = times_transposed(delta[...], held[j]).astype(jnp.bfloat16)
        near[:, sel] = back[:half]
        far[:, sel] = back[half:]
        return 0

    lax.fori_loop(0, held.shape[0], behind, 0)


def entry_kernel(source, gain, *normed):
    rows = normed[0].shape[0]
    for c, out in enumerate(normed):
        values = source[c * rows : (c + 1) * rows].astype(jnp.float32)
        out[...] = layer_norm(values, gain[...][None, :], vis_eps)[0].astype(jnp.bfloat16)


def entry_norm(source, gain):
    rows, width = source.shape
    return pl.pallas_call(
        entry_kernel,
        in_specs=whole_blocks(2),
        out_specs=whole_blocks(chunks),
        out_shape=[jax.ShapeDtypeStruct((rows // chunks, width), jnp.bfloat16)] * chunks,
        cost_estimate=pl.CostEstimate(
            flops=8 * rows * width, bytes_accessed=4 * rows * width, transcendentals=rows
        ),
    )(source, gain)


def settings(limit):
    return pltpu.CompilerParams(vmem_limit_bytes=limit * 1024 * 1024)


def whole_blocks(count):
    return [pl.BlockSpec(memory_space=pltpu.VMEM)] * count


def vision_pass(pieces, early, late, slope=None):
    rows = sum(p.shape[0] for p in pieces)
    units, width = early.shape
    size = min(256, units)
    blocks = -(-units // size)
    given = [] if slope is None else [slope]
    slopes = [jax.ShapeDtypeStruct((blocks, rows, size), jnp.float32)] * (1 - len(given))
    return pl.pallas_call(
        functools.partial(vision_kernel, len(pieces), slope is None),
        in_specs=whole_blocks(len(pieces))
        + [pl.BlockSpec(memory_space=pl.ANY)] * 2
        + whole_blocks(len(given)),
        out_specs=whole_blocks(2 + len(slopes)),
        out_shape=[jax.ShapeDtypeStruct((rows // 2, width), jnp.bfloat16)] * 2 + slopes,
        scratch_shapes=[
            pltpu.VMEM((blocks, size, width), jnp.bfloat16),
            pltpu.VMEM((blocks, size, width), jnp.bfloat16),
            pltpu.VMEM((rows, width), jnp.bfloat16),
            pltpu.VMEM((rows, size), jnp.float32),
            pltpu.VMEM((rows, blocks * size), jnp.bfloat16),
            pltpu.SemaphoreType.DMA((blocks,)),
            pltpu.SemaphoreType.DMA((blocks,)),
        ],
        compiler_params=settings(56),
        cost_estimate=pl.CostEstimate(
            flops=4 * rows * width * units,
            bytes_accessed=4 * width * units + 4 * rows * (width + units),
            transcendentals=2 * rows * units,
        ),
    )(*pieces, early, late, *given)


def weight_cost(rows, depth, units):
    return pl.CostEstimate(
        flops=2 * rows * depth * units,
        bytes_accessed=2 * depth * units + 4 * rows * (depth + units),
        transcendentals=2 * rows * units,
    )


def project(pieces, weight, upstream):
    rows = sum(p.shape[0] for p in pieces)
    depth, units = weight.shape
    size = tile_of(depth, 1280)
    return pl.pallas_call(
        functools.partial(project_kernel, len(pieces)),
        in_specs=whole_blocks(len(pieces)) + [pl.BlockSpec(memory_space=pl.ANY)] + whole_blocks(1),
        out_specs=whole_blocks(2),
        out_shape=[jax.ShapeDtypeStruct((rows, units), jnp.bfloat16)] * 2,
        scratch_shapes=[
            pltpu.VMEM((depth // size, size, units), jnp.bfloat16),
            pltpu.VMEM((rows, depth), jnp.bfloat16),
            pltpu.VMEM((rows, units), jnp.float32),
            pltpu.SemaphoreType.DMA((depth // size,)),
        ],
        compiler_params=settings(40),
        cost_estimate=weight_cost(rows, depth, units),
    )(*pieces, weight, upstream)


def project_back(delta, weight):
    rows = delta.shape[0]
    depth, units = weight.shape
    size = tile_of(depth, 1280)
    return pl.pallas_call(
        project_back_kernel,
        in_specs=whole_blocks(1) + [pl.BlockSpec(memory_space=pl.ANY)],
        out_specs=whole_blocks(2),
        out_shape=[jax.ShapeDtypeStruct((rows // 2, depth), jnp.bfloat16)] * 2,
        scratch_shapes=[
            pltpu.VMEM((depth // size, size, units), jnp.bfloat16),
            pltpu.SemaphoreType.DMA((depth // size,)),
        ],
        compiler_params=settings(40),
        cost_estimate=weight_cost(rows, depth, units),
    )(delta, weight)


class Direct:
    def __init__(self):
        self.size = lax.axis_size("tp")
        self.places = self.size // cores
        rank = lax.axis_index("tp")
        place, core = rank // cores, rank % cores
        self.partners = [0, *range(2, self.places), *range(1, min(2, self.places))]
        partner = (place ^ jnp.array(self.partners)) * cores
        self.ranks = jnp.concatenate([partner + core, partner + 1 - core])
        every = jnp.arange(self.size)
        block = jnp.array([self.partners.index(k) for k in range(self.places)])
        self.blocks = (every + core) % cores * self.places + block[every // cores ^ place]
        self.pairs = [(a, a + 1 - 2 * (a % cores)) for a in range(self.size)]

    def shift(self, block, k):
        pairs = [(a, (a // cores ^ k) * cores + a % cores) for a in range(self.size)]
        return lax.ppermute(block, "tp", pairs)

    def spread(self, block):
        return [block] + [self.shift(block, k) for k in self.partners[1:]]

    def gathered(self, mine):
        other = [lax.ppermute(m, "tp", self.pairs) for m in mine]
        if mine[0].shape[0] % 8:
            return [jnp.concatenate(mine + other, 0)]
        return mine + other

    def combine(self, near, far):
        rows = near.shape[0] // self.places
        got = lax.ppermute(far, "tp", self.pairs)
        both = near.astype(jnp.float32) + got.astype(jnp.float32)
        cut = [both[k * rows : (k + 1) * rows] for k in range(self.places)]
        return cut[:1] + [c.astype(jnp.bfloat16) for c in cut[1:]]

    def send(self, cut):
        return cut[:1] + [self.shift(c, k) for c, k in zip(cut[1:], self.partners[1:])]

    def summed(self, terms):
        return sum([t.astype(jnp.float32) for t in terms[1:]], terms[0])

    def by_rank(self, rows, size):
        return jnp.take(rows.reshape(size, -1, rows.shape[-1]), self.blocks, axis=0, mode="clip")

    def by_row(self, ranks):
        return jnp.take(ranks, self.ranks, axis=0, mode="clip").reshape(-1, ranks.shape[-1])


def per_device(
    vision_in,
    vis_gain,
    first_weight,
    second_weight,
    layer_scale,
    proj_gain,
    proj_weight,
    text_embed,
    dest_row,
    cotangent,
):
    moves = Direct()
    groups = lax.axis_size("grp")
    size = lax.axis_size("tp")
    grp_rank = lax.axis_index("grp")
    seq_len, width = text_embed.shape
    merged_total = dest_row.shape[0] // groups
    image_rows = merged_total // images
    own_rows, vis_width = vision_in.shape
    merged_width = proj_gain.shape[0]
    fold = merged_width // vis_width
    rows = own_rows // chunks
    merged_rows = rows // fold

    normed = list(entry_norm(vision_in, vis_gain))
    x = [vision_in[c * rows : (c + 1) * rows].astype(jnp.float32) for c in range(chunks)]

    tied = lax.optimization_barrier
    rail_b = moves.spread(normed[1])

    starts = dest_row.reshape(groups, images, image_rows)[:, :, 0]
    start_pos = starts % seq_len
    shift = starts[0] // seq_len
    matches = (shift[None, :] == jnp.arange(groups)[:, None]).astype(jnp.int32)
    image_of = jnp.sum(matches * jnp.arange(images), 1)
    used = jnp.sum(matches, 1) > 0
    source = (grp_rank - jnp.arange(groups)) % groups
    from_group = (source[:, None] == jnp.arange(groups)).astype(jnp.int32)
    spot = jnp.sum(matches[:, None, :] * from_group[:, :, None] * start_pos[None], (1, 2))

    span = jnp.arange(image_rows)
    picked = jnp.take(cotangent, (spot[:, None] + span).reshape(-1), axis=0, mode="clip")
    picked = [picked[s * image_rows : (s + 1) * image_rows] for s in range(groups)]
    for s in range(1, groups):
        pairs = [(g, (g - s) % groups) for g in range(groups)]
        picked[s] = lax.ppermute(picked[s], "grp", pairs)

    normed[0], rail_b, picked = tied((normed[0], rail_b, picked))
    rail_a = moves.spread(normed[0])
    patches_b = moves.gathered(rail_b)

    def grad_of(picked, c):
        returned = jnp.take(jnp.stack(picked), shift, axis=0, mode="clip").reshape(size, -1, width)
        return moves.by_row(returned[:, c * merged_rows : (c + 1) * merged_rows])

    def merge(c, summed):
        outputs = (x[c] + layer_scale * summed).astype(jnp.bfloat16)
        merged = outputs.reshape(merged_rows, merged_width).astype(jnp.float32)
        scaled, own_hat, own_inv = layer_norm(merged, proj_gain, proj_eps)
        return scaled.astype(jnp.bfloat16), own_hat, own_inv

    def unmerge(back_sum, own_hat, own_inv):
        merged_grad = norm_back(back_sum, proj_gain, own_hat, own_inv).astype(jnp.bfloat16)
        own_grad = merged_grad.reshape(rows, vis_width).astype(jnp.float32)
        return own_grad, (own_grad * layer_scale).astype(jnp.bfloat16)

    early, late = first_weight.T, second_weight
    near_b, far_b, slope_b = vision_pass(patches_b, early, late)
    near_b, far_b, rail_a = tied((near_b, far_b, rail_a))
    patches_a = moves.gathered(rail_a)
    terms_b = moves.send(moves.combine(near_b, far_b))
    near_a, far_a, slope_a = vision_pass(patches_a, early, late)
    near_a, terms_b, picked = tied((near_a, terms_b, picked))
    mixed_b, *stats_b = merge(1, moves.summed(terms_b))
    rail_b = moves.spread(mixed_b)
    near_a, mixed_b = tied((near_a, mixed_b))
    cut_a, upstream = tied(
        (moves.combine(near_a, far_a), [grad_of(picked, c) for c in range(chunks)])
    )
    terms_a = moves.send(cut_a)
    rail_b, terms_a[-1] = tied((rail_b, terms_a[-1]))
    merged_b = moves.gathered(rail_b)
    projected_b, delta_b = project(merged_b, proj_weight, upstream[1])
    projected_b, delta_b, terms_a = tied((projected_b, delta_b, terms_a))
    mixed_a, *stats_a = merge(0, moves.summed(terms_a))
    rail_a = moves.spread(mixed_a)
    delta_b, mixed_a = tied((delta_b, mixed_a))
    near_b, far_b = project_back(delta_b, proj_weight)
    near_b, far_b, rail_a = tied((near_b, far_b, rail_a))
    terms_b = moves.send(moves.combine(near_b, far_b))
    merged_a = moves.gathered(rail_a)
    projected_a, delta_a = project(merged_a, proj_weight, upstream[0])
    projected_a, delta_a, terms_b = tied((projected_a, delta_a, terms_b))
    own_b, scaled_b = unmerge(moves.summed(terms_b), *stats_b)
    rail_b = moves.spread(scaled_b)
    delta_a, scaled_b = tied((delta_a, scaled_b))
    near_a, far_a = project_back(delta_a, proj_weight)
    near_a, far_a, rail_b = tied((near_a, far_a, rail_b))
    terms_a = moves.send(moves.combine(near_a, far_a))
    grad_out_b = moves.gathered(rail_b)
    near_b, far_b = vision_pass(grad_out_b, late, early, slope_b)
    near_b, terms_a, projected_a, projected_b = tied((near_b, terms_a, projected_a, projected_b))
    own_a, scaled_a = unmerge(moves.summed(terms_a), *stats_a)
    rail_a = moves.spread(scaled_a)
    near_b, scaled_a, projected_a, projected_b = tied((near_b, scaled_a, projected_a, projected_b))
    cut_b = moves.combine(near_b, far_b)

    projected = jnp.concatenate(
        [moves.by_rank(projected_a, size), moves.by_rank(projected_b, size)], 1
    ).reshape(images, image_rows, width)
    chosen = jnp.take(projected, image_of, axis=0, mode="clip")
    arrived = [chosen[s] for s in range(groups)]
    for s in range(1, groups):
        pairs = [(g, (g + s) % groups) for g in range(groups)]
        arrived[s] = lax.ppermute(arrived[s], "grp", pairs)

    def embed(text, arrived):
        goes_to = jnp.where(used[:, None], spot[:, None] + span, seq_len).reshape(-1)
        picks = jnp.arange(seq_len)[:, None] == goes_to[None, :]
        placed = jnp.dot(
            picks.astype(jnp.bfloat16),
            jnp.concatenate(arrived, 0),
            preferred_element_type=jnp.float32,
        ).astype(jnp.bfloat16)
        return jnp.where(jnp.any(picks, 1, keepdims=True), placed, text)

    cut_b, arrived = tied((cut_b, arrived))
    terms_b = moves.send(cut_b)
    rail_a, terms_b[-1] = tied((rail_a, terms_b[-1]))
    grad_out_a = moves.gathered(rail_a)
    near_a, far_a = vision_pass(grad_out_a, late, early, slope_a)
    near_a, terms_b, arrived = tied((near_a, terms_b, arrived))
    terms_a = moves.send(moves.combine(near_a, far_a))
    normed_b = moves.summed(terms_b)
    terms_a, seq_embed, normed_b = tied((terms_a, embed(text_embed, arrived), normed_b))
    normed_a = moves.summed(terms_a)
    parts = [layer_norm(x[c], vis_gain, vis_eps) for c in range(chunks)]
    grads = [
        own_a + norm_back(normed_a, vis_gain, parts[0][1], parts[0][2]),
        own_b + norm_back(normed_b, vis_gain, parts[1][1], parts[1][2]),
    ]
    grad_vision = jnp.concatenate(grads, 0).astype(jnp.bfloat16)
    return (seq_embed, grad_vision)


def solution(mesh):
    placed = (
        P(("grp", "tp"), None),
        P(),
        P(None, "tp"),
        P("tp", None),
        P(),
        P(),
        P(None, "tp"),
        P("grp", "tp"),
        P(),
        P("grp", "tp"),
    )
    return jax.shard_map(
        per_device,
        mesh=mesh,
        in_specs=placed,
        out_specs=(P("grp", "tp"), P(("grp", "tp"), None)),
        check_vma=False,
    )
```

```python
import functools

import jax
import jax.numpy as jnp
from jax import lax
from jax.experimental import pallas as pl
from jax.experimental.pallas import tpu as pltpu
from jax.sharding import PartitionSpec as P

vis_eps = 1e-06
proj_eps = 1e-05
chunks = 2
images = 4
cores = 2


def layer_norm(values, scale_vec, epsilon):
    mean_val = jnp.mean(values, -1, keepdims=True)
    centred = values - mean_val
    inv_std = lax.rsqrt(jnp.mean(centred * centred, -1, keepdims=True) + epsilon)
    normed = centred * inv_std
    return (normed * scale_vec, normed, inv_std)


def norm_back(upstream, scale_vec, normed, inv_std):
    scaled = upstream * scale_vec
    return inv_std * (
        scaled
        - jnp.mean(scaled, -1, keepdims=True)
        - normed * jnp.mean(scaled * normed, -1, keepdims=True)
    )


def times_transposed(left, right):
    return lax.dot_general(
        left, right, (((1,), (1,)), ((), ())), preferred_element_type=jnp.float32
    )


def tile_of(length, most):
    return max(t for t in range(128, most + 1, 128) if length % t == 0)


def laid(pieces):
    if len(pieces) == 1:
        return pieces[0][...]
    if pieces[0].shape[0] % 16 == 0:
        return jnp.concatenate([p[...] for p in pieces], 0)
    return jnp.concatenate([p[...].astype(jnp.float32) for p in pieces], 0).astype(jnp.bfloat16)


def each_rows(total, body):
    step = 32 if total % 32 == 0 else total

    def run(i, _):
        body(pl.ds(pl.multiple_of(i * step, step), step))
        return 0

    lax.fori_loop(0, total // step, run, 0)


def block_start(total, rows, j):
    return pl.multiple_of(jnp.minimum(j * rows, total - rows), 16)


def fetch(source, held, sems, j):
    count, rows = held.shape[:2]

    @pl.when(j < count)
    def _():
        part = source.at[pl.ds(block_start(source.shape[0], rows, j), rows)]
        pltpu.make_async_copy(part, held.at[j], sems.at[j]).start()


def arrive(source, held, sems, j):
    rows = held.shape[1]
    pltpu.make_async_copy(source.at[pl.ds(0, rows)], held.at[j], sems.at[j]).wait()


def vision_kernel(count, ahead, *refs):
    pieces = refs[:count]
    if ahead:
        early, late, near, far, slope = refs[count : count + 5]
    else:
        early, late, slope, near, far = refs[count : count + 5]
    first, second, rows, pre, hidden, first_sems, second_sems = refs[count + 5 :]
    blocks, size, width = first.shape
    for j in range(blocks):
        fetch(early, first, first_sems, j)
    rows[...] = laid(pieces)

    def block(j, _):
        arrive(early, first, first_sems, j)
        fetch(late, second, second_sems, j)
        pre[...] = times_transposed(rows[...], first[j])
        repeated = j * size - jnp.minimum(j * size, early.shape[0] - size)
        place = pl.ds(pl.multiple_of(j * size, min(size, 128)), size)

        def act(sel):
            u = pre[sel, :]
            if ahead:
                fresh = lax.broadcasted_iota(jnp.int32, u.shape, 1) >= repeated
                cumul = 0.5 * (1.0 + lax.erf(u * 0.7071067811865476))
                dense = jnp.exp(-0.5 * u * u) * 0.3989422804014327
                hidden[sel, place] = jnp.where(fresh, u * cumul, 0.0).astype(jnp.bfloat16)
                slope[j, sel, :] = jnp.where(fresh, cumul + u * dense, 0.0)
            else:
                hidden[sel, place] = (u * slope[j, sel, :]).astype(jnp.bfloat16)

        each_rows(pre.shape[0], act)
        return 0

    lax.fori_loop(0, blocks, block, 0)
    for j in range(blocks):
        arrive(late, second, second_sems, j)
    half = near.shape[0]
    tile = min(1280, width)
    for k in range(0, width, tile):
        span = slice(k, min(k + tile, width))
        held = second[:, :, span]
        both = jnp.dot(
            hidden[...],
            held.reshape(blocks * size, held.shape[2]),
            preferred_element_type=jnp.float32,
        ).astype(jnp.bfloat16)
        near[:, span] = both[:half]
        far[:, span] = both[half:]


def project_kernel(count, *refs):
    pieces = refs[:count]
    weight, upstream, projected, delta, held, rows, pre, sems = refs[count:]
    for j in range(3):
        fetch(weight, held, sems, j)
    rows[...] = laid(pieces)
    pre[...] = jnp.zeros_like(pre)
    chunk = held.shape[1]

    def ahead(j, _):
        arrive(weight, held, sems, j)
        fetch(weight, held, sems, j + 3)
        sel = pl.ds(pl.multiple_of(j * chunk, 128), chunk)
        pre[...] += jnp.dot(rows[:, sel], held[j], preferred_element_type=jnp.float32)
        return 0

    lax.fori_loop(0, held.shape[0], ahead, 0)

    def act(sel):
        u = pre[sel, :]
        cumul = 0.5 * (1.0 + lax.erf(u * 0.7071067811865476))
        dense = jnp.exp(-0.5 * u * u) * 0.3989422804014327
        projected[sel, :] = (u * cumul).astype(jnp.bfloat16)
        grad = upstream[sel, :].astype(jnp.float32)
        delta[sel, :] = (grad * (cumul + u * dense)).astype(jnp.bfloat16)

    each_rows(pre.shape[0], act)


def project_back_kernel(delta, weight, near, far, held, sems):
    for j in range(3):
        fetch(weight, held, sems, j)
    chunk = held.shape[1]
    half = near.shape[0]

    def behind(j, _):
        arrive(weight, held, sems, j)
        fetch(weight, held, sems, j + 3)
        sel = pl.ds(pl.multiple_of(j * chunk, 128), chunk)
        back = times_transposed(delta[...], held[j]).astype(jnp.bfloat16)
        near[:, sel] = back[:half]
        far[:, sel] = back[half:]
        return 0

    lax.fori_loop(0, held.shape[0], behind, 0)


def entry_kernel(source, gain, *normed):
    rows = normed[0].shape[0]
    for c, out in enumerate(normed):
        values = source[c * rows : (c + 1) * rows].astype(jnp.float32)
        out[...] = layer_norm(values, gain[...][None, :], vis_eps)[0].astype(jnp.bfloat16)


def entry_norm(source, gain):
    rows, width = source.shape
    return pl.pallas_call(
        entry_kernel,
        in_specs=whole_blocks(2),
        out_specs=whole_blocks(chunks),
        out_shape=[jax.ShapeDtypeStruct((rows // chunks, width), jnp.bfloat16)] * chunks,
        cost_estimate=pl.CostEstimate(
            flops=8 * rows * width, bytes_accessed=4 * rows * width, transcendentals=rows
        ),
    )(source, gain)


def settings(limit):
    return pltpu.CompilerParams(vmem_limit_bytes=limit * 1024 * 1024)


def whole_blocks(count):
    return [pl.BlockSpec(memory_space=pltpu.VMEM)] * count


def vision_pass(pieces, early, late, slope=None):
    rows = sum(p.shape[0] for p in pieces)
    units, width = early.shape
    size = min(256, units)
    blocks = -(-units // size)
    given = [] if slope is None else [slope]
    slopes = [jax.ShapeDtypeStruct((blocks, rows, size), jnp.float32)] * (1 - len(given))
    return pl.pallas_call(
        functools.partial(vision_kernel, len(pieces), slope is None),
        in_specs=whole_blocks(len(pieces))
        + [pl.BlockSpec(memory_space=pl.ANY)] * 2
        + whole_blocks(len(given)),
        out_specs=whole_blocks(2 + len(slopes)),
        out_shape=[jax.ShapeDtypeStruct((rows // 2, width), jnp.bfloat16)] * 2 + slopes,
        scratch_shapes=[
            pltpu.VMEM((blocks, size, width), jnp.bfloat16),
            pltpu.VMEM((blocks, size, width), jnp.bfloat16),
            pltpu.VMEM((rows, width), jnp.bfloat16),
            pltpu.VMEM((rows, size), jnp.float32),
            pltpu.VMEM((rows, blocks * size), jnp.bfloat16),
            pltpu.SemaphoreType.DMA((blocks,)),
            pltpu.SemaphoreType.DMA((blocks,)),
        ],
        compiler_params=settings(53),
        cost_estimate=pl.CostEstimate(
            flops=4 * rows * width * units,
            bytes_accessed=4 * width * units + 4 * rows * (width + units),
            transcendentals=2 * rows * units,
        ),
    )(*pieces, early, late, *given)


def weight_cost(rows, depth, units):
    return pl.CostEstimate(
        flops=2 * rows * depth * units,
        bytes_accessed=2 * depth * units + 4 * rows * (depth + units),
        transcendentals=2 * rows * units,
    )


def project(pieces, weight, upstream):
    rows = sum(p.shape[0] for p in pieces)
    depth, units = weight.shape
    size = tile_of(depth, 1280)
    return pl.pallas_call(
        functools.partial(project_kernel, len(pieces)),
        in_specs=whole_blocks(len(pieces)) + [pl.BlockSpec(memory_space=pl.ANY)] + whole_blocks(1),
        out_specs=whole_blocks(2),
        out_shape=[jax.ShapeDtypeStruct((rows, units), jnp.bfloat16)] * 2,
        scratch_shapes=[
            pltpu.VMEM((depth // size, size, units), jnp.bfloat16),
            pltpu.VMEM((rows, depth), jnp.bfloat16),
            pltpu.VMEM((rows, units), jnp.float32),
            pltpu.SemaphoreType.DMA((depth // size,)),
        ],
        compiler_params=settings(40),
        cost_estimate=weight_cost(rows, depth, units),
    )(*pieces, weight, upstream)


def project_back(delta, weight):
    rows = delta.shape[0]
    depth, units = weight.shape
    size = tile_of(depth, 1280)
    return pl.pallas_call(
        project_back_kernel,
        in_specs=whole_blocks(1) + [pl.BlockSpec(memory_space=pl.ANY)],
        out_specs=whole_blocks(2),
        out_shape=[jax.ShapeDtypeStruct((rows // 2, depth), jnp.bfloat16)] * 2,
        scratch_shapes=[
            pltpu.VMEM((depth // size, size, units), jnp.bfloat16),
            pltpu.SemaphoreType.DMA((depth // size,)),
        ],
        compiler_params=settings(40),
        cost_estimate=weight_cost(rows, depth, units),
    )(delta, weight)


class Direct:
    def __init__(self):
        self.size = lax.axis_size("tp")
        self.places = self.size // cores
        rank = lax.axis_index("tp")
        place, core = rank // cores, rank % cores
        self.partners = [0, *range(2, self.places), *range(1, min(2, self.places))]
        partner = (place ^ jnp.array(self.partners)) * cores
        self.ranks = jnp.concatenate([partner + core, partner + 1 - core])
        every = jnp.arange(self.size)
        block = jnp.array([self.partners.index(k) for k in range(self.places)])
        self.blocks = (every + core) % cores * self.places + block[every // cores ^ place]
        self.pairs = [(a, a + 1 - 2 * (a % cores)) for a in range(self.size)]

    def shift(self, block, k):
        pairs = [(a, (a // cores ^ k) * cores + a % cores) for a in range(self.size)]
        return lax.ppermute(block, "tp", pairs)

    def spread(self, block):
        return [block] + [self.shift(block, k) for k in self.partners[1:]]

    def gathered(self, mine):
        other = [lax.ppermute(m, "tp", self.pairs) for m in mine]
        if mine[0].shape[0] % 8:
            return [jnp.concatenate(mine + other, 0)]
        return mine + other

    def combine(self, near, far):
        rows = near.shape[0] // self.places
        got = lax.ppermute(far, "tp", self.pairs)
        both = near.astype(jnp.float32) + got.astype(jnp.float32)
        cut = [both[k * rows : (k + 1) * rows] for k in range(self.places)]
        return cut[:1] + [c.astype(jnp.bfloat16) for c in cut[1:]]

    def send(self, cut):
        return cut[:1] + [self.shift(c, k) for c, k in zip(cut[1:], self.partners[1:])]

    def summed(self, terms):
        return sum([t.astype(jnp.float32) for t in terms[1:]], terms[0])

    def by_rank(self, rows, size):
        return jnp.take(rows.reshape(size, -1, rows.shape[-1]), self.blocks, axis=0, mode="clip")

    def by_row(self, ranks):
        return jnp.take(ranks, self.ranks, axis=0, mode="clip").reshape(-1, ranks.shape[-1])


def per_device(
    vision_in,
    vis_gain,
    first_weight,
    second_weight,
    layer_scale,
    proj_gain,
    proj_weight,
    text_embed,
    dest_row,
    cotangent,
):
    moves = Direct()
    groups = lax.axis_size("grp")
    size = lax.axis_size("tp")
    grp_rank = lax.axis_index("grp")
    seq_len, width = text_embed.shape
    merged_total = dest_row.shape[0] // groups
    image_rows = merged_total // images
    own_rows, vis_width = vision_in.shape
    merged_width = proj_gain.shape[0]
    fold = merged_width // vis_width
    rows = own_rows // chunks
    merged_rows = rows // fold

    normed = list(entry_norm(vision_in, vis_gain))
    x = [vision_in[c * rows : (c + 1) * rows].astype(jnp.float32) for c in range(chunks)]

    tied = lax.optimization_barrier
    rail_b = moves.spread(normed[1])

    starts = dest_row.reshape(groups, images, image_rows)[:, :, 0]
    start_pos = starts % seq_len
    shift = starts[0] // seq_len
    matches = (shift[None, :] == jnp.arange(groups)[:, None]).astype(jnp.int32)
    image_of = jnp.sum(matches * jnp.arange(images), 1)
    used = jnp.sum(matches, 1) > 0
    source = (grp_rank - jnp.arange(groups)) % groups
    from_group = (source[:, None] == jnp.arange(groups)).astype(jnp.int32)
    spot = jnp.sum(matches[:, None, :] * from_group[:, :, None] * start_pos[None], (1, 2))

    span = jnp.arange(image_rows)
    picked = jnp.take(cotangent, (spot[:, None] + span).reshape(-1), axis=0, mode="clip")
    picked = [picked[s * image_rows : (s + 1) * image_rows] for s in range(groups)]
    for s in range(1, groups):
        pairs = [(g, (g - s) % groups) for g in range(groups)]
        picked[s] = lax.ppermute(picked[s], "grp", pairs)

    normed[0], rail_b, picked = tied((normed[0], rail_b, picked))
    rail_a = moves.spread(normed[0])
    patches_b = moves.gathered(rail_b)

    def grad_of(picked, c):
        returned = jnp.take(jnp.stack(picked), shift, axis=0, mode="clip").reshape(size, -1, width)
        return moves.by_row(returned[:, c * merged_rows : (c + 1) * merged_rows])

    def merge(c, summed):
        outputs = (x[c] + layer_scale * summed).astype(jnp.bfloat16)
        merged = outputs.reshape(merged_rows, merged_width).astype(jnp.float32)
        scaled, own_hat, own_inv = layer_norm(merged, proj_gain, proj_eps)
        return scaled.astype(jnp.bfloat16), own_hat, own_inv

    def unmerge(back_sum, own_hat, own_inv):
        merged_grad = norm_back(back_sum, proj_gain, own_hat, own_inv).astype(jnp.bfloat16)
        own_grad = merged_grad.reshape(rows, vis_width).astype(jnp.float32)
        return own_grad, (own_grad * layer_scale).astype(jnp.bfloat16)

    early, late = first_weight.T, second_weight
    near_b, far_b, slope_b = vision_pass(patches_b, early, late)
    near_b, far_b, rail_a = tied((near_b, far_b, rail_a))
    patches_a = moves.gathered(rail_a)
    terms_b = moves.send(moves.combine(near_b, far_b))
    near_a, far_a, slope_a = vision_pass(patches_a, early, late)
    near_a, terms_b, picked = tied((near_a, terms_b, picked))
    mixed_b, *stats_b = merge(1, moves.summed(terms_b))
    rail_b = moves.spread(mixed_b)
    near_a, mixed_b = tied((near_a, mixed_b))
    cut_a, upstream = tied(
        (moves.combine(near_a, far_a), [grad_of(picked, c) for c in range(chunks)])
    )
    terms_a = moves.send(cut_a)
    rail_b, terms_a[-1] = tied((rail_b, terms_a[-1]))
    merged_b = moves.gathered(rail_b)
    projected_b, delta_b = project(merged_b, proj_weight, upstream[1])
    projected_b, delta_b, terms_a = tied((projected_b, delta_b, terms_a))
    mixed_a, *stats_a = merge(0, moves.summed(terms_a))
    rail_a = moves.spread(mixed_a)
    delta_b, mixed_a = tied((delta_b, mixed_a))
    near_b, far_b = project_back(delta_b, proj_weight)
    near_b, far_b, rail_a = tied((near_b, far_b, rail_a))
    terms_b = moves.send(moves.combine(near_b, far_b))
    merged_a = moves.gathered(rail_a)
    projected_a, delta_a = project(merged_a, proj_weight, upstream[0])
    projected_a, delta_a, terms_b = tied((projected_a, delta_a, terms_b))
    own_b, scaled_b = unmerge(moves.summed(terms_b), *stats_b)
    rail_b = moves.spread(scaled_b)
    delta_a, scaled_b = tied((delta_a, scaled_b))
    near_a, far_a = project_back(delta_a, proj_weight)
    near_a, far_a, rail_b = tied((near_a, far_a, rail_b))
    terms_a = moves.send(moves.combine(near_a, far_a))
    grad_out_b = moves.gathered(rail_b)
    near_b, far_b = vision_pass(grad_out_b, late, early, slope_b)
    near_b, terms_a, projected_a, projected_b = tied((near_b, terms_a, projected_a, projected_b))
    own_a, scaled_a = unmerge(moves.summed(terms_a), *stats_a)
    rail_a = moves.spread(scaled_a)
    near_b, scaled_a, projected_a, projected_b = tied((near_b, scaled_a, projected_a, projected_b))
    cut_b = moves.combine(near_b, far_b)

    projected = jnp.concatenate(
        [moves.by_rank(projected_a, size), moves.by_rank(projected_b, size)], 1
    ).reshape(images, image_rows, width)
    chosen = jnp.take(projected, image_of, axis=0, mode="clip")
    arrived = [chosen[s] for s in range(groups)]
    for s in range(1, groups):
        pairs = [(g, (g + s) % groups) for g in range(groups)]
        arrived[s] = lax.ppermute(arrived[s], "grp", pairs)

    def embed(text, arrived):
        goes_to = jnp.where(used[:, None], spot[:, None] + span, seq_len).reshape(-1)
        picks = jnp.arange(seq_len)[:, None] == goes_to[None, :]
        placed = jnp.dot(
            picks.astype(jnp.bfloat16),
            jnp.concatenate(arrived, 0),
            preferred_element_type=jnp.float32,
        ).astype(jnp.bfloat16)
        return jnp.where(jnp.any(picks, 1, keepdims=True), placed, text)

    cut_b, rail_a, arrived = tied((cut_b, rail_a, arrived))
    terms_b = moves.send(cut_b)
    grad_out_a = moves.gathered(rail_a)
    near_a, far_a = vision_pass(grad_out_a, late, early, slope_a)
    near_a, terms_b, arrived = tied((near_a, terms_b, arrived))
    terms_a = moves.send(moves.combine(near_a, far_a))
    normed_b = moves.summed(terms_b)
    terms_a, seq_embed, normed_b = tied((terms_a, embed(text_embed, arrived), normed_b))
    normed_a = moves.summed(terms_a)
    parts = [layer_norm(x[c], vis_gain, vis_eps) for c in range(chunks)]
    grads = [
        own_a + norm_back(normed_a, vis_gain, parts[0][1], parts[0][2]),
        own_b + norm_back(normed_b, vis_gain, parts[1][1], parts[1][2]),
    ]
    grad_vision = jnp.concatenate(grads, 0).astype(jnp.bfloat16)
    return (seq_embed, grad_vision)


def solution(mesh):
    placed = (
        P(("grp", "tp"), None),
        P(),
        P(None, "tp"),
        P("tp", None),
        P(),
        P(),
        P(None, "tp"),
        P("grp", "tp"),
        P(),
        P("grp", "tp"),
    )
    return jax.shard_map(
        per_device,
        mesh=mesh,
        in_specs=placed,
        out_specs=(P("grp", "tp"), P(("grp", "tp"), None)),
        check_vma=False,
    )
```

```python
import functools

import jax
import jax.numpy as jnp
from jax import lax
from jax.experimental import pallas as pl
from jax.experimental.pallas import tpu as pltpu
from jax.sharding import PartitionSpec as P

vis_eps = 1e-06
proj_eps = 1e-05
chunks = 2
images = 4
cores = 2


def layer_norm(values, scale_vec, epsilon):
    mean_val = jnp.mean(values, -1, keepdims=True)
    centred = values - mean_val
    inv_std = lax.rsqrt(jnp.mean(centred * centred, -1, keepdims=True) + epsilon)
    normed = centred * inv_std
    return (normed * scale_vec, normed, inv_std)


def norm_back(upstream, scale_vec, normed, inv_std):
    scaled = upstream * scale_vec
    return inv_std * (
        scaled
        - jnp.mean(scaled, -1, keepdims=True)
        - normed * jnp.mean(scaled * normed, -1, keepdims=True)
    )


def times_transposed(left, right):
    return lax.dot_general(
        left, right, (((1,), (1,)), ((), ())), preferred_element_type=jnp.float32
    )


def tile_of(length, most):
    return max(t for t in range(128, most + 1, 128) if length % t == 0)


def laid(pieces):
    if len(pieces) == 1:
        return pieces[0][...]
    if pieces[0].shape[0] % 16 == 0:
        return jnp.concatenate([p[...] for p in pieces], 0)
    return jnp.concatenate([p[...].astype(jnp.float32) for p in pieces], 0).astype(jnp.bfloat16)


def each_rows(total, body):
    step = 32 if total % 32 == 0 else total

    def run(i, _):
        body(pl.ds(pl.multiple_of(i * step, step), step))
        return 0

    lax.fori_loop(0, total // step, run, 0)


def block_start(total, rows, j):
    return pl.multiple_of(jnp.minimum(j * rows, total - rows), 16)


def fetch(source, held, sems, j):
    count, rows = held.shape[:2]

    @pl.when(j < count)
    def _():
        part = source.at[pl.ds(block_start(source.shape[0], rows, j), rows)]
        pltpu.make_async_copy(part, held.at[j], sems.at[j]).start()


def arrive(source, held, sems, j):
    rows = held.shape[1]
    pltpu.make_async_copy(source.at[pl.ds(0, rows)], held.at[j], sems.at[j]).wait()


def vision_kernel(count, ahead, *refs):
    pieces = refs[:count]
    if ahead:
        early, late, near, far, slope = refs[count : count + 5]
    else:
        early, late, slope, near, far = refs[count : count + 5]
    first, second, rows, pre, hidden, first_sems, second_sems = refs[count + 5 :]
    blocks, size, width = first.shape
    for j in range(blocks):
        fetch(early, first, first_sems, j)
    rows[...] = laid(pieces)

    def block(j, _):
        arrive(early, first, first_sems, j)
        fetch(late, second, second_sems, j)
        pre[...] = times_transposed(rows[...], first[j])
        repeated = j * size - jnp.minimum(j * size, early.shape[0] - size)
        place = pl.ds(pl.multiple_of(j * size, min(size, 128)), size)

        def act(sel):
            u = pre[sel, :]
            if ahead:
                fresh = lax.broadcasted_iota(jnp.int32, u.shape, 1) >= repeated
                cumul = 0.5 * (1.0 + lax.erf(u * 0.7071067811865476))
                dense = jnp.exp(-0.5 * u * u) * 0.3989422804014327
                hidden[sel, place] = jnp.where(fresh, u * cumul, 0.0).astype(jnp.bfloat16)
                slope[j, sel, :] = jnp.where(fresh, cumul + u * dense, 0.0)
            else:
                hidden[sel, place] = (u * slope[j, sel, :]).astype(jnp.bfloat16)

        each_rows(pre.shape[0], act)
        return 0

    lax.fori_loop(0, blocks, block, 0)
    for j in range(blocks):
        arrive(late, second, second_sems, j)
    half = near.shape[0]
    tile = min(1280, width)
    for k in range(0, width, tile):
        span = slice(k, min(k + tile, width))
        held = second[:, :, span]
        both = jnp.dot(
            hidden[...],
            held.reshape(blocks * size, held.shape[2]),
            preferred_element_type=jnp.float32,
        ).astype(jnp.bfloat16)
        near[:, span] = both[:half]
        far[:, span] = both[half:]


def project_kernel(count, *refs):
    pieces = refs[:count]
    weight, upstream, projected, delta, held, rows, pre, sems = refs[count:]
    for j in range(3):
        fetch(weight, held, sems, j)
    rows[...] = laid(pieces)
    pre[...] = jnp.zeros_like(pre)
    chunk = held.shape[1]

    def ahead(j, _):
        arrive(weight, held, sems, j)
        fetch(weight, held, sems, j + 3)
        sel = pl.ds(pl.multiple_of(j * chunk, 128), chunk)
        pre[...] += jnp.dot(rows[:, sel], held[j], preferred_element_type=jnp.float32)
        return 0

    lax.fori_loop(0, held.shape[0], ahead, 0)

    def act(sel):
        u = pre[sel, :]
        cumul = 0.5 * (1.0 + lax.erf(u * 0.7071067811865476))
        dense = jnp.exp(-0.5 * u * u) * 0.3989422804014327
        projected[sel, :] = (u * cumul).astype(jnp.bfloat16)
        grad = upstream[sel, :].astype(jnp.float32)
        delta[sel, :] = (grad * (cumul + u * dense)).astype(jnp.bfloat16)

    each_rows(pre.shape[0], act)


def project_back_kernel(delta, weight, near, far, held, sems):
    for j in range(3):
        fetch(weight, held, sems, j)
    chunk = held.shape[1]
    half = near.shape[0]

    def behind(j, _):
        arrive(weight, held, sems, j)
        fetch(weight, held, sems, j + 3)
        sel = pl.ds(pl.multiple_of(j * chunk, 128), chunk)
        back = times_transposed(delta[...], held[j]).astype(jnp.bfloat16)
        near[:, sel] = back[:half]
        far[:, sel] = back[half:]
        return 0

    lax.fori_loop(0, held.shape[0], behind, 0)


def entry_kernel(source, gain, *normed):
    rows = normed[0].shape[0]
    for c, out in enumerate(normed):
        values = source[c * rows : (c + 1) * rows].astype(jnp.float32)
        out[...] = layer_norm(values, gain[...][None, :], vis_eps)[0].astype(jnp.bfloat16)


def entry_norm(source, gain):
    rows, width = source.shape
    return pl.pallas_call(
        entry_kernel,
        in_specs=whole_blocks(2),
        out_specs=whole_blocks(chunks),
        out_shape=[jax.ShapeDtypeStruct((rows // chunks, width), jnp.bfloat16)] * chunks,
        cost_estimate=pl.CostEstimate(
            flops=8 * rows * width, bytes_accessed=4 * rows * width, transcendentals=rows
        ),
    )(source, gain)


def settings(limit):
    return pltpu.CompilerParams(vmem_limit_bytes=limit * 1024 * 1024)


def whole_blocks(count):
    return [pl.BlockSpec(memory_space=pltpu.VMEM)] * count


def vision_pass(pieces, early, late, slope=None):
    rows = sum(p.shape[0] for p in pieces)
    units, width = early.shape
    size = min(256, units)
    blocks = -(-units // size)
    given = [] if slope is None else [slope]
    slopes = [jax.ShapeDtypeStruct((blocks, rows, size), jnp.float32)] * (1 - len(given))
    return pl.pallas_call(
        functools.partial(vision_kernel, len(pieces), slope is None),
        in_specs=whole_blocks(len(pieces))
        + [pl.BlockSpec(memory_space=pl.ANY)] * 2
        + whole_blocks(len(given)),
        out_specs=whole_blocks(2 + len(slopes)),
        out_shape=[jax.ShapeDtypeStruct((rows // 2, width), jnp.bfloat16)] * 2 + slopes,
        scratch_shapes=[
            pltpu.VMEM((blocks, size, width), jnp.bfloat16),
            pltpu.VMEM((blocks, size, width), jnp.bfloat16),
            pltpu.VMEM((rows, width), jnp.bfloat16),
            pltpu.VMEM((rows, size), jnp.float32),
            pltpu.VMEM((rows, blocks * size), jnp.bfloat16),
            pltpu.SemaphoreType.DMA((blocks,)),
            pltpu.SemaphoreType.DMA((blocks,)),
        ],
        compiler_params=settings(56),
        cost_estimate=pl.CostEstimate(
            flops=4 * rows * width * units,
            bytes_accessed=4 * width * units + 4 * rows * (width + units),
            transcendentals=2 * rows * units,
        ),
    )(*pieces, early, late, *given)


def weight_cost(rows, depth, units):
    return pl.CostEstimate(
        flops=2 * rows * depth * units,
        bytes_accessed=2 * depth * units + 4 * rows * (depth + units),
        transcendentals=2 * rows * units,
    )


def project(pieces, weight, upstream):
    rows = sum(p.shape[0] for p in pieces)
    depth, units = weight.shape
    size = tile_of(depth, 1280)
    return pl.pallas_call(
        functools.partial(project_kernel, len(pieces)),
        in_specs=whole_blocks(len(pieces)) + [pl.BlockSpec(memory_space=pl.ANY)] + whole_blocks(1),
        out_specs=whole_blocks(2),
        out_shape=[jax.ShapeDtypeStruct((rows, units), jnp.bfloat16)] * 2,
        scratch_shapes=[
            pltpu.VMEM((depth // size, size, units), jnp.bfloat16),
            pltpu.VMEM((rows, depth), jnp.bfloat16),
            pltpu.VMEM((rows, units), jnp.float32),
            pltpu.SemaphoreType.DMA((depth // size,)),
        ],
        compiler_params=settings(40),
        cost_estimate=weight_cost(rows, depth, units),
    )(*pieces, weight, upstream)


def project_back(delta, weight):
    rows = delta.shape[0]
    depth, units = weight.shape
    size = tile_of(depth, 1280)
    return pl.pallas_call(
        project_back_kernel,
        in_specs=whole_blocks(1) + [pl.BlockSpec(memory_space=pl.ANY)],
        out_specs=whole_blocks(2),
        out_shape=[jax.ShapeDtypeStruct((rows // 2, depth), jnp.bfloat16)] * 2,
        scratch_shapes=[
            pltpu.VMEM((depth // size, size, units), jnp.bfloat16),
            pltpu.SemaphoreType.DMA((depth // size,)),
        ],
        compiler_params=settings(40),
        cost_estimate=weight_cost(rows, depth, units),
    )(delta, weight)


class Direct:
    def __init__(self):
        self.size = lax.axis_size("tp")
        self.places = self.size // cores
        rank = lax.axis_index("tp")
        place, core = rank // cores, rank % cores
        self.partners = [0, *range(2, self.places), *range(1, min(2, self.places))]
        partner = (place ^ jnp.array(self.partners)) * cores
        self.ranks = jnp.concatenate([partner + core, partner + 1 - core])
        every = jnp.arange(self.size)
        block = jnp.array([self.partners.index(k) for k in range(self.places)])
        self.blocks = (every + core) % cores * self.places + block[every // cores ^ place]
        self.pairs = [(a, a + 1 - 2 * (a % cores)) for a in range(self.size)]

    def shift(self, block, k):
        pairs = [(a, (a // cores ^ k) * cores + a % cores) for a in range(self.size)]
        return lax.ppermute(block, "tp", pairs)

    def spread(self, block):
        return [block] + [self.shift(block, k) for k in self.partners[1:]]

    def gathered(self, mine):
        other = [lax.ppermute(m, "tp", self.pairs) for m in mine]
        if mine[0].shape[0] % 8:
            return [jnp.concatenate(mine + other, 0)]
        return mine + other

    def combine(self, near, far):
        rows = near.shape[0] // self.places
        got = lax.ppermute(far, "tp", self.pairs)
        both = near.astype(jnp.float32) + got.astype(jnp.float32)
        cut = [both[k * rows : (k + 1) * rows] for k in range(self.places)]
        return cut[:1] + [c.astype(jnp.bfloat16) for c in cut[1:]]

    def send(self, cut):
        return cut[:1] + [self.shift(c, k) for c, k in zip(cut[1:], self.partners[1:])]

    def summed(self, terms):
        return sum([t.astype(jnp.float32) for t in terms[1:]], terms[0])

    def by_rank(self, rows, size):
        return jnp.take(rows.reshape(size, -1, rows.shape[-1]), self.blocks, axis=0, mode="clip")

    def by_row(self, ranks):
        return jnp.take(ranks, self.ranks, axis=0, mode="clip").reshape(-1, ranks.shape[-1])


def per_device(
    vision_in,
    vis_gain,
    first_weight,
    second_weight,
    layer_scale,
    proj_gain,
    proj_weight,
    text_embed,
    dest_row,
    cotangent,
):
    moves = Direct()
    groups = lax.axis_size("grp")
    size = lax.axis_size("tp")
    grp_rank = lax.axis_index("grp")
    seq_len, width = text_embed.shape
    merged_total = dest_row.shape[0] // groups
    image_rows = merged_total // images
    own_rows, vis_width = vision_in.shape
    merged_width = proj_gain.shape[0]
    fold = merged_width // vis_width
    rows = own_rows // chunks
    merged_rows = rows // fold

    normed = list(entry_norm(vision_in, vis_gain))
    x = [vision_in[c * rows : (c + 1) * rows].astype(jnp.float32) for c in range(chunks)]

    tied = lax.optimization_barrier
    rail_b = moves.spread(normed[1])

    starts = dest_row.reshape(groups, images, image_rows)[:, :, 0]
    start_pos = starts % seq_len
    shift = starts[0] // seq_len
    matches = (shift[None, :] == jnp.arange(groups)[:, None]).astype(jnp.int32)
    image_of = jnp.sum(matches * jnp.arange(images), 1)
    used = jnp.sum(matches, 1) > 0
    source = (grp_rank - jnp.arange(groups)) % groups
    from_group = (source[:, None] == jnp.arange(groups)).astype(jnp.int32)
    spot = jnp.sum(matches[:, None, :] * from_group[:, :, None] * start_pos[None], (1, 2))

    span = jnp.arange(image_rows)
    picked = jnp.take(cotangent, (spot[:, None] + span).reshape(-1), axis=0, mode="clip")
    picked = [picked[s * image_rows : (s + 1) * image_rows] for s in range(groups)]
    for s in range(1, groups):
        pairs = [(g, (g - s) % groups) for g in range(groups)]
        picked[s] = lax.ppermute(picked[s], "grp", pairs)

    normed[0], rail_b, picked = tied((normed[0], rail_b, picked))
    rail_a = moves.spread(normed[0])
    patches_b = moves.gathered(rail_b)

    def grad_of(picked, c):
        returned = jnp.take(jnp.stack(picked), shift, axis=0, mode="clip").reshape(size, -1, width)
        return moves.by_row(returned[:, c * merged_rows : (c + 1) * merged_rows])

    def merge(c, summed):
        outputs = (x[c] + layer_scale * summed).astype(jnp.bfloat16)
        merged = outputs.reshape(merged_rows, merged_width).astype(jnp.float32)
        scaled, own_hat, own_inv = layer_norm(merged, proj_gain, proj_eps)
        return scaled.astype(jnp.bfloat16), own_hat, own_inv

    def unmerge(back_sum, own_hat, own_inv):
        merged_grad = norm_back(back_sum, proj_gain, own_hat, own_inv).astype(jnp.bfloat16)
        own_grad = merged_grad.reshape(rows, vis_width).astype(jnp.float32)
        return own_grad, (own_grad * layer_scale).astype(jnp.bfloat16)

    early, late = first_weight.T, second_weight
    near_b, far_b, slope_b = vision_pass(patches_b, early, late)
    near_b, far_b, rail_a = tied((near_b, far_b, rail_a))
    patches_a = moves.gathered(rail_a)
    terms_b = moves.send(moves.combine(near_b, far_b))
    near_a, far_a, slope_a = vision_pass(patches_a, early, late)
    near_a, terms_b, picked = tied((near_a, terms_b, picked))
    mixed_b, *stats_b = merge(1, moves.summed(terms_b))
    rail_b = moves.spread(mixed_b)
    near_a, mixed_b = tied((near_a, mixed_b))
    cut_a, upstream = tied(
        (moves.combine(near_a, far_a), [grad_of(picked, c) for c in range(chunks)])
    )
    terms_a = moves.send(cut_a)
    rail_b, terms_a[-1] = tied((rail_b, terms_a[-1]))
    merged_b = moves.gathered(rail_b)
    projected_b, delta_b = project(merged_b, proj_weight, upstream[1])
    projected_b, delta_b, terms_a = tied((projected_b, delta_b, terms_a))
    mixed_a, *stats_a = merge(0, moves.summed(terms_a))
    rail_a = moves.spread(mixed_a)
    delta_b, mixed_a = tied((delta_b, mixed_a))
    near_b, far_b = project_back(delta_b, proj_weight)
    near_b, far_b, rail_a = tied((near_b, far_b, rail_a))
    terms_b = moves.send(moves.combine(near_b, far_b))
    merged_a = moves.gathered(rail_a)
    projected_a, delta_a = project(merged_a, proj_weight, upstream[0])
    projected_a, delta_a, terms_b = tied((projected_a, delta_a, terms_b))
    own_b, scaled_b = unmerge(moves.summed(terms_b), *stats_b)
    rail_b = moves.spread(scaled_b)
    delta_a, scaled_b = tied((delta_a, scaled_b))
    near_a, far_a = project_back(delta_a, proj_weight)
    near_a, far_a, rail_b = tied((near_a, far_a, rail_b))
    terms_a = moves.send(moves.combine(near_a, far_a))
    grad_out_b = moves.gathered(rail_b)
    near_b, far_b = vision_pass(grad_out_b, late, early, slope_b)
    near_b, terms_a, projected_a, projected_b = tied((near_b, terms_a, projected_a, projected_b))
    own_a, scaled_a = unmerge(moves.summed(terms_a), *stats_a)
    rail_a = moves.spread(scaled_a)
    near_b, scaled_a, projected_a, projected_b = tied((near_b, scaled_a, projected_a, projected_b))
    cut_b = moves.combine(near_b, far_b)

    projected = jnp.concatenate(
        [moves.by_rank(projected_a, size), moves.by_rank(projected_b, size)], 1
    ).reshape(images, image_rows, width)
    chosen = jnp.take(projected, image_of, axis=0, mode="clip")
    arrived = [chosen[s] for s in range(groups)]
    for s in range(1, groups):
        pairs = [(g, (g + s) % groups) for g in range(groups)]
        arrived[s] = lax.ppermute(arrived[s], "grp", pairs)

    def embed(text, arrived):
        goes_to = jnp.where(used[:, None], spot[:, None] + span, seq_len).reshape(-1)
        picks = jnp.arange(seq_len)[:, None] == goes_to[None, :]
        placed = jnp.dot(
            picks.astype(jnp.bfloat16),
            jnp.concatenate(arrived, 0),
            preferred_element_type=jnp.float32,
        ).astype(jnp.bfloat16)
        return jnp.where(jnp.any(picks, 1, keepdims=True), placed, text)

    cut_b, rail_a, arrived = tied((cut_b, rail_a, arrived))
    terms_b = moves.send(cut_b)
    grad_out_a = moves.gathered(rail_a)
    near_a, far_a = vision_pass(grad_out_a, late, early, slope_a)
    near_a, terms_b, arrived = tied((near_a, terms_b, arrived))
    terms_a = moves.send(moves.combine(near_a, far_a))
    normed_b = moves.summed(terms_b)
    terms_a, seq_embed, normed_b = tied((terms_a, embed(text_embed, arrived), normed_b))
    normed_a = moves.summed(terms_a)
    parts = [layer_norm(x[c], vis_gain, vis_eps) for c in range(chunks)]
    grads = [
        own_a + norm_back(normed_a, vis_gain, parts[0][1], parts[0][2]),
        own_b + norm_back(normed_b, vis_gain, parts[1][1], parts[1][2]),
    ]
    grad_vision = jnp.concatenate(grads, 0).astype(jnp.bfloat16)
    return (seq_embed, grad_vision)


def solution(mesh):
    placed = (
        P(("grp", "tp"), None),
        P(),
        P(None, "tp"),
        P("tp", None),
        P(),
        P(),
        P(None, "tp"),
        P("grp", "tp"),
        P(),
        P("grp", "tp"),
    )
    return jax.shard_map(
        per_device,
        mesh=mesh,
        in_specs=placed,
        out_specs=(P("grp", "tp"), P(("grp", "tp"), None)),
        check_vma=False,
    )
```

```python
import functools

import jax
import jax.numpy as jnp
from jax import lax
from jax.experimental import pallas as pl
from jax.experimental.pallas import tpu as pltpu
from jax.sharding import PartitionSpec as P

vis_eps = 1e-06
proj_eps = 1e-05
chunks = 2
images = 4
cores = 2


def layer_norm(values, scale_vec, epsilon):
    mean_val = jnp.mean(values, -1, keepdims=True)
    centred = values - mean_val
    inv_std = lax.rsqrt(jnp.mean(centred * centred, -1, keepdims=True) + epsilon)
    normed = centred * inv_std
    return (normed * scale_vec, normed, inv_std)


def norm_back(upstream, scale_vec, normed, inv_std):
    scaled = upstream * scale_vec
    return inv_std * (
        scaled
        - jnp.mean(scaled, -1, keepdims=True)
        - normed * jnp.mean(scaled * normed, -1, keepdims=True)
    )


def times_transposed(left, right):
    return lax.dot_general(
        left, right, (((1,), (1,)), ((), ())), preferred_element_type=jnp.float32
    )


def tile_of(length, most):
    return max(t for t in range(128, most + 1, 128) if length % t == 0)


def laid(pieces):
    if len(pieces) == 1:
        return pieces[0][...]
    if pieces[0].shape[0] % 16 == 0:
        return jnp.concatenate([p[...] for p in pieces], 0)
    return jnp.concatenate([p[...].astype(jnp.float32) for p in pieces], 0).astype(jnp.bfloat16)


def each_rows(total, body):
    step = 32 if total % 32 == 0 else total

    def run(i, _):
        body(pl.ds(pl.multiple_of(i * step, step), step))
        return 0

    lax.fori_loop(0, total // step, run, 0)


def block_start(total, rows, j):
    return pl.multiple_of(jnp.minimum(j * rows, total - rows), 16)


def fetch(source, held, sems, j):
    count, rows = held.shape[:2]

    @pl.when(j < count)
    def _():
        part = source.at[pl.ds(block_start(source.shape[0], rows, j), rows)]
        pltpu.make_async_copy(part, held.at[j], sems.at[j]).start()


def arrive(source, held, sems, j):
    rows = held.shape[1]
    pltpu.make_async_copy(source.at[pl.ds(0, rows)], held.at[j], sems.at[j]).wait()


def vision_kernel(count, ahead, *refs):
    pieces = refs[:count]
    if ahead:
        early, late, near, far, slope = refs[count : count + 5]
    else:
        early, late, slope, near, far = refs[count : count + 5]
    first, second, rows, pre, hidden, first_sems, second_sems = refs[count + 5 :]
    blocks, size, width = first.shape
    for j in range(blocks):
        fetch(early, first, first_sems, j)
    rows[...] = laid(pieces)

    def block(j, _):
        arrive(early, first, first_sems, j)
        fetch(late, second, second_sems, j)
        pre[...] = times_transposed(rows[...], first[j])
        repeated = j * size - jnp.minimum(j * size, early.shape[0] - size)
        place = pl.ds(pl.multiple_of(j * size, min(size, 128)), size)

        def act(sel):
            u = pre[sel, :]
            if ahead:
                fresh = lax.broadcasted_iota(jnp.int32, u.shape, 1) >= repeated
                cumul = 0.5 * (1.0 + lax.erf(u * 0.7071067811865476))
                dense = jnp.exp(-0.5 * u * u) * 0.3989422804014327
                hidden[sel, place] = jnp.where(fresh, u * cumul, 0.0).astype(jnp.bfloat16)
                slope[j, sel, :] = jnp.where(fresh, cumul + u * dense, 0.0)
            else:
                hidden[sel, place] = (u * slope[j, sel, :]).astype(jnp.bfloat16)

        each_rows(pre.shape[0], act)
        return 0

    lax.fori_loop(0, blocks, block, 0)
    for j in range(blocks):
        arrive(late, second, second_sems, j)
    half = near.shape[0]
    tile = min(1280, width)
    for k in range(0, width, tile):
        span = slice(k, min(k + tile, width))
        held = second[:, :, span]
        both = jnp.dot(
            hidden[...],
            held.reshape(blocks * size, held.shape[2]),
            preferred_element_type=jnp.float32,
        ).astype(jnp.bfloat16)
        near[:, span] = both[:half]
        far[:, span] = both[half:]


def project_kernel(count, *refs):
    pieces = refs[:count]
    weight, upstream, projected, delta, held, rows, pre, sems = refs[count:]
    for j in range(3):
        fetch(weight, held, sems, j)
    rows[...] = laid(pieces)
    pre[...] = jnp.zeros_like(pre)
    chunk = held.shape[1]

    def ahead(j, _):
        arrive(weight, held, sems, j)
        fetch(weight, held, sems, j + 3)
        sel = pl.ds(pl.multiple_of(j * chunk, 128), chunk)
        pre[...] += jnp.dot(rows[:, sel], held[j], preferred_element_type=jnp.float32)
        return 0

    lax.fori_loop(0, held.shape[0], ahead, 0)

    def act(sel):
        u = pre[sel, :]
        cumul = 0.5 * (1.0 + lax.erf(u * 0.7071067811865476))
        dense = jnp.exp(-0.5 * u * u) * 0.3989422804014327
        projected[sel, :] = (u * cumul).astype(jnp.bfloat16)
        grad = upstream[sel, :].astype(jnp.float32)
        delta[sel, :] = (grad * (cumul + u * dense)).astype(jnp.bfloat16)

    each_rows(pre.shape[0], act)


def project_back_kernel(delta, weight, near, far, held, sems):
    for j in range(3):
        fetch(weight, held, sems, j)
    chunk = held.shape[1]
    half = near.shape[0]

    def behind(j, _):
        arrive(weight, held, sems, j)
        fetch(weight, held, sems, j + 3)
        sel = pl.ds(pl.multiple_of(j * chunk, 128), chunk)
        back = times_transposed(delta[...], held[j]).astype(jnp.bfloat16)
        near[:, sel] = back[:half]
        far[:, sel] = back[half:]
        return 0

    lax.fori_loop(0, held.shape[0], behind, 0)


def entry_kernel(source, gain, *normed):
    rows = normed[0].shape[0]
    for c, out in enumerate(normed):
        values = source[c * rows : (c + 1) * rows].astype(jnp.float32)
        out[...] = layer_norm(values, gain[...][None, :], vis_eps)[0].astype(jnp.bfloat16)


def entry_norm(source, gain):
    rows, width = source.shape
    return pl.pallas_call(
        entry_kernel,
        in_specs=whole_blocks(2),
        out_specs=whole_blocks(chunks),
        out_shape=[jax.ShapeDtypeStruct((rows // chunks, width), jnp.bfloat16)] * chunks,
        cost_estimate=pl.CostEstimate(
            flops=8 * rows * width, bytes_accessed=4 * rows * width, transcendentals=rows
        ),
    )(source, gain)


def settings(limit):
    return pltpu.CompilerParams(vmem_limit_bytes=limit * 1024 * 1024)


def whole_blocks(count):
    return [pl.BlockSpec(memory_space=pltpu.VMEM)] * count


def vision_pass(pieces, early, late, slope=None):
    rows = sum(p.shape[0] for p in pieces)
    units, width = early.shape
    size = min(256, units)
    blocks = -(-units // size)
    given = [] if slope is None else [slope]
    slopes = [jax.ShapeDtypeStruct((blocks, rows, size), jnp.float32)] * (1 - len(given))
    return pl.pallas_call(
        functools.partial(vision_kernel, len(pieces), slope is None),
        in_specs=whole_blocks(len(pieces))
        + [pl.BlockSpec(memory_space=pl.ANY)] * 2
        + whole_blocks(len(given)),
        out_specs=whole_blocks(2 + len(slopes)),
        out_shape=[jax.ShapeDtypeStruct((rows // 2, width), jnp.bfloat16)] * 2 + slopes,
        scratch_shapes=[
            pltpu.VMEM((blocks, size, width), jnp.bfloat16),
            pltpu.VMEM((blocks, size, width), jnp.bfloat16),
            pltpu.VMEM((rows, width), jnp.bfloat16),
            pltpu.VMEM((rows, size), jnp.float32),
            pltpu.VMEM((rows, blocks * size), jnp.bfloat16),
            pltpu.SemaphoreType.DMA((blocks,)),
            pltpu.SemaphoreType.DMA((blocks,)),
        ],
        compiler_params=settings(56),
        cost_estimate=pl.CostEstimate(
            flops=4 * rows * width * units,
            bytes_accessed=4 * width * units + 4 * rows * (width + units),
            transcendentals=2 * rows * units,
        ),
    )(*pieces, early, late, *given)


def weight_cost(rows, depth, units):
    return pl.CostEstimate(
        flops=2 * rows * depth * units,
        bytes_accessed=2 * depth * units + 4 * rows * (depth + units),
        transcendentals=2 * rows * units,
    )


def project(pieces, weight, upstream):
    rows = sum(p.shape[0] for p in pieces)
    depth, units = weight.shape
    size = tile_of(depth, 1280)
    return pl.pallas_call(
        functools.partial(project_kernel, len(pieces)),
        in_specs=whole_blocks(len(pieces)) + [pl.BlockSpec(memory_space=pl.ANY)] + whole_blocks(1),
        out_specs=whole_blocks(2),
        out_shape=[jax.ShapeDtypeStruct((rows, units), jnp.bfloat16)] * 2,
        scratch_shapes=[
            pltpu.VMEM((depth // size, size, units), jnp.bfloat16),
            pltpu.VMEM((rows, depth), jnp.bfloat16),
            pltpu.VMEM((rows, units), jnp.float32),
            pltpu.SemaphoreType.DMA((depth // size,)),
        ],
        compiler_params=settings(40),
        cost_estimate=weight_cost(rows, depth, units),
    )(*pieces, weight, upstream)


def project_back(delta, weight):
    rows = delta.shape[0]
    depth, units = weight.shape
    size = tile_of(depth, 1280)
    return pl.pallas_call(
        project_back_kernel,
        in_specs=whole_blocks(1) + [pl.BlockSpec(memory_space=pl.ANY)],
        out_specs=whole_blocks(2),
        out_shape=[jax.ShapeDtypeStruct((rows // 2, depth), jnp.bfloat16)] * 2,
        scratch_shapes=[
            pltpu.VMEM((depth // size, size, units), jnp.bfloat16),
            pltpu.SemaphoreType.DMA((depth // size,)),
        ],
        compiler_params=settings(40),
        cost_estimate=weight_cost(rows, depth, units),
    )(delta, weight)


class Direct:
    def __init__(self):
        self.size = lax.axis_size("tp")
        self.places = self.size // cores
        rank = lax.axis_index("tp")
        place, core = rank // cores, rank % cores
        self.partners = [0, *range(2, self.places), *range(1, min(2, self.places))]
        partner = (place ^ jnp.array(self.partners)) * cores
        self.ranks = jnp.concatenate([partner + core, partner + 1 - core])
        every = jnp.arange(self.size)
        block = jnp.array([self.partners.index(k) for k in range(self.places)])
        self.blocks = (every + core) % cores * self.places + block[every // cores ^ place]
        self.pairs = [(a, a + 1 - 2 * (a % cores)) for a in range(self.size)]

    def shift(self, block, k):
        pairs = [(a, (a // cores ^ k) * cores + a % cores) for a in range(self.size)]
        return lax.ppermute(block, "tp", pairs)

    def spread(self, block):
        return [block] + [self.shift(block, k) for k in self.partners[1:]]

    def gathered(self, mine):
        other = [lax.ppermute(m, "tp", self.pairs) for m in mine]
        if mine[0].shape[0] % 8:
            return [jnp.concatenate(mine + other, 0)]
        return mine + other

    def combine(self, near, far):
        rows = near.shape[0] // self.places
        got = lax.ppermute(far, "tp", self.pairs)
        both = near.astype(jnp.float32) + got.astype(jnp.float32)
        cut = [both[k * rows : (k + 1) * rows] for k in range(self.places)]
        return cut[:1] + [c.astype(jnp.bfloat16) for c in cut[1:]]

    def send(self, cut):
        return cut[:1] + [self.shift(c, k) for c, k in zip(cut[1:], self.partners[1:])]

    def summed(self, terms):
        return sum([t.astype(jnp.float32) for t in terms[1:]], terms[0])

    def by_rank(self, rows, size):
        return jnp.take(rows.reshape(size, -1, rows.shape[-1]), self.blocks, axis=0, mode="clip")

    def by_row(self, ranks):
        return jnp.take(ranks, self.ranks, axis=0, mode="clip").reshape(-1, ranks.shape[-1])


def per_device(
    vision_in,
    vis_gain,
    first_weight,
    second_weight,
    layer_scale,
    proj_gain,
    proj_weight,
    text_embed,
    dest_row,
    cotangent,
):
    moves = Direct()
    groups = lax.axis_size("grp")
    size = lax.axis_size("tp")
    grp_rank = lax.axis_index("grp")
    seq_len, width = text_embed.shape
    merged_total = dest_row.shape[0] // groups
    image_rows = merged_total // images
    own_rows, vis_width = vision_in.shape
    merged_width = proj_gain.shape[0]
    fold = merged_width // vis_width
    rows = own_rows // chunks
    merged_rows = rows // fold

    normed = list(entry_norm(vision_in, vis_gain))
    x = [vision_in[c * rows : (c + 1) * rows].astype(jnp.float32) for c in range(chunks)]

    tied = lax.optimization_barrier
    rail_b = moves.spread(normed[1])

    starts = dest_row.reshape(groups, images, image_rows)[:, :, 0]
    start_pos = starts % seq_len
    shift = starts[0] // seq_len
    matches = (shift[None, :] == jnp.arange(groups)[:, None]).astype(jnp.int32)
    image_of = jnp.sum(matches * jnp.arange(images), 1)
    used = jnp.sum(matches, 1) > 0
    source = (grp_rank - jnp.arange(groups)) % groups
    from_group = (source[:, None] == jnp.arange(groups)).astype(jnp.int32)
    spot = jnp.sum(matches[:, None, :] * from_group[:, :, None] * start_pos[None], (1, 2))

    span = jnp.arange(image_rows)
    picked = jnp.take(cotangent, (spot[:, None] + span).reshape(-1), axis=0, mode="clip")
    picked = [picked[s * image_rows : (s + 1) * image_rows] for s in range(groups)]
    for s in range(1, groups):
        pairs = [(g, (g - s) % groups) for g in range(groups)]
        picked[s] = lax.ppermute(picked[s], "grp", pairs)

    normed[0], rail_b, picked = tied((normed[0], rail_b, picked))
    rail_a = moves.spread(normed[0])
    patches_b = moves.gathered(rail_b)

    def grad_of(picked, c):
        returned = jnp.take(jnp.stack(picked), shift, axis=0, mode="clip").reshape(size, -1, width)
        return moves.by_row(returned[:, c * merged_rows : (c + 1) * merged_rows])

    def merge(c, summed):
        outputs = (x[c] + layer_scale * summed).astype(jnp.bfloat16)
        merged = outputs.reshape(merged_rows, merged_width).astype(jnp.float32)
        scaled, own_hat, own_inv = layer_norm(merged, proj_gain, proj_eps)
        return scaled.astype(jnp.bfloat16), own_hat, own_inv

    def unmerge(back_sum, own_hat, own_inv):
        merged_grad = norm_back(back_sum, proj_gain, own_hat, own_inv).astype(jnp.bfloat16)
        own_grad = merged_grad.reshape(rows, vis_width).astype(jnp.float32)
        return own_grad, (own_grad * layer_scale).astype(jnp.bfloat16)

    early, late = first_weight.T, second_weight
    near_b, far_b, slope_b = vision_pass(patches_b, early, late)
    near_b, far_b, rail_a = tied((near_b, far_b, rail_a))
    patches_a = moves.gathered(rail_a)
    terms_b = moves.send(moves.combine(near_b, far_b))
    near_a, far_a, slope_a = vision_pass(patches_a, early, late)
    near_a, terms_b, picked = tied((near_a, terms_b, picked))
    mixed_b, *stats_b = merge(1, moves.summed(terms_b))
    rail_b = moves.spread(mixed_b)
    near_a, mixed_b = tied((near_a, mixed_b))
    cut_a, upstream = tied(
        (moves.combine(near_a, far_a), [grad_of(picked, c) for c in range(chunks)])
    )
    terms_a = moves.send(cut_a)
    merged_b = moves.gathered(rail_b)
    projected_b, delta_b = project(merged_b, proj_weight, upstream[1])
    projected_b, delta_b, terms_a = tied((projected_b, delta_b, terms_a))
    mixed_a, *stats_a = merge(0, moves.summed(terms_a))
    rail_a = moves.spread(mixed_a)
    delta_b, mixed_a = tied((delta_b, mixed_a))
    near_b, far_b = project_back(delta_b, proj_weight)
    near_b, far_b, rail_a = tied((near_b, far_b, rail_a))
    terms_b = moves.send(moves.combine(near_b, far_b))
    merged_a = moves.gathered(rail_a)
    projected_a, delta_a = project(merged_a, proj_weight, upstream[0])
    projected_a, delta_a, terms_b = tied((projected_a, delta_a, terms_b))
    own_b, scaled_b = unmerge(moves.summed(terms_b), *stats_b)
    rail_b = moves.spread(scaled_b)
    delta_a, scaled_b = tied((delta_a, scaled_b))
    near_a, far_a = project_back(delta_a, proj_weight)
    near_a, far_a, rail_b = tied((near_a, far_a, rail_b))
    terms_a = moves.send(moves.combine(near_a, far_a))
    grad_out_b = moves.gathered(rail_b)
    near_b, far_b = vision_pass(grad_out_b, late, early, slope_b)
    near_b, terms_a, projected_a, projected_b = tied((near_b, terms_a, projected_a, projected_b))
    own_a, scaled_a = unmerge(moves.summed(terms_a), *stats_a)
    rail_a = moves.spread(scaled_a)
    near_b, scaled_a, projected_a, projected_b = tied((near_b, scaled_a, projected_a, projected_b))
    cut_b = moves.combine(near_b, far_b)

    projected = jnp.concatenate(
        [moves.by_rank(projected_a, size), moves.by_rank(projected_b, size)], 1
    ).reshape(images, image_rows, width)
    chosen = jnp.take(projected, image_of, axis=0, mode="clip")
    arrived = [chosen[s] for s in range(groups)]
    for s in range(1, groups):
        pairs = [(g, (g + s) % groups) for g in range(groups)]
        arrived[s] = lax.ppermute(arrived[s], "grp", pairs)

    def embed(text, arrived):
        goes_to = jnp.where(used[:, None], spot[:, None] + span, seq_len).reshape(-1)
        picks = jnp.arange(seq_len)[:, None] == goes_to[None, :]
        placed = jnp.dot(
            picks.astype(jnp.bfloat16),
            jnp.concatenate(arrived, 0),
            preferred_element_type=jnp.float32,
        ).astype(jnp.bfloat16)
        return jnp.where(jnp.any(picks, 1, keepdims=True), placed, text)

    cut_b, rail_a, arrived = tied((cut_b, rail_a, arrived))
    terms_b = moves.send(cut_b)
    grad_out_a = moves.gathered(rail_a)
    near_a, far_a = vision_pass(grad_out_a, late, early, slope_a)
    near_a, terms_b, arrived = tied((near_a, terms_b, arrived))
    terms_a = moves.send(moves.combine(near_a, far_a))
    normed_b = moves.summed(terms_b)
    terms_a, seq_embed, normed_b = tied((terms_a, embed(text_embed, arrived), normed_b))
    normed_a = moves.summed(terms_a)
    parts = [layer_norm(x[c], vis_gain, vis_eps) for c in range(chunks)]
    grads = [
        own_a + norm_back(normed_a, vis_gain, parts[0][1], parts[0][2]),
        own_b + norm_back(normed_b, vis_gain, parts[1][1], parts[1][2]),
    ]
    grad_vision = jnp.concatenate(grads, 0).astype(jnp.bfloat16)
    return (seq_embed, grad_vision)


def solution(mesh):
    placed = (
        P(("grp", "tp"), None),
        P(),
        P(None, "tp"),
        P("tp", None),
        P(),
        P(),
        P(None, "tp"),
        P("grp", "tp"),
        P(),
        P("grp", "tp"),
    )
    return jax.shard_map(
        per_device,
        mesh=mesh,
        in_specs=placed,
        out_specs=(P("grp", "tp"), P(("grp", "tp"), None)),
        check_vma=False,
    )
```

```python
import functools

import jax
import jax.numpy as jnp
from jax import lax
from jax.experimental import pallas as pl
from jax.experimental.pallas import tpu as pltpu
from jax.sharding import PartitionSpec as P

vis_eps = 1e-06
proj_eps = 1e-05
chunks = 2
images = 4
cores = 2


def layer_norm(values, scale_vec, epsilon):
    mean_val = jnp.mean(values, -1, keepdims=True)
    centred = values - mean_val
    inv_std = lax.rsqrt(jnp.mean(centred * centred, -1, keepdims=True) + epsilon)
    normed = centred * inv_std
    return (normed * scale_vec, normed, inv_std)


def norm_back(upstream, scale_vec, normed, inv_std):
    scaled = upstream * scale_vec
    return inv_std * (
        scaled
        - jnp.mean(scaled, -1, keepdims=True)
        - normed * jnp.mean(scaled * normed, -1, keepdims=True)
    )


def times_transposed(left, right):
    return lax.dot_general(
        left, right, (((1,), (1,)), ((), ())), preferred_element_type=jnp.float32
    )


def tile_of(length, most):
    return max(t for t in range(128, most + 1, 128) if length % t == 0)


def laid(pieces):
    if len(pieces) == 1:
        return pieces[0][...]
    if pieces[0].shape[0] % 16 == 0:
        return jnp.concatenate([p[...] for p in pieces], 0)
    return jnp.concatenate([p[...].astype(jnp.float32) for p in pieces], 0).astype(jnp.bfloat16)


def each_rows(total, body):
    step = 32 if total % 32 == 0 else total

    def run(i, _):
        body(pl.ds(pl.multiple_of(i * step, step), step))
        return 0

    lax.fori_loop(0, total // step, run, 0)


def block_start(total, rows, j):
    return pl.multiple_of(jnp.minimum(j * rows, total - rows), 16)


def fetch(source, held, sems, j):
    count, rows = held.shape[:2]

    @pl.when(j < count)
    def _():
        part = source.at[pl.ds(block_start(source.shape[0], rows, j), rows)]
        pltpu.make_async_copy(part, held.at[j], sems.at[j]).start()


def arrive(source, held, sems, j):
    rows = held.shape[1]
    pltpu.make_async_copy(source.at[pl.ds(0, rows)], held.at[j], sems.at[j]).wait()


def vision_kernel(count, ahead, *refs):
    pieces = refs[:count]
    if ahead:
        early, late, near, far, slope = refs[count : count + 5]
    else:
        early, late, slope, near, far = refs[count : count + 5]
    first, second, rows, pre, hidden, first_sems, second_sems = refs[count + 5 :]
    blocks, size, width = first.shape
    for j in range(blocks):
        fetch(early, first, first_sems, j)
    rows[...] = laid(pieces)

    def block(j, _):
        arrive(early, first, first_sems, j)
        fetch(late, second, second_sems, j)
        pre[...] = times_transposed(rows[...], first[j])
        repeated = j * size - jnp.minimum(j * size, early.shape[0] - size)
        place = pl.ds(pl.multiple_of(j * size, min(size, 128)), size)

        def act(sel):
            u = pre[sel, :]
            if ahead:
                fresh = lax.broadcasted_iota(jnp.int32, u.shape, 1) >= repeated
                cumul = 0.5 * (1.0 + lax.erf(u * 0.7071067811865476))
                dense = jnp.exp(-0.5 * u * u) * 0.3989422804014327
                hidden[sel, place] = jnp.where(fresh, u * cumul, 0.0).astype(jnp.bfloat16)
                slope[j, sel, :] = jnp.where(fresh, cumul + u * dense, 0.0)
            else:
                hidden[sel, place] = (u * slope[j, sel, :]).astype(jnp.bfloat16)

        each_rows(pre.shape[0], act)
        return 0

    lax.fori_loop(0, blocks, block, 0)
    for j in range(blocks):
        arrive(late, second, second_sems, j)
    half = near.shape[0]
    tile = min(1280, width)
    for k in range(0, width, tile):
        span = slice(k, min(k + tile, width))
        held = second[:, :, span]
        both = jnp.dot(
            hidden[...],
            held.reshape(blocks * size, held.shape[2]),
            preferred_element_type=jnp.float32,
        ).astype(jnp.bfloat16)
        near[:, span] = both[:half]
        far[:, span] = both[half:]


def project_kernel(count, *refs):
    pieces = refs[:count]
    weight, upstream, projected, delta, held, rows, pre, sems = refs[count:]
    for j in range(3):
        fetch(weight, held, sems, j)
    rows[...] = laid(pieces)
    pre[...] = jnp.zeros_like(pre)
    chunk = held.shape[1]

    def ahead(j, _):
        arrive(weight, held, sems, j)
        fetch(weight, held, sems, j + 3)
        sel = pl.ds(pl.multiple_of(j * chunk, 128), chunk)
        pre[...] += jnp.dot(rows[:, sel], held[j], preferred_element_type=jnp.float32)
        return 0

    lax.fori_loop(0, held.shape[0], ahead, 0)

    def act(sel):
        u = pre[sel, :]
        cumul = 0.5 * (1.0 + lax.erf(u * 0.7071067811865476))
        dense = jnp.exp(-0.5 * u * u) * 0.3989422804014327
        projected[sel, :] = (u * cumul).astype(jnp.bfloat16)
        grad = upstream[sel, :].astype(jnp.float32)
        delta[sel, :] = (grad * (cumul + u * dense)).astype(jnp.bfloat16)

    each_rows(pre.shape[0], act)


def project_back_kernel(delta, weight, near, far, held, sems):
    for j in range(3):
        fetch(weight, held, sems, j)
    chunk = held.shape[1]
    half = near.shape[0]

    def behind(j, _):
        arrive(weight, held, sems, j)
        fetch(weight, held, sems, j + 3)
        sel = pl.ds(pl.multiple_of(j * chunk, 128), chunk)
        back = times_transposed(delta[...], held[j]).astype(jnp.bfloat16)
        near[:, sel] = back[:half]
        far[:, sel] = back[half:]
        return 0

    lax.fori_loop(0, held.shape[0], behind, 0)


def entry_kernel(source, gain, *normed):
    rows = normed[0].shape[0]
    for c, out in enumerate(normed):
        values = source[c * rows : (c + 1) * rows].astype(jnp.float32)
        out[...] = layer_norm(values, gain[...][None, :], vis_eps)[0].astype(jnp.bfloat16)


def entry_norm(source, gain):
    rows, width = source.shape
    return pl.pallas_call(
        entry_kernel,
        in_specs=whole_blocks(2),
        out_specs=whole_blocks(chunks),
        out_shape=[jax.ShapeDtypeStruct((rows // chunks, width), jnp.bfloat16)] * chunks,
        cost_estimate=pl.CostEstimate(
            flops=8 * rows * width, bytes_accessed=4 * rows * width, transcendentals=rows
        ),
    )(source, gain)


def settings(limit):
    return pltpu.CompilerParams(vmem_limit_bytes=limit * 1024 * 1024)


def whole_blocks(count):
    return [pl.BlockSpec(memory_space=pltpu.VMEM)] * count


def vision_pass(pieces, early, late, slope=None):
    rows = sum(p.shape[0] for p in pieces)
    units, width = early.shape
    size = min(256, units)
    blocks = -(-units // size)
    given = [] if slope is None else [slope]
    slopes = [jax.ShapeDtypeStruct((blocks, rows, size), jnp.float32)] * (1 - len(given))
    return pl.pallas_call(
        functools.partial(vision_kernel, len(pieces), slope is None),
        in_specs=whole_blocks(len(pieces))
        + [pl.BlockSpec(memory_space=pl.ANY)] * 2
        + whole_blocks(len(given)),
        out_specs=whole_blocks(2 + len(slopes)),
        out_shape=[jax.ShapeDtypeStruct((rows // 2, width), jnp.bfloat16)] * 2 + slopes,
        scratch_shapes=[
            pltpu.VMEM((blocks, size, width), jnp.bfloat16),
            pltpu.VMEM((blocks, size, width), jnp.bfloat16),
            pltpu.VMEM((rows, width), jnp.bfloat16),
            pltpu.VMEM((rows, size), jnp.float32),
            pltpu.VMEM((rows, blocks * size), jnp.bfloat16),
            pltpu.SemaphoreType.DMA((blocks,)),
            pltpu.SemaphoreType.DMA((blocks,)),
        ],
        compiler_params=settings(56),
        cost_estimate=pl.CostEstimate(
            flops=4 * rows * width * units,
            bytes_accessed=4 * width * units + 4 * rows * (width + units),
            transcendentals=2 * rows * units,
        ),
    )(*pieces, early, late, *given)


def weight_cost(rows, depth, units):
    return pl.CostEstimate(
        flops=2 * rows * depth * units,
        bytes_accessed=2 * depth * units + 4 * rows * (depth + units),
        transcendentals=2 * rows * units,
    )


def project(pieces, weight, upstream):
    rows = sum(p.shape[0] for p in pieces)
    depth, units = weight.shape
    size = tile_of(depth, 1280)
    return pl.pallas_call(
        functools.partial(project_kernel, len(pieces)),
        in_specs=whole_blocks(len(pieces)) + [pl.BlockSpec(memory_space=pl.ANY)] + whole_blocks(1),
        out_specs=whole_blocks(2),
        out_shape=[jax.ShapeDtypeStruct((rows, units), jnp.bfloat16)] * 2,
        scratch_shapes=[
            pltpu.VMEM((depth // size, size, units), jnp.bfloat16),
            pltpu.VMEM((rows, depth), jnp.bfloat16),
            pltpu.VMEM((rows, units), jnp.float32),
            pltpu.SemaphoreType.DMA((depth // size,)),
        ],
        compiler_params=settings(40),
        cost_estimate=weight_cost(rows, depth, units),
    )(*pieces, weight, upstream)


def project_back(delta, weight):
    rows = delta.shape[0]
    depth, units = weight.shape
    size = tile_of(depth, 1280)
    return pl.pallas_call(
        project_back_kernel,
        in_specs=whole_blocks(1) + [pl.BlockSpec(memory_space=pl.ANY)],
        out_specs=whole_blocks(2),
        out_shape=[jax.ShapeDtypeStruct((rows // 2, depth), jnp.bfloat16)] * 2,
        scratch_shapes=[
            pltpu.VMEM((depth // size, size, units), jnp.bfloat16),
            pltpu.SemaphoreType.DMA((depth // size,)),
        ],
        compiler_params=settings(40),
        cost_estimate=weight_cost(rows, depth, units),
    )(delta, weight)


class Direct:
    def __init__(self):
        self.size = lax.axis_size("tp")
        self.places = self.size // cores
        rank = lax.axis_index("tp")
        place, core = rank // cores, rank % cores
        self.partners = [0, *range(2, self.places), *range(1, min(2, self.places))]
        partner = (place ^ jnp.array(self.partners)) * cores
        self.ranks = jnp.concatenate([partner + core, partner + 1 - core])
        every = jnp.arange(self.size)
        block = jnp.array([self.partners.index(k) for k in range(self.places)])
        self.blocks = (every + core) % cores * self.places + block[every // cores ^ place]
        self.pairs = [(a, a + 1 - 2 * (a % cores)) for a in range(self.size)]

    def shift(self, block, k):
        pairs = [(a, (a // cores ^ k) * cores + a % cores) for a in range(self.size)]
        return lax.ppermute(block, "tp", pairs)

    def spread(self, block):
        return [block] + [self.shift(block, k) for k in self.partners[1:]]

    def gathered(self, mine):
        other = [lax.ppermute(m, "tp", self.pairs) for m in mine]
        if mine[0].shape[0] % 8:
            return [jnp.concatenate(mine + other, 0)]
        return mine + other

    def combine(self, near, far):
        rows = near.shape[0] // self.places
        got = lax.ppermute(far, "tp", self.pairs)
        both = near.astype(jnp.float32) + got.astype(jnp.float32)
        cut = [both[k * rows : (k + 1) * rows] for k in range(self.places)]
        return cut[:1] + [c.astype(jnp.bfloat16) for c in cut[1:]]

    def send(self, cut):
        return cut[:1] + [self.shift(c, k) for c, k in zip(cut[1:], self.partners[1:])]

    def summed(self, terms):
        return sum([t.astype(jnp.float32) for t in terms[1:]], terms[0])

    def by_rank(self, rows, size):
        return jnp.take(rows.reshape(size, -1, rows.shape[-1]), self.blocks, axis=0, mode="clip")

    def by_row(self, ranks):
        return jnp.take(ranks, self.ranks, axis=0, mode="clip").reshape(-1, ranks.shape[-1])


def per_device(
    vision_in,
    vis_gain,
    first_weight,
    second_weight,
    layer_scale,
    proj_gain,
    proj_weight,
    text_embed,
    dest_row,
    cotangent,
):
    moves = Direct()
    groups = lax.axis_size("grp")
    size = lax.axis_size("tp")
    grp_rank = lax.axis_index("grp")
    seq_len, width = text_embed.shape
    merged_total = dest_row.shape[0] // groups
    image_rows = merged_total // images
    own_rows, vis_width = vision_in.shape
    merged_width = proj_gain.shape[0]
    fold = merged_width // vis_width
    rows = own_rows // chunks
    merged_rows = rows // fold

    normed = list(entry_norm(vision_in, vis_gain))
    x = [vision_in[c * rows : (c + 1) * rows].astype(jnp.float32) for c in range(chunks)]

    tied = lax.optimization_barrier
    rail_b = moves.spread(normed[1])

    starts = dest_row.reshape(groups, images, image_rows)[:, :, 0]
    start_pos = starts % seq_len
    shift = starts[0] // seq_len
    matches = (shift[None, :] == jnp.arange(groups)[:, None]).astype(jnp.int32)
    image_of = jnp.sum(matches * jnp.arange(images), 1)
    used = jnp.sum(matches, 1) > 0
    source = (grp_rank - jnp.arange(groups)) % groups
    from_group = (source[:, None] == jnp.arange(groups)).astype(jnp.int32)
    spot = jnp.sum(matches[:, None, :] * from_group[:, :, None] * start_pos[None], (1, 2))

    span = jnp.arange(image_rows)
    picked = jnp.take(cotangent, (spot[:, None] + span).reshape(-1), axis=0, mode="clip")
    picked = [picked[s * image_rows : (s + 1) * image_rows] for s in range(groups)]
    for s in range(1, groups):
        pairs = [(g, (g - s) % groups) for g in range(groups)]
        picked[s] = lax.ppermute(picked[s], "grp", pairs)

    normed[0], rail_b, picked = tied((normed[0], rail_b, picked))
    rail_a = moves.spread(normed[0])
    patches_b = moves.gathered(rail_b)

    def grad_of(picked, c):
        returned = jnp.take(jnp.stack(picked), shift, axis=0, mode="clip").reshape(size, -1, width)
        return moves.by_row(returned[:, c * merged_rows : (c + 1) * merged_rows])

    def merge(c, summed):
        outputs = (x[c] + layer_scale * summed).astype(jnp.bfloat16)
        merged = outputs.reshape(merged_rows, merged_width).astype(jnp.float32)
        scaled, own_hat, own_inv = layer_norm(merged, proj_gain, proj_eps)
        return scaled.astype(jnp.bfloat16), own_hat, own_inv

    def unmerge(back_sum, own_hat, own_inv):
        merged_grad = norm_back(back_sum, proj_gain, own_hat, own_inv).astype(jnp.bfloat16)
        own_grad = merged_grad.reshape(rows, vis_width).astype(jnp.float32)
        return own_grad, (own_grad * layer_scale).astype(jnp.bfloat16)

    early, late = first_weight.T, second_weight
    near_b, far_b, slope_b = vision_pass(patches_b, early, late)
    near_b, far_b, rail_a = tied((near_b, far_b, rail_a))
    patches_a = moves.gathered(rail_a)
    terms_b = moves.send(moves.combine(near_b, far_b))
    near_a, far_a, slope_a = vision_pass(patches_a, early, late)
    near_a, terms_b, picked = tied((near_a, terms_b, picked))
    mixed_b, *stats_b = merge(1, moves.summed(terms_b))
    rail_b = moves.spread(mixed_b)
    near_a, mixed_b = tied((near_a, mixed_b))
    cut_a, upstream = tied(
        (moves.combine(near_a, far_a), [grad_of(picked, c) for c in range(chunks)])
    )
    terms_a = moves.send(cut_a)
    rail_b, terms_a[-1] = tied((rail_b, terms_a[-1]))
    merged_b = moves.gathered(rail_b)
    projected_b, delta_b = project(merged_b, proj_weight, upstream[1])
    projected_b, delta_b, terms_a = tied((projected_b, delta_b, terms_a))
    mixed_a, *stats_a = merge(0, moves.summed(terms_a))
    rail_a = moves.spread(mixed_a)
    delta_b, mixed_a = tied((delta_b, mixed_a))
    near_b, far_b = project_back(delta_b, proj_weight)
    near_b, far_b, rail_a = tied((near_b, far_b, rail_a))
    terms_b = moves.send(moves.combine(near_b, far_b))
    merged_a = moves.gathered(rail_a)
    projected_a, delta_a = project(merged_a, proj_weight, upstream[0])
    projected_a, delta_a, terms_b = tied((projected_a, delta_a, terms_b))
    own_b, scaled_b = unmerge(moves.summed(terms_b), *stats_b)
    rail_b = moves.spread(scaled_b)
    delta_a, scaled_b = tied((delta_a, scaled_b))
    near_a, far_a = project_back(delta_a, proj_weight)
    near_a, far_a, rail_b = tied((near_a, far_a, rail_b))
    terms_a = moves.send(moves.combine(near_a, far_a))
    grad_out_b = moves.gathered(rail_b)
    near_b, far_b = vision_pass(grad_out_b, late, early, slope_b)
    near_b, terms_a, projected_a, projected_b = tied((near_b, terms_a, projected_a, projected_b))
    own_a, scaled_a = unmerge(moves.summed(terms_a), *stats_a)
    rail_a = moves.spread(scaled_a)
    near_b, scaled_a, projected_a, projected_b = tied((near_b, scaled_a, projected_a, projected_b))
    cut_b = moves.combine(near_b, far_b)

    projected = jnp.concatenate(
        [moves.by_rank(projected_a, size), moves.by_rank(projected_b, size)], 1
    ).reshape(images, image_rows, width)
    chosen = jnp.take(projected, image_of, axis=0, mode="clip")
    arrived = [chosen[s] for s in range(groups)]
    for s in range(1, groups):
        pairs = [(g, (g + s) % groups) for g in range(groups)]
        arrived[s] = lax.ppermute(arrived[s], "grp", pairs)

    def embed(text, arrived):
        goes_to = jnp.where(used[:, None], spot[:, None] + span, seq_len).reshape(-1)
        picks = jnp.arange(seq_len)[:, None] == goes_to[None, :]
        placed = jnp.dot(
            picks.astype(jnp.bfloat16),
            jnp.concatenate(arrived, 0),
            preferred_element_type=jnp.float32,
        ).astype(jnp.bfloat16)
        return jnp.where(jnp.any(picks, 1, keepdims=True), placed, text)

    cut_b, arrived, rail_a[-1] = tied((cut_b, arrived, rail_a[-1]))
    terms_b = moves.send(cut_b)
    rail_a, terms_b[-1] = tied((rail_a, terms_b[-1]))
    grad_out_a = moves.gathered(rail_a)
    near_a, far_a = vision_pass(grad_out_a, late, early, slope_a)
    near_a, terms_b, arrived = tied((near_a, terms_b, arrived))
    terms_a = moves.send(moves.combine(near_a, far_a))
    normed_b = moves.summed(terms_b)
    terms_a, seq_embed, normed_b = tied((terms_a, embed(text_embed, arrived), normed_b))
    normed_a = moves.summed(terms_a)
    parts = [layer_norm(x[c], vis_gain, vis_eps) for c in range(chunks)]
    grads = [
        own_a + norm_back(normed_a, vis_gain, parts[0][1], parts[0][2]),
        own_b + norm_back(normed_b, vis_gain, parts[1][1], parts[1][2]),
    ]
    grad_vision = jnp.concatenate(grads, 0).astype(jnp.bfloat16)
    return (seq_embed, grad_vision)


def solution(mesh):
    placed = (
        P(("grp", "tp"), None),
        P(),
        P(None, "tp"),
        P("tp", None),
        P(),
        P(),
        P(None, "tp"),
        P("grp", "tp"),
        P(),
        P("grp", "tp"),
    )
    return jax.shard_map(
        per_device,
        mesh=mesh,
        in_specs=placed,
        out_specs=(P("grp", "tp"), P(("grp", "tp"), None)),
        check_vma=False,
    )
```
